32 devices in a mesh: grp: 8 (over z, x), kin: 4 (over y, core).
Axes of the slice: x: 2, y: 2, z: 4, core: 2. Of those that a mesh axis runs over, the one named last changes fastest.
Arguments:
- waves: bfloat16 [32, 2, 8, 1024], P(('grp', 'kin')), may hold values from -6 to 6
- vector: float32 [32, 2, 16], P(('grp', 'kin')), may hold values from -6 to 6
- energies: float32 [32, 16], P(('grp', 'kin')), may hold values from 0.5 to 1.5
- basis: bfloat16 [2, 1024, 1536], replicated, may hold values from -0.1875 to 0.1875
- screening: float32 [32, 1536], replicated, may hold values from 0.05 to 1
- coulomb: float32 [1536], replicated, may hold values from 0.01 to 0.2
- qmap: int32 [32, 32], P(('grp', 'kin')), may hold values from 0 to 31, as said below
Outputs:
- applied: float32 [32, 2, 16], P(('grp', 'kin'))
The draws below stay inside these ranges and needn't reach their ends.
Inputs may be any that keep to these rules, and one draw needn't show every extreme that they name: qmap[s, s2] is the index, on the periodic 8 x 4 k-grid, of the difference of the grid points of the stored k-points s and s2 (grid point x * 4 + y); the stored k-points are a permutation of the grid points, so each row holds every value once.
All inputs are finite; a program needn't handle non-finite values.
Results may differ from the reference program's by a relative error of at most 0.0057.
Values may be sent and summed in bfloat16 or wider, within the bound.
A program may use at most 64 MiB of HBM per device.

```python
import math
import jax
import jax.numpy as jnp
from jax import lax

NV = 4
NC = 4
NB = 8
NT = 16
NMU = 1024
NG = 1536
KD = 1
NK = 32
KX = 8
KY = 4
N_GRP = 8
N_KIN = 4


def draw_qmap(key, part):
    key = jax.random.fold_in(key, 11)
    order = jax.random.permutation(key, NK).astype(jnp.int32)
    first = order // KY
    second = order % KY
    step_x = (first[:, None] - first[None, :]) % KX
    step_y = (second[:, None] - second[None, :]) % KY
    return (step_x * KY + step_y).astype(jnp.int32)


def block_scale(own_key, extent, cuts, smallest, top_value):
    gain, own = 1.0, jax.random.fold_in(own_key, 6)
    for axis_at, parts in cuts:
        steps = jnp.exp(jax.random.uniform(jax.random.fold_in(own, axis_at), (parts,), jnp.float32, smallest / len(cuts), top_value / len(cuts)))
        gain = gain * jnp.repeat(steps, extent[axis_at] // parts).reshape([-1 if axis == axis_at else 1 for axis in range(len(extent))])
    return gain


def noise(own_key, dims, spread, reach, pieces=(), kind=jnp.bfloat16):
    entries = spread * jax.random.normal(own_key, dims, jnp.float32)
    if pieces:
        entries = entries * block_scale(own_key, dims, pieces, -0.22, 0.18)
    return jnp.clip(entries, -reach, reach).astype(kind)


def setup_inputs(seed: int = 0) -> dict:
    seeds = jax.random.split(jax.random.key(seed), 8)
    return {
        "waves": noise(seeds[0], (NK, 2, NB, NMU), 1.0, 6.0, ((0, 32),)),
        "vector": noise(seeds[1], (NK, 2, NT), 1.0, 6.0, ((0, 32),), jnp.float32),
        "energies": jnp.clip(0.5 + 1.0 * jax.random.uniform(seeds[2], (NK, NT), jnp.float32) ** block_scale(seeds[2], (NK, NT), ((0, 32),), -0.2, 0.2), 0.5, 1.5),
        "basis": noise(seeds[3], (2, NMU, NG), NMU ** -0.5, 0.1875),
        "screening": jnp.clip(jnp.exp(jax.random.uniform(seeds[4], (NK, NG), jnp.float32, math.log(0.05), math.log(1.0))), 0.05, 1.0),
        "coulomb": jnp.clip(jnp.exp(jax.random.uniform(seeds[5], (NG,), jnp.float32, math.log(0.01), math.log(0.2))), 0.01, 0.2),
        "qmap": draw_qmap(jax.random.fold_in(seeds[7], 71), 0),
    }


def conj_products(left, right):
    left_re = left[:, 0].astype(jnp.float32)[:, None, :, None, :]
    left_im = left[:, 1].astype(jnp.float32)[:, None, :, None, :]
    right_re = right[:, 0].astype(jnp.float32)[None, :, None, :, :]
    right_im = right[:, 1].astype(jnp.float32)[None, :, None, :, :]
    real_part = (left_re * right_re + left_im * right_im).astype(jnp.bfloat16)
    imag_part = (left_re * right_im - left_im * right_re).astype(jnp.bfloat16)
    return real_part, imag_part


def densities(pair_re, pair_im, basis):
    rows = pair_re.shape[0]
    stacked = jnp.concatenate([pair_re, pair_im], 0)
    first = jnp.dot(stacked, basis[0], preferred_element_type=jnp.float32)
    second = jnp.dot(stacked, basis[1], preferred_element_type=jnp.float32)
    real_part = (first[:rows] - second[rows:]).astype(jnp.bfloat16)
    imag_part = (second[:rows] + first[rows:]).astype(jnp.bfloat16)
    return real_part, imag_part


def block_terms(own_waves, own_vector, part_waves, part_vector, weights, basis):
    highest = lax.Precision.HIGHEST
    owners = own_waves.shape[0]
    partners = part_waves.shape[0]
    points = own_waves.shape[3]
    cond_re, cond_im = conj_products(own_waves[:, :, NV:], part_waves[:, :, NV:])
    val_re, val_im = conj_products(own_waves[:, :, :NV], part_waves[:, :, :NV])
    pair_re = jnp.concatenate([cond_re.reshape(owners, partners, NC * NC, points), val_re.reshape(owners, partners, NV * NV, points)], 2).reshape(-1, points)
    pair_im = jnp.concatenate([cond_im.reshape(owners, partners, NC * NC, points), val_im.reshape(owners, partners, NV * NV, points)], 2).reshape(-1, points)
    dens_re, dens_im = densities(pair_re, pair_im, basis)
    dens_re = dens_re.reshape(owners, partners, NC * NC + NV * NV, -1)
    dens_im = dens_im.reshape(owners, partners, NC * NC + NV * NV, -1)
    wcond_re = dens_re[:, :, :NC * NC].astype(jnp.float32) * weights[:, :, None, :]
    wcond_im = dens_im[:, :, :NC * NC].astype(jnp.float32) * weights[:, :, None, :]
    val_dre = dens_re[:, :, NC * NC:].astype(jnp.float32)
    val_dim = dens_im[:, :, NC * NC:].astype(jnp.float32)
    kern_re = jnp.einsum("abpg,abqg->abpq", wcond_re, val_dre, precision=highest) + jnp.einsum("abpg,abqg->abpq", wcond_im, val_dim, precision=highest)
    kern_im = jnp.einsum("abpg,abqg->abpq", wcond_re, val_dim, precision=highest) - jnp.einsum("abpg,abqg->abpq", wcond_im, val_dre, precision=highest)
    kern_re = kern_re.reshape(owners, partners, NC, NC, NV, NV)
    kern_im = kern_im.reshape(owners, partners, NC, NC, NV, NV)
    own_x = own_vector.astype(jnp.float32).reshape(owners, 2, NV, NC)
    part_x = part_vector.astype(jnp.float32).reshape(partners, 2, NV, NC)
    form_d = "abcdvw,bwd->avc"
    direct_re = jnp.einsum(form_d, kern_re, part_x[:, 0], precision=highest) - jnp.einsum(form_d, kern_im, part_x[:, 1], precision=highest)
    direct_im = jnp.einsum(form_d, kern_re, part_x[:, 1], precision=highest) + jnp.einsum(form_d, kern_im, part_x[:, 0], precision=highest)
    form_h = "abcdvw,avc->bwd"
    herm_re = jnp.einsum(form_h, kern_re, own_x[:, 0], precision=highest) + jnp.einsum(form_h, kern_im, own_x[:, 1], precision=highest)
    herm_im = jnp.einsum(form_h, kern_re, own_x[:, 1], precision=highest) - jnp.einsum(form_h, kern_im, own_x[:, 0], precision=highest)
    direct = jnp.stack([direct_re.reshape(owners, NT), direct_im.reshape(owners, NT)], 1)
    hermitian = jnp.stack([herm_re.reshape(partners, NT), herm_im.reshape(partners, NT)], 1)
    return direct, hermitian


def own_densities(waves, basis):
    count = waves.shape[0]
    points = waves.shape[3]
    val_re = waves[:, 0, :NV].astype(jnp.float32)[:, :, None, :]
    val_im = waves[:, 1, :NV].astype(jnp.float32)[:, :, None, :]
    con_re = waves[:, 0, NV:].astype(jnp.float32)[:, None, :, :]
    con_im = waves[:, 1, NV:].astype(jnp.float32)[:, None, :, :]
    pair_re = (val_re * con_re + val_im * con_im).astype(jnp.bfloat16).reshape(-1, points)
    pair_im = (val_re * con_im - val_im * con_re).astype(jnp.bfloat16).reshape(-1, points)
    dens_re, dens_im = densities(pair_re, pair_im, basis)
    return dens_re.reshape(count, NT, -1), dens_im.reshape(count, NT, -1)


def reference(waves, vector, energies, basis, screening, coulomb, qmap):
    highest = lax.Precision.HIGHEST
    offset = N_GRP // 4
    block = KD * N_KIN
    total = block * N_GRP
    coarse = vector.astype(jnp.bfloat16)

    def one_group(group):
        partner = (group - offset) % N_GRP
        own_start = (group * block).astype(jnp.int32)
        part_start = (partner * block).astype(jnp.int32)
        own_waves = lax.dynamic_slice_in_dim(waves, own_start, block, 0)
        part_waves = lax.dynamic_slice_in_dim(waves, part_start, block, 0)
        own_vector = lax.dynamic_slice_in_dim(coarse, own_start, block, 0)
        part_vector = lax.dynamic_slice_in_dim(coarse, part_start, block, 0)
        qrows = lax.dynamic_slice(qmap, (own_start, part_start), (block, block))
        weights = jnp.take(screening, qrows.reshape(-1), axis=0).reshape(block, block, -1)
        return block_terms(own_waves, own_vector, part_waves, part_vector, weights, basis)

    direct, hermitian = lax.map(one_group, jnp.arange(N_GRP, dtype=jnp.int32))
    direct = direct.reshape(total, 2, NT)
    hermitian = jnp.roll(hermitian, -offset, axis=0).reshape(total, 2, NT)
    ex_re, ex_im = own_densities(waves, basis)
    ex_re = ex_re.astype(jnp.float32)
    ex_im = ex_im.astype(jnp.float32)
    coarse_x = coarse.astype(jnp.float32)
    sum_re = jnp.einsum("atg,at->g", ex_re, coarse_x[:, 0], precision=highest) - jnp.einsum("atg,at->g", ex_im, coarse_x[:, 1], precision=highest)
    sum_im = jnp.einsum("atg,at->g", ex_re, coarse_x[:, 1], precision=highest) + jnp.einsum("atg,at->g", ex_im, coarse_x[:, 0], precision=highest)
    pot_re = coulomb * sum_re
    pot_im = coulomb * sum_im
    exch_re = jnp.einsum("atg,g->at", ex_re, pot_re, precision=highest) + jnp.einsum("atg,g->at", ex_im, pot_im, precision=highest)
    exch_im = jnp.einsum("atg,g->at", ex_re, pot_im, precision=highest) - jnp.einsum("atg,g->at", ex_im, pot_re, precision=highest)
    exchange = jnp.stack([exch_re, exch_im], 1)
    scale = jnp.float32(1.0 / total)
    return energies[:, None, :] * vector + 2.0 * scale * exchange - scale * (direct + hermitian)
```

```python
import functools

import jax
import jax.numpy as jnp
from jax import lax
from jax.experimental import pallas as pl
from jax.experimental.pallas import tpu as pltpu
from jax.sharding import PartitionSpec as P

NV = 4
NC = 4
NB = 8
NT = 16
BLK = 4
ROWS = BLK * NC * NC
CHUNK = 256
MESH = pl.DeviceIdType.MESH
F32 = jnp.float32
BF16 = jnp.bfloat16


def iota(shape, dim):
    return lax.broadcasted_iota(jnp.int32, shape, dim)


def mm(left, right):
    return jnp.dot(left, right, preferred_element_type=F32)


def mm_nt(left, right):
    return lax.dot_general(left, right, (((1,), (1,)), ((), ())), preferred_element_type=F32)


def hi_lo(value):
    high = value.astype(BF16)
    low = (value - high.astype(F32)).astype(BF16)
    return jnp.concatenate([high, low], 0)


def one_hot(cond):
    return jnp.where(cond, 1.0, 0.0).astype(BF16)


def conj_mul(lre, lim, rre, rim):
    return lre * rre + lim * rim, lre * rim - lim * rre


def kernel(
    groups, members, n_k, n_g,
    waves, vector, energies, basis, screening, coulomb, qmap, out,
    basis_v, screen_v, wrecv, vrecv, own_p, pair_p, own_d, s_own, s_a, s_plane, s_b, h_send, h_recv,
    basis_sem, screen_sem, w_ssem, w_rsem, v_ssem, v_rsem, a_ssem, a_rsem, b_ssem, b_rsem, h_ssem, h_rsem,
):
    offset = groups // 4
    planes = 4
    block = members
    points = waves.shape[3]
    n_chunk = n_g // CHUNK
    grp = lax.axis_index("grp")
    kin = lax.axis_index("kin")
    plane = lax.div(grp, offset)
    spot = lax.rem(grp, offset)

    def at(dp, ds, dk):
        g = lax.rem(plane + dp, planes) * offset + lax.rem(spot + ds, offset)
        return (g, lax.rem(kin + dk, members))

    basis_in = []
    for n in range(n_chunk):
        cols = pl.ds(n * CHUNK, CHUNK)
        copy = pltpu.make_async_copy(basis.at[:, :, cols], basis_v.at[:, :, cols], basis_sem.at[n])
        copy.start()
        basis_in.append(copy)
    screen_in = pltpu.make_async_copy(screening, screen_v, screen_sem)
    screen_in.start()

    mates = [(0, ds, dk) for ds in range(offset) for dk in range(members) if (ds, dk) != (0, 0)]
    others = [(dp, 0, dk) for dp in (1, 3) for dk in range(members)] + [(2, 0, 0)]
    barrier = pltpu.get_barrier_semaphore()
    for where in others + mates:
        pl.semaphore_signal(barrier, inc=1, device_id=at(*where), device_id_type=MESH)
    pl.semaphore_wait(barrier, len(others) + len(mates))

    def remote(src, dst, ssem, rsem, where):
        return pltpu.make_async_remote_copy(
            src_ref=src, dst_ref=dst, send_sem=ssem, recv_sem=rsem, device_id=at(*where), device_id_type=MESH
        )

    w_copies = []
    for i in range(members):
        w_copies.append(remote(waves, wrecv.at[pl.ds(i, 1)], w_ssem.at[i], w_rsem.at[i], (1, 0, i)))
        w_copies[-1].start()
    v_copies = []
    for i in range(members):
        v_copies.append(remote(vector, vrecv.at[pl.ds(i, 1)], v_ssem.at[i], v_rsem.at[i], (1, 0, i)))
        v_copies[-1].start()

    low_half = iota((8, points), 0) < 4
    own_re = waves[0, 0].astype(F32)
    own_im = waves[0, 1].astype(F32)

    def cond_twice(part):
        return jnp.concatenate([part[NV:], part[NV:]], 0)

    cre, cim = cond_twice(own_re), cond_twice(own_im)
    re_parts, im_parts = [], []
    for j in range(2):
        vre = jnp.where(low_half, own_re[2 * j:2 * j + 1], own_re[2 * j + 1:2 * j + 2])
        vim = jnp.where(low_half, own_im[2 * j:2 * j + 1], own_im[2 * j + 1:2 * j + 2])
        pre, pim = conj_mul(vre, vim, cre, cim)
        re_parts.append(pre)
        im_parts.append(pim)
    pre = jnp.concatenate(re_parts, 0)
    pim = jnp.concatenate(im_parts, 0)
    own_p[0:NT, 0:points] = pre.astype(BF16)
    own_p[0:NT, points:] = (-pim).astype(BF16)
    own_p[NT:2 * NT, 0:points] = pim.astype(BF16)
    own_p[NT:2 * NT, points:] = pre.astype(BF16)

    own_vec = vector[0]
    x_own = own_vec.astype(BF16).astype(F32)
    xr, xi = x_own[0:1], x_own[1:2]
    x_rows = jnp.concatenate(
        [jnp.concatenate([xr, -xi], 1), jnp.concatenate([xi, xr], 1), jnp.zeros((6, 2 * NT), F32)], 0
    ).astype(BF16)

    def basis_cols(n):
        cols = pl.ds(n * CHUNK, CHUNK)
        return jnp.concatenate([basis_v[0, :, cols], basis_v[1, :, cols]], 0)

    for n in range(n_chunk):
        basis_in[n].wait()
        cols = pl.ds(n * CHUNK, CHUNK)
        dens = mm(own_p[...], basis_cols(n)).astype(BF16)
        own_d[:, cols] = dens
        s_own[:, cols] = mm(x_rows, dens)[0:2]

    a_copies = []
    for i, where in enumerate(mates):
        a_copies.append(remote(s_own, s_a.at[i], a_ssem.at[i], a_rsem.at[i], where))
        a_copies[-1].start()

    side = 2 * ROWS
    row = iota((side, NT), 0)
    lane = iota((side, NT), 1)
    row_b = (row // 32) % 2 * 2 + (row // 4) % 2
    a_band = (row // 8) % 4
    b_band = row % 4
    col = iota((NT, side), 1)
    tr = iota((NT, side), 0)
    pick_v = one_hot((col // 8) % 4 == tr // 4)
    pick_w = one_hot(col % 4 == tr // 4)
    full_r = iota((side, side), 0)
    full_c = iota((side, side), 1)
    same_b = ((full_r // 32) % 2 == (full_c // 32) % 2) & ((full_r // 4) % 2 == (full_c // 4) % 2)
    r_im = full_r >= ROWS
    c_im = full_c >= ROWS
    same_comp = r_im == c_im
    sign = jnp.where(r_im, 1.0, -1.0)

    def spread(x_re, x_im, pick):
        xx_re = jnp.where(same_b, mm(x_re.astype(BF16), pick), 0.0)
        xx_im = jnp.where(same_b, mm(x_im.astype(BF16), pick), 0.0)
        return xx_re, xx_im

    own_rows_re = jnp.where(a_band == lane % 4, xr, 0.0)
    own_rows_im = jnp.where(a_band == lane % 4, xi, 0.0)
    oa_re, oa_im = spread(own_rows_re, own_rows_im, pick_v)
    h_re_w = jnp.where(same_comp, oa_re, -sign * oa_im)
    h_im_w = jnp.where(same_comp, oa_im, sign * oa_re)

    screen_in.wait()
    low_chunk = iota((8, CHUNK), 0) < 4
    base = lax.rem(grp + groups - offset, groups) * block
    s_done = False
    d_re = jnp.zeros((NC * 8, side), F32)
    d_im = jnp.zeros((NC * 8, side), F32)
    q_cat = jnp.concatenate([pick_v, pick_w], 0)
    h_copies = []
    for blk in range(members // BLK):
        slots = [blk * BLK + j for j in range(BLK)]
        for i in slots:
            w_copies[i].wait_recv()
            v_copies[i].wait_recv()

        for kind, first_band in ((0, NV), (1, 0)):
            for q in range(2):
                s0, s1 = slots[2 * q], slots[2 * q + 1]
                rre = jnp.concatenate(
                    [wrecv[s0, 0].astype(F32)[first_band:first_band + 4], wrecv[s1, 0].astype(F32)[first_band:first_band + 4]], 0)
                rim = jnp.concatenate(
                    [wrecv[s0, 1].astype(F32)[first_band:first_band + 4], wrecv[s1, 1].astype(F32)[first_band:first_band + 4]], 0)
                for half in range(2):
                    res, ims = [], []
                    for c in (2 * half, 2 * half + 1):
                        band = first_band + c
                        a, b = conj_mul(own_re[band:band + 1], own_im[band:band + 1], rre, rim)
                        res.append(a)
                        ims.append(b)
                    pre = jnp.concatenate(res, 0)
                    pim = jnp.concatenate(ims, 0)
                    r0 = kind * 2 * ROWS + q * 32 + half * 16
                    pair_p[r0:r0 + 16, 0:points] = pre.astype(BF16)
                    pair_p[r0:r0 + 16, points:] = (-pim).astype(BF16)
                    pair_p[r0 + ROWS:r0 + ROWS + 16, 0:points] = pim.astype(BF16)
                    pair_p[r0 + ROWS:r0 + ROWS + 16, points:] = pre.astype(BF16)

        rows_w = [qmap[0, base + lax.rem(kin + members - i, members)] for i in slots]
        kern = jnp.zeros((side, side), F32)
        for n in range(n_chunk):
            cols = pl.ds(n * CHUNK, CHUNK)
            dens = mm(pair_p[...], basis_cols(n)).astype(BF16)
            tiles = []
            for q in range(2):
                w0 = screen_v[pl.ds(rows_w[2 * q], 1), cols]
                w1 = screen_v[pl.ds(rows_w[2 * q + 1], 1), cols]
                tiles += [jnp.where(low_chunk, w0, w1)] * 4
            weight = jnp.concatenate(tiles * 2, 0)
            cond = (dens[0:side].astype(F32) * weight).astype(BF16)
            kern = kern + mm_nt(cond, dens[side:])
            if n == n_chunk // 2 and not s_done:
                s_done = True
                for copy in a_copies:
                    copy.wait_recv()
                total = s_own[...]
                for i in range(len(mates)):
                    total = total + s_a[i]
                s_plane[...] = total
                b_copies = []
                for i in range(planes - 1):
                    b_copies.append(remote(s_plane, s_b.at[i], b_ssem.at[i], b_rsem.at[i], (i + 1, 0, 0)))
                    b_copies[-1].start()

        part_re = jnp.zeros((side, NT), F32)
        part_im = jnp.zeros((side, NT), F32)
        for j, i in enumerate(slots):
            xb = vrecv[i].astype(BF16).astype(F32)
            hit = (row_b == j) & (b_band == lane % 4)
            part_re = part_re + jnp.where(hit, xb[0:1], 0.0)
            part_im = part_im + jnp.where(hit, xb[1:2], 0.0)
        pa_re, pa_im = spread(part_re, part_im, pick_w)
        d_re_w = jnp.where(same_comp, pa_re, sign * pa_im)
        d_im_w = jnp.where(same_comp, pa_im, -sign * pa_re)

        def fold_d(value):
            return value[0:32] + value[32:64] + value[64:96] + value[96:128]

        def fold_h(value):
            halves = value[0:64] + value[64:128]
            return jnp.concatenate(
                [halves[32 * q:32 * q + 8] + halves[32 * q + 8:32 * q + 16]
                 + halves[32 * q + 16:32 * q + 24] + halves[32 * q + 24:32 * q + 32] for q in range(2)], 0)

        d_re = d_re + fold_d(kern * d_re_w)
        d_im = d_im + fold_d(kern * d_im_w)
        h_rows = jnp.concatenate([fold_h(kern * h_re_w), fold_h(kern * h_im_w)], 0)
        h_sums = mm_nt(hi_lo(h_rows), pick_w)
        h_sums = h_sums[0:32] + h_sums[32:64]
        hr = iota((32, NT), 0)
        hl = iota((32, NT), 1)
        h_sums = jnp.where(hr % 4 == hl % 4, h_sums, 0.0)
        for j, i in enumerate(slots):
            for comp in range(2):
                r0 = comp * 16 + j // 2 * 8
                mine = jnp.where((iota((8, NT), 0) // 4) == j % 2, h_sums[r0:r0 + 8], 0.0)
                h_send[i, comp:comp + 1] = jnp.sum(mine, 0, keepdims=True)
        for i in slots:
            h_copies.append(remote(h_send.at[i], h_recv.at[i], h_ssem.at[i], h_rsem.at[i], (3, 0, members - i)))
            h_copies[-1].start()

    d_sums = mm_nt(hi_lo(jnp.concatenate([d_re, d_im], 0)), pick_v)
    d_sums = d_sums[0:64] + d_sums[64:128]
    dr = iota((64, NT), 0)
    dl = iota((64, NT), 1)
    d_sums = jnp.where((dr // 8) % 4 == dl % 4, d_sums, 0.0)
    direct = jnp.concatenate(
        [jnp.sum(d_sums[0:32], 0, keepdims=True), jnp.sum(d_sums[32:64], 0, keepdims=True)], 0)

    total = s_plane[...]
    for i in range(planes - 1):
        b_copies[i].wait_recv()
        total = total + s_b[i]
    pot = coulomb[...] * total
    pot_rows = jnp.concatenate([hi_lo(pot), jnp.zeros((4, n_g), BF16)], 0)
    ex = mm_nt(pot_rows, own_d[...])
    ex = ex[0:2] + ex[2:4]
    ex_re = ex[0:1, 0:NT] + ex[1:2, NT:]
    ex_im = ex[1:2, 0:NT] - ex[0:1, NT:]
    exchange = jnp.concatenate([ex_re, ex_im], 0)

    scale = 1.0 / n_k
    result = energies[...] * own_vec + (2.0 * scale) * exchange - scale * direct
    back = jnp.zeros((2, NT), F32)
    for i in range(members):
        h_copies[i].wait_recv()
        back = back + h_recv[i]
    out[0] = result - scale * back

    for copy in w_copies + v_copies + a_copies + b_copies + h_copies:
        copy.wait_send()


def on_device(waves, vector, energies, basis, screening, coulomb, qmap):
    groups = lax.axis_size("grp")
    members = lax.axis_size("kin")
    offset = groups // 4
    n_mates = offset * members - 1
    points = waves.shape[3]
    n_g = basis.shape[2]
    vmem = pl.BlockSpec(memory_space=pltpu.VMEM)
    smem = pl.BlockSpec(memory_space=pltpu.SMEM)
    hbm = pl.BlockSpec(memory_space=pl.ANY)
    dma = pltpu.SemaphoreType.DMA
    return pl.pallas_call(
        functools.partial(kernel, groups, members, groups * members, n_g),
        out_shape=jax.ShapeDtypeStruct(vector.shape, F32),
        in_specs=[vmem, vmem, vmem, hbm, hbm, vmem, smem],
        out_specs=vmem,
        scratch_shapes=[
            pltpu.VMEM(basis.shape, BF16),
            pltpu.VMEM(screening.shape, F32),
            pltpu.VMEM((members,) + waves.shape[1:], BF16),
            pltpu.VMEM((members, 2, NT), F32),
            pltpu.VMEM((2 * NT, 2 * points), BF16),
            pltpu.VMEM((4 * ROWS, 2 * points), BF16),
            pltpu.VMEM((2 * NT, n_g), BF16),
            pltpu.VMEM((2, n_g), F32),
            pltpu.VMEM((n_mates, 2, n_g), F32),
            pltpu.VMEM((2, n_g), F32),
            pltpu.VMEM((3, 2, n_g), F32),
            pltpu.VMEM((members, 2, NT), F32),
            pltpu.VMEM((members, 2, NT), F32),
            dma((n_g // CHUNK,)),
            dma,
            dma((members,)), dma((members,)),
            dma((members,)), dma((members,)),
            dma((n_mates,)), dma((n_mates,)),
            dma((3,)), dma((3,)),
            dma((members,)), dma((members,)),
        ],
        compiler_params=pltpu.CompilerParams(
            collective_id=0, has_side_effects=True, vmem_limit_bytes=40 * 1024 * 1024
        ),
    )(waves, vector, energies, basis, screening, coulomb.reshape(1, n_g), qmap)


def solution(mesh):
    return jax.shard_map(
        on_device,
        mesh=mesh,
        in_specs=(
            P(("grp", "kin"), None, None, None),
            P(("grp", "kin"), None, None),
            P(("grp", "kin"), None),
            P(),
            P(),
            P(),
            P(("grp", "kin"), None),
        ),
        out_specs=P(("grp", "kin"), None, None),
        check_vma=False,
    )
```

```python
import functools

import jax
import jax.numpy as jnp
from jax import lax
from jax.experimental import pallas as pl
from jax.experimental.pallas import tpu as pltpu
from jax.sharding import PartitionSpec as P

NV = 4
NC = 4
NB = 8
NT = 16
BLK = 4
ROWS = BLK * NC * NC
CHUNK = 256
MESH = pl.DeviceIdType.MESH
F32 = jnp.float32
BF16 = jnp.bfloat16


def iota(shape, dim):
    return lax.broadcasted_iota(jnp.int32, shape, dim)


def mm(left, right):
    return jnp.dot(left, right, preferred_element_type=F32)


def mm_nt(left, right):
    return lax.dot_general(left, right, (((1,), (1,)), ((), ())), preferred_element_type=F32)


def hi_lo(value):
    high = value.astype(BF16)
    low = (value - high.astype(F32)).astype(BF16)
    return jnp.concatenate([high, low], 0)


def one_hot(cond):
    return jnp.where(cond, 1.0, 0.0).astype(BF16)


def conj_mul(lre, lim, rre, rim):
    return lre * rre + lim * rim, lre * rim - lim * rre


def kernel(
    groups, members, n_k, n_g,
    waves_h, vector_h, energies_h, basis, screening, coulomb_h, qmap_h, out,
    waves, vector, energies, coulomb, qmap, basis_v, screen_v, wrecv, vrecv, own_p, pair_p, own_d, s_own, s_a, s_plane, s_b, h_send, h_recv,
    small_sem, basis_sem, screen_sem, w_ssem, w_rsem, v_ssem, v_rsem, a_ssem, a_rsem, b_ssem, b_rsem, h_ssem, h_rsem,
):
    offset = groups // 4
    planes = 4
    block = members
    points = waves_h.shape[3]
    n_chunk = n_g // CHUNK
    grp = lax.axis_index("grp")
    kin = lax.axis_index("kin")
    plane = lax.div(grp, offset)
    spot = lax.rem(grp, offset)

    def at(dp, ds, dk):
        g = lax.rem(plane + dp, planes) * offset + lax.rem(spot + ds, offset)
        return (g, lax.rem(kin + dk, members))

    small = []
    pairs = [(waves_h, waves), (vector_h, vector), (energies_h, energies), (coulomb_h, coulomb), (qmap_h, qmap)]
    for i, (src, dst) in enumerate(pairs):
        small.append(pltpu.make_async_copy(src, dst, small_sem.at[i]))
        small[-1].start()
    basis_in = []
    for n in range(n_chunk):
        cols = pl.ds(n * CHUNK, CHUNK)
        copy = pltpu.make_async_copy(basis.at[:, :, cols], basis_v.at[:, :, cols], basis_sem.at[n])
        copy.start()
        basis_in.append(copy)
    screen_in = pltpu.make_async_copy(screening, screen_v, screen_sem)
    screen_in.start()

    mates = [(0, ds, dk) for ds in range(offset) for dk in range(members) if (ds, dk) != (0, 0)]
    others = [(dp, 0, dk) for dp in (1, 3) for dk in range(members)] + [(2, 0, 0)]
    barrier = pltpu.get_barrier_semaphore()
    for where in others + mates:
        pl.semaphore_signal(barrier, inc=1, device_id=at(*where), device_id_type=MESH)
    pl.semaphore_wait(barrier, len(others) + len(mates))

    def remote(src, dst, ssem, rsem, where):
        return pltpu.make_async_remote_copy(
            src_ref=src, dst_ref=dst, send_sem=ssem, recv_sem=rsem, device_id=at(*where), device_id_type=MESH
        )

    w_copies = []
    for i in range(members):
        w_copies.append(remote(waves_h, wrecv.at[pl.ds(i, 1)], w_ssem.at[i], w_rsem.at[i], (1, 0, i)))
        w_copies[-1].start()
    v_copies = []
    for i in range(members):
        v_copies.append(remote(vector_h, vrecv.at[pl.ds(i, 1)], v_ssem.at[i], v_rsem.at[i], (1, 0, i)))
        v_copies[-1].start()

    for copy in small:
        copy.wait()
    low_half = iota((8, points), 0) < 4
    own_re = waves[0, 0].astype(F32)
    own_im = waves[0, 1].astype(F32)

    def cond_twice(part):
        return jnp.concatenate([part[NV:], part[NV:]], 0)

    cre, cim = cond_twice(own_re), cond_twice(own_im)
    re_parts, im_parts = [], []
    for j in range(2):
        vre = jnp.where(low_half, own_re[2 * j:2 * j + 1], own_re[2 * j + 1:2 * j + 2])
        vim = jnp.where(low_half, own_im[2 * j:2 * j + 1], own_im[2 * j + 1:2 * j + 2])
        pre, pim = conj_mul(vre, vim, cre, cim)
        re_parts.append(pre)
        im_parts.append(pim)
    pre = jnp.concatenate(re_parts, 0)
    pim = jnp.concatenate(im_parts, 0)
    own_p[0:NT, 0:points] = pre.astype(BF16)
    own_p[0:NT, points:] = (-pim).astype(BF16)
    own_p[NT:2 * NT, 0:points] = pim.astype(BF16)
    own_p[NT:2 * NT, points:] = pre.astype(BF16)

    own_vec = vector[0]
    x_own = own_vec.astype(BF16).astype(F32)
    xr, xi = x_own[0:1], x_own[1:2]
    x_rows = jnp.concatenate(
        [jnp.concatenate([xr, -xi], 1), jnp.concatenate([xi, xr], 1), jnp.zeros((6, 2 * NT), F32)], 0
    ).astype(BF16)

    def basis_cols(n):
        cols = pl.ds(n * CHUNK, CHUNK)
        return jnp.concatenate([basis_v[0, :, cols], basis_v[1, :, cols]], 0)

    for n in range(n_chunk):
        basis_in[n].wait()
        cols = pl.ds(n * CHUNK, CHUNK)
        dens = mm(own_p[...], basis_cols(n)).astype(BF16)
        own_d[:, cols] = dens
        s_own[:, cols] = mm(x_rows, dens)[0:2]

    a_copies = []
    for i, where in enumerate(mates):
        a_copies.append(remote(s_own, s_a.at[i], a_ssem.at[i], a_rsem.at[i], where))
        a_copies[-1].start()

    side = 2 * ROWS
    row = iota((side, NT), 0)
    lane = iota((side, NT), 1)
    row_b = (row // 32) % 2 * 2 + (row // 4) % 2
    a_band = (row // 8) % 4
    b_band = row % 4
    col = iota((NT, side), 1)
    tr = iota((NT, side), 0)
    pick_v = one_hot((col // 8) % 4 == tr // 4)
    pick_w = one_hot(col % 4 == tr // 4)
    full_r = iota((side, side), 0)
    full_c = iota((side, side), 1)
    same_b = ((full_r // 32) % 2 == (full_c // 32) % 2) & ((full_r // 4) % 2 == (full_c // 4) % 2)
    r_im = full_r >= ROWS
    c_im = full_c >= ROWS
    same_comp = r_im == c_im
    sign = jnp.where(r_im, 1.0, -1.0)

    def spread(x_re, x_im, pick):
        xx_re = jnp.where(same_b, mm(x_re.astype(BF16), pick), 0.0)
        xx_im = jnp.where(same_b, mm(x_im.astype(BF16), pick), 0.0)
        return xx_re, xx_im

    own_rows_re = jnp.where(a_band == lane % 4, xr, 0.0)
    own_rows_im = jnp.where(a_band == lane % 4, xi, 0.0)
    oa_re, oa_im = spread(own_rows_re, own_rows_im, pick_v)
    h_re_w = jnp.where(same_comp, oa_re, -sign * oa_im)
    h_im_w = jnp.where(same_comp, oa_im, sign * oa_re)

    screen_in.wait()
    low_chunk = iota((8, CHUNK), 0) < 4
    base = lax.rem(grp + groups - offset, groups) * block
    s_done = False
    d_re = jnp.zeros((NC * 8, side), F32)
    d_im = jnp.zeros((NC * 8, side), F32)
    q_cat = jnp.concatenate([pick_v, pick_w], 0)
    h_copies = []
    for blk in range(members // BLK):
        slots = [blk * BLK + j for j in range(BLK)]
        for i in slots:
            w_copies[i].wait_recv()
            v_copies[i].wait_recv()

        for kind, first_band in ((0, NV), (1, 0)):
            for q in range(2):
                s0, s1 = slots[2 * q], slots[2 * q + 1]
                rre = jnp.concatenate(
                    [wrecv[s0, 0].astype(F32)[first_band:first_band + 4], wrecv[s1, 0].astype(F32)[first_band:first_band + 4]], 0)
                rim = jnp.concatenate(
                    [wrecv[s0, 1].astype(F32)[first_band:first_band + 4], wrecv[s1, 1].astype(F32)[first_band:first_band + 4]], 0)
                for half in range(2):
                    res, ims = [], []
                    for c in (2 * half, 2 * half + 1):
                        band = first_band + c
                        a, b = conj_mul(own_re[band:band + 1], own_im[band:band + 1], rre, rim)
                        res.append(a)
                        ims.append(b)
                    pre = jnp.concatenate(res, 0)
                    pim = jnp.concatenate(ims, 0)
                    r0 = kind * 2 * ROWS + q * 32 + half * 16
                    pair_p[r0:r0 + 16, 0:points] = pre.astype(BF16)
                    pair_p[r0:r0 + 16, points:] = (-pim).astype(BF16)
                    pair_p[r0 + ROWS:r0 + ROWS + 16, 0:points] = pim.astype(BF16)
                    pair_p[r0 + ROWS:r0 + ROWS + 16, points:] = pre.astype(BF16)

        rows_w = [qmap[0, base + lax.rem(kin + members - i, members)] for i in slots]
        kern = jnp.zeros((side, side), F32)
        for n in range(n_chunk):
            cols = pl.ds(n * CHUNK, CHUNK)
            dens = mm(pair_p[...], basis_cols(n)).astype(BF16)
            tiles = []
            for q in range(2):
                w0 = screen_v[pl.ds(rows_w[2 * q], 1), cols]
                w1 = screen_v[pl.ds(rows_w[2 * q + 1], 1), cols]
                tiles += [jnp.where(low_chunk, w0, w1)] * 4
            weight = jnp.concatenate(tiles * 2, 0)
            cond = (dens[0:side].astype(F32) * weight).astype(BF16)
            kern = kern + mm_nt(cond, dens[side:])
            if n == n_chunk // 2 and not s_done:
                s_done = True
                for copy in a_copies:
                    copy.wait_recv()
                total = s_own[...]
                for i in range(len(mates)):
                    total = total + s_a[i]
                s_plane[...] = total
                b_copies = []
                for i in range(planes - 1):
                    b_copies.append(remote(s_plane, s_b.at[i], b_ssem.at[i], b_rsem.at[i], (i + 1, 0, 0)))
                    b_copies[-1].start()

        part_re = jnp.zeros((side, NT), F32)
        part_im = jnp.zeros((side, NT), F32)
        for j, i in enumerate(slots):
            xb = vrecv[i].astype(BF16).astype(F32)
            hit = (row_b == j) & (b_band == lane % 4)
            part_re = part_re + jnp.where(hit, xb[0:1], 0.0)
            part_im = part_im + jnp.where(hit, xb[1:2], 0.0)
        pa_re, pa_im = spread(part_re, part_im, pick_w)
        d_re_w = jnp.where(same_comp, pa_re, sign * pa_im)
        d_im_w = jnp.where(same_comp, pa_im, -sign * pa_re)

        def fold_d(value):
            return value[0:32] + value[32:64] + value[64:96] + value[96:128]

        def fold_h(value):
            halves = value[0:64] + value[64:128]
            return jnp.concatenate(
                [halves[32 * q:32 * q + 8] + halves[32 * q + 8:32 * q + 16]
                 + halves[32 * q + 16:32 * q + 24] + halves[32 * q + 24:32 * q + 32] for q in range(2)], 0)

        d_re = d_re + fold_d(kern * d_re_w)
        d_im = d_im + fold_d(kern * d_im_w)
        h_rows = jnp.concatenate([fold_h(kern * h_re_w), fold_h(kern * h_im_w)], 0)
        h_sums = mm_nt(hi_lo(h_rows), pick_w)
        h_sums = h_sums[0:32] + h_sums[32:64]
        hr = iota((32, NT), 0)
        hl = iota((32, NT), 1)
        h_sums = jnp.where(hr % 4 == hl % 4, h_sums, 0.0)
        for j, i in enumerate(slots):
            for comp in range(2):
                r0 = comp * 16 + j // 2 * 8
                mine = jnp.where((iota((8, NT), 0) // 4) == j % 2, h_sums[r0:r0 + 8], 0.0)
                h_send[i, comp:comp + 1] = jnp.sum(mine, 0, keepdims=True)
        for i in slots:
            h_copies.append(remote(h_send.at[i], h_recv.at[i], h_ssem.at[i], h_rsem.at[i], (3, 0, members - i)))
            h_copies[-1].start()

    d_sums = mm_nt(hi_lo(jnp.concatenate([d_re, d_im], 0)), pick_v)
    d_sums = d_sums[0:64] + d_sums[64:128]
    dr = iota((64, NT), 0)
    dl = iota((64, NT), 1)
    d_sums = jnp.where((dr // 8) % 4 == dl % 4, d_sums, 0.0)
    direct = jnp.concatenate(
        [jnp.sum(d_sums[0:32], 0, keepdims=True), jnp.sum(d_sums[32:64], 0, keepdims=True)], 0)

    total = s_plane[...]
    for i in range(planes - 1):
        b_copies[i].wait_recv()
        total = total + s_b[i]
    pot = coulomb[...].reshape(1, n_g) * total
    pot_rows = jnp.concatenate([hi_lo(pot), jnp.zeros((4, n_g), BF16)], 0)
    ex = mm_nt(pot_rows, own_d[...])
    ex = ex[0:2] + ex[2:4]
    ex_re = ex[0:1, 0:NT] + ex[1:2, NT:]
    ex_im = ex[1:2, 0:NT] - ex[0:1, NT:]
    exchange = jnp.concatenate([ex_re, ex_im], 0)

    scale = 1.0 / n_k
    result = energies[...] * own_vec + (2.0 * scale) * exchange - scale * direct
    back = jnp.zeros((2, NT), F32)
    for i in range(members):
        h_copies[i].wait_recv()
        back = back + h_recv[i]
    out[0] = result - scale * back

    for copy in w_copies + v_copies + a_copies + b_copies + h_copies:
        copy.wait_send()


def on_device(waves, vector, energies, basis, screening, coulomb, qmap):
    groups = lax.axis_size("grp")
    members = lax.axis_size("kin")
    offset = groups // 4
    n_mates = offset * members - 1
    points = waves.shape[3]
    n_g = basis.shape[2]
    vmem = pl.BlockSpec(memory_space=pltpu.VMEM)
    hbm = pl.BlockSpec(memory_space=pl.ANY)
    dma = pltpu.SemaphoreType.DMA
    return pl.pallas_call(
        functools.partial(kernel, groups, members, groups * members, n_g),
        out_shape=jax.ShapeDtypeStruct(vector.shape, F32),
        in_specs=[hbm] * 7,
        out_specs=vmem,
        scratch_shapes=[
            pltpu.VMEM(waves.shape, BF16),
            pltpu.VMEM(vector.shape, F32),
            pltpu.VMEM(energies.shape, F32),
            pltpu.VMEM(coulomb.shape, F32),
            pltpu.SMEM(qmap.shape, jnp.int32),
            pltpu.VMEM(basis.shape, BF16),
            pltpu.VMEM(screening.shape, F32),
            pltpu.VMEM((members,) + waves.shape[1:], BF16),
            pltpu.VMEM((members, 2, NT), F32),
            pltpu.VMEM((2 * NT, 2 * points), BF16),
            pltpu.VMEM((4 * ROWS, 2 * points), BF16),
            pltpu.VMEM((2 * NT, n_g), BF16),
            pltpu.VMEM((2, n_g), F32),
            pltpu.VMEM((n_mates, 2, n_g), F32),
            pltpu.VMEM((2, n_g), F32),
            pltpu.VMEM((3, 2, n_g), F32),
            pltpu.VMEM((members, 2, NT), F32),
            pltpu.VMEM((members, 2, NT), F32),
            dma((5,)),
            dma((n_g // CHUNK,)),
            dma,
            dma((members,)), dma((members,)),
            dma((members,)), dma((members,)),
            dma((n_mates,)), dma((n_mates,)),
            dma((3,)), dma((3,)),
            dma((members,)), dma((members,)),
        ],
        compiler_params=pltpu.CompilerParams(
            collective_id=0, has_side_effects=True, vmem_limit_bytes=60 * 1024 * 1024
        ),
    )(waves, vector, energies, basis, screening, coulomb, qmap)


def solution(mesh):
    return jax.shard_map(
        on_device,
        mesh=mesh,
        in_specs=(
            P(("grp", "kin"), None, None, None),
            P(("grp", "kin"), None, None),
            P(("grp", "kin"), None),
            P(),
            P(),
            P(),
            P(("grp", "kin"), None),
        ),
        out_specs=P(("grp", "kin"), None, None),
        check_vma=False,
    )
```

```python
import functools

import jax
import jax.numpy as jnp
from jax import lax
from jax.experimental import pallas as pl
from jax.experimental.pallas import tpu as pltpu
from jax.sharding import PartitionSpec as P

NV = 4
NC = 4
NT = 16
TEAM = 4
ROWS = TEAM * NT
MESH = pl.DeviceIdType.MESH
F32 = jnp.float32
BF16 = jnp.bfloat16


def iota(shape, dim):
    return lax.broadcasted_iota(jnp.int32, shape, dim)


def mm(left, right):
    return jnp.dot(left, right, preferred_element_type=F32)


def mm_nt(left, right):
    return lax.dot_general(left, right, (((1,), (1,)), ((), ())), preferred_element_type=F32)


def hi_lo(value):
    high = value.astype(BF16)
    low = (value - high.astype(F32)).astype(BF16)
    return jnp.concatenate([high, low], 0)


def one_hot(cond):
    return jnp.where(cond, 1.0, 0.0).astype(BF16)


def conj_mul(lre, lim, rre, rim):
    return lre * rre + lim * rim, lre * rim - lim * rre


def twice(rows):
    return jnp.concatenate([rows, rows], 0)


def kernel(
    groups, members, n_g,
    waves_h, vector_h, energies_h, basis_h, screening_h, coulomb_h, qmap_h, out,
    vector, energies, coulomb, qmap, basis, screening,
    stage, team, part, left, weights, weights_in, own_p, pair_p, own_d, s_own, s_in, h_send, h_recv, t_send, t_recv,
    small_sem, basis_sem, screen_sem, t_ssem, t_rsem, p_ssem, p_rsem, r_ssem, r_rsem,
    w_ssem, w_rsem, s_ssem, s_rsem, h_ssem, h_rsem, d_ssem, d_rsem,
):
    offset = groups // 4
    half = members // 2
    teams = members // TEAM
    n_k = groups * members
    points = waves_h.shape[3]
    quarter = n_g // TEAM
    grp = lax.axis_index("grp")
    kin = lax.axis_index("kin")
    rank = lax.rem(kin, TEAM)
    sib = kin + 1 - 2 * lax.rem(kin, 2)

    def mate(s, who=kin):
        who = who + (s % 2) * (1 - 2 * lax.rem(who, 2))
        return who + (s // 2) * (2 - 4 * lax.rem(lax.div(who, 2), 2))

    def source(i):
        if i < half:
            return lax.rem(kin + members - 2 * i, members)
        return lax.rem(sib + members - 2 * (i - half), members)

    up = lax.rem(grp + offset, groups)
    down = lax.rem(grp + groups - offset, groups)

    my_cols = pl.ds(pl.multiple_of(rank * quarter, 128), quarter)
    pairs = [
        (waves_h.at[0], stage.at[:, :, 0:points]), (vector_h, vector), (qmap_h, qmap),
        (energies_h, energies), (coulomb_h, coulomb),
    ]
    small = []
    for i, (src, dst) in enumerate(pairs):
        small.append(pltpu.make_async_copy(src, dst, small_sem.at[i]))
        small[-1].start()
    screen_in = pltpu.make_async_copy(screening_h, screening, screen_sem)
    screen_in.start()
    basis_in = pltpu.make_async_copy(basis_h.at[:, :, my_cols], basis, basis_sem)
    basis_in.start()

    rel_s = [(dg, dt) for dg in range(groups) for dt in range(teams) if (dg, dt) != (0, 0)]

    def s_target(dg, dt):
        return (lax.rem(grp + dg, groups), lax.rem(kin + dt * TEAM, members))

    barrier = pltpu.get_barrier_semaphore()
    greet = [s_target(dg, dt) for dg, dt in rel_s] + [(grp, mate(s)) for s in range(1, TEAM)]
    for dk in range(members):
        if dk % TEAM:
            greet += [(up, lax.rem(kin + dk, members)), (down, lax.rem(kin + dk, members))]
    for target in greet:
        pl.semaphore_signal(barrier, inc=1, device_id=target, device_id_type=MESH)

    for copy in small:
        copy.wait()
    own_vec = vector[0]
    x_pad = jnp.concatenate([own_vec, jnp.zeros((2, 128 - NT), F32)], 1)
    for comp in range(2):
        stage[comp, :, points:] = jnp.broadcast_to(x_pad[comp:comp + 1], (8, 128)).astype(BF16)
    pl.semaphore_wait(barrier, len(greet))

    def remote(src, dst, ssem, rsem, target):
        return pltpu.make_async_remote_copy(
            src_ref=src, dst_ref=dst, send_sem=ssem, recv_sem=rsem, device_id=target, device_id_type=MESH
        )

    started = []

    def go(copy):
        copy.start()
        started.append(copy)
        return copy

    team_in = [None] * TEAM
    for s in (2, 1):
        team_in[s] = go(remote(stage, team.at[s], t_ssem.at[s], t_rsem.at[s], (grp, mate(s))))
    part_in = [None] * members
    for i in range(half):
        part_in[i] = go(remote(stage, part.at[i], p_ssem.at[i], p_rsem.at[i], (up, lax.rem(kin + 2 * i, members))))

    screen_in.wait()
    base = down * members
    for b in range(members):
        weights[b:b + 1, :] = screening[pl.ds(qmap[0, base + b], 1), :]
    weight_in = [None] * TEAM
    for s in range(1, TEAM):
        cols = pl.ds(pl.multiple_of(lax.rem(mate(s), TEAM) * quarter, 128), quarter)
        weight_in[s] = go(remote(weights.at[:, cols], weights_in.at[s], w_ssem.at[s], w_rsem.at[s], (grp, mate(s))))
    weights_in[0] = weights[:, my_cols]

    side = 2 * ROWS
    col = iota((NT, side), 1)
    tr = iota((NT, side), 0)
    pick_v = one_hot((col // 4) % 4 == tr // 4)
    pick_w = one_hot(col % 4 == tr // 4)
    same_a = (iota((side, side), 0) // NT) % TEAM == (iota((side, side), 1) // NT) % TEAM
    first = iota((8, side), 1) < ROWS
    low_half = iota((8, points), 0) < 4
    row8 = iota((8, NT), 0)
    lane8 = iota((8, NT), 1)

    xs = []
    team_in[3] = remote(team.at[2], team.at[3], t_ssem.at[3], t_rsem.at[3], (grp, sib))
    for s in range(TEAM):
        if s == 1:
            team_in[2].wait_recv()
            go(team_in[3])
        if s in (1, 3):
            team_in[s].wait_recv()
        src = stage if s == 0 else team.at[s]
        wre = src[0, :, 0:points].astype(F32)
        wim = src[1, :, 0:points].astype(F32)
        xs.append((src[0, :, points:].astype(F32)[0:1, 0:NT], src[1, :, points:].astype(F32)[0:1, 0:NT]))
        cre, cim = twice(wre[NV:]), twice(wim[NV:])
        res, ims = [], []
        for h in range(4):
            lre = jnp.where(low_half, wre[2 * h:2 * h + 1], wre[2 * h + 1:2 * h + 2])
            lim = jnp.where(low_half, wim[2 * h:2 * h + 1], wim[2 * h + 1:2 * h + 2])
            left[s, h, 0] = lre
            left[s, h, 1] = lim
            if h < 2:
                pre, pim = conj_mul(lre, lim, cre, cim)
                res.append(pre)
                ims.append(pim)
        pre = jnp.concatenate(res, 0)
        pim = jnp.concatenate(ims, 0)
        r0 = s * NT
        own_p[r0:r0 + NT, 0:points] = pre.astype(BF16)
        own_p[r0:r0 + NT, points:] = (-pim).astype(BF16)
        own_p[ROWS + r0:ROWS + r0 + NT, 0:points] = pim.astype(BF16)
        own_p[ROWS + r0:ROWS + r0 + NT, points:] = pre.astype(BF16)

    xr = jnp.concatenate([x[0] for x in xs], 1)
    xi = jnp.concatenate([x[1] for x in xs], 1)
    x_rows = jnp.concatenate(
        [jnp.concatenate([xr, -xi], 1), jnp.concatenate([xi, xr], 1), jnp.zeros((6, side), F32)], 0
    ).astype(BF16)

    basis_in.wait()
    dens = mm(own_p[...], basis[...].reshape(2 * points, quarter)).astype(BF16)
    own_d[...] = dens
    s_own[...] = mm(x_rows, dens)[0:2]
    s_copies = []
    for i, (dg, dt) in enumerate(rel_s):
        s_copies.append(go(remote(s_own, s_in.at[i], s_ssem.at[i], s_rsem.at[i], s_target(dg, dt))))

    a_re, a_im = [], []
    for s in range(TEAM):
        for c in range(0, NC, 2):
            hit = lane8 % 4 == c + row8 // 4
            a_re.append(jnp.where(hit, xs[s][0], 0.0))
            a_im.append(jnp.where(hit, xs[s][1], 0.0))
    spread = mm(jnp.concatenate(a_re + a_im, 0).astype(BF16), pick_v)
    a_re, a_im = spread[0:ROWS], spread[ROWS:]
    first_all = iota((ROWS, side), 1) < ROWS
    u1 = jnp.where(first_all, a_re, a_im)
    u2 = jnp.where(first_all, -a_im, a_re)

    for s in range(1, TEAM):
        weight_in[s].wait_recv()

    d_re = jnp.zeros((ROWS, side), F32)
    d_im = jnp.zeros((ROWS, side), F32)
    exchange = None
    h_copies = []
    for i in range(members):
        if i >= half:
            part_in[i] = remote(part.at[i - half], part.at[i], r_ssem.at[i - half], r_rsem.at[i - half], (grp, sib))
        part_in[i].wait_recv()
        if i < half:
            go(remote(part.at[i], part.at[half + i], r_ssem.at[i], r_rsem.at[i], (grp, sib)))
        if i == members - 1:
            total = s_own[...]
            for j, copy in enumerate(s_copies):
                copy.wait_recv()
                total = total + s_in[j]
            pot = coulomb[my_cols].reshape(1, quarter) * total
            ex = mm_nt(jnp.concatenate([hi_lo(pot), jnp.zeros((4, quarter), BF16)], 0), own_d[...])
            ex = ex[0:2] + ex[2:4]
            exchange = jnp.concatenate(
                [ex[0:1, 0:ROWS] + ex[1:2, ROWS:], ex[1:2, 0:ROWS] - ex[0:1, ROWS:]], 0)

        slot = i % 2
        wre = part[i, 0, :, 0:points].astype(F32)
        wim = part[i, 1, :, 0:points].astype(F32)
        for kind in range(2):
            rows = slice(NV, NV + NC) if kind == 0 else slice(0, NV)
            rre, rim = twice(wre[rows]), twice(wim[rows])
            for s in range(TEAM):
                res, ims = [], []
                for h in range(2):
                    t = h + 2 - 2 * kind
                    pre, pim = conj_mul(left[s, t, 0], left[s, t, 1], rre, rim)
                    res.append(pre)
                    ims.append(pim)
                pre = jnp.concatenate(res, 0)
                pim = jnp.concatenate(ims, 0)
                r0 = kind * side + s * NT
                pair_p[slot, r0:r0 + NT, 0:points] = pre.astype(BF16)
                pair_p[slot, r0:r0 + NT, points:] = (-pim).astype(BF16)
                pair_p[slot, ROWS + r0:ROWS + r0 + NT, 0:points] = pim.astype(BF16)
                pair_p[slot, ROWS + r0:ROWS + r0 + NT, points:] = pre.astype(BF16)

        dens = mm(pair_p[slot], basis[...].reshape(2 * points, quarter)).astype(BF16)
        b = source(i)
        weight = jnp.concatenate(
            [jnp.broadcast_to(weights_in[s, pl.ds(b, 1), :], (NT, quarter)) for s in range(TEAM)] * 2, 0)
        cond = (dens[0:side].astype(F32) * weight).astype(BF16)
        kern = jnp.where(same_a, mm_nt(cond, dens[side:]), 0.0)
        k_re, k_im = kern[0:ROWS], kern[ROWS:]

        h_re = k_re * u1 + k_im * u2
        h_im = k_im * u1 - k_re * u2

        def fold(value):
            total = value[0:8]
            for r in range(8, ROWS, 8):
                total = total + value[r:r + 8]
            return total

        h_sums = mm_nt(hi_lo(jnp.concatenate([fold(h_re), fold(h_im)], 0)), pick_w)
        h_sums = h_sums[0:16] + h_sums[16:32]
        hit = row8 % 4 == lane8 % 4
        h_send[i] = jnp.concatenate(
            [jnp.sum(jnp.where(hit, h_sums[0:8], 0.0), 0, keepdims=True),
             jnp.sum(jnp.where(hit, h_sums[8:16], 0.0), 0, keepdims=True)], 0)
        h_copies.append(go(remote(h_send.at[i], h_recv.at[i], h_ssem.at[i], h_rsem.at[i], (down, b))))

        xbr = part[i, 0, :, points:].astype(F32)[:, 0:NT]
        xbi = part[i, 1, :, points:].astype(F32)[:, 0:NT]
        xx = mm(jnp.concatenate([jnp.where(hit, xbr, 0.0), jnp.where(hit, xbi, 0.0)], 0).astype(BF16), pick_w)
        w1 = jnp.where(first, xx[0:8], -xx[8:16])
        w2 = jnp.where(first, xx[8:16], xx[0:8])
        w1 = jnp.concatenate([w1] * (ROWS // 8), 0)
        w2 = jnp.concatenate([w2] * (ROWS // 8), 0)
        d_re = d_re + (k_re * w1 + k_im * w2)
        d_im = d_im + (k_re * w2 - k_im * w1)

    scale = 1.0 / n_k
    d_sums = mm_nt(hi_lo(jnp.concatenate([d_re, d_im], 0)), pick_v)
    d_sums = d_sums[0:side] + d_sums[side:]
    d_sums = jnp.where((iota((side, NT), 0) // 4) % 4 == iota((side, NT), 1) % 4, d_sums, 0.0)
    mine = None
    d_copies = []
    for s in (3, 2, 1, 0):
        direct = jnp.concatenate(
            [jnp.sum(d_sums[r:r + NT], 0, keepdims=True) for r in (s * NT, ROWS + s * NT)], 0)
        both = (2.0 * scale) * exchange[:, s * NT:(s + 1) * NT] - scale * direct
        if s == 0:
            mine = both
        else:
            t_send[s] = both
            d_copies.append(go(remote(t_send.at[s], t_recv.at[s], d_ssem.at[s], d_rsem.at[s], (grp, mate(s)))))

    result = energies[...] * own_vec + mine
    for copy in h_copies:
        copy.wait_recv()
    back = h_recv[0]
    for i in range(1, members):
        back = back + h_recv[i]
    for copy in d_copies:
        copy.wait_recv()
    for s in range(1, TEAM):
        result = result + t_recv[s]
    out[0] = result - scale * back

    for copy in started:
        copy.wait_send()


def on_device(waves, vector, energies, basis, screening, coulomb, qmap):
    groups = lax.axis_size("grp")
    members = lax.axis_size("kin")
    half = members // 2
    n_s = groups * (members // TEAM) - 1
    points = waves.shape[3]
    n_g = basis.shape[2]
    quarter = n_g // TEAM
    any_space = pl.BlockSpec(memory_space=pl.ANY)
    dma = pltpu.SemaphoreType.DMA
    vmem = pltpu.VMEM
    stage = (2, 8, points + 128)
    return pl.pallas_call(
        functools.partial(kernel, groups, members, n_g),
        out_shape=jax.ShapeDtypeStruct(vector.shape, F32),
        in_specs=[any_space] * 7,
        out_specs=pl.BlockSpec(memory_space=vmem),
        scratch_shapes=[
            vmem(vector.shape, F32),
            vmem(energies.shape, F32),
            vmem(coulomb.shape, F32),
            pltpu.SMEM(qmap.shape, jnp.int32),
            vmem((2, points, quarter), BF16),
            vmem(screening.shape, F32),
            vmem(stage, BF16),
            vmem((TEAM,) + stage, BF16),
            vmem((members,) + stage, BF16),
            vmem((TEAM, 4, 2, 8, points), F32),
            vmem((members, n_g), F32),
            vmem((TEAM, members, quarter), F32),
            vmem((2 * ROWS, 2 * points), BF16),
            vmem((2, 4 * ROWS, 2 * points), BF16),
            vmem((2 * ROWS, quarter), BF16),
            vmem((2, quarter), F32),
            vmem((n_s, 2, quarter), F32),
            vmem((members, 2, NT), F32),
            vmem((members, 2, NT), F32),
            vmem((TEAM, 2, NT), F32),
            vmem((TEAM, 2, NT), F32),
            dma((5,)), dma, dma,
            dma((TEAM,)), dma((TEAM,)),
            dma((half,)), dma((half,)),
            dma((half,)), dma((half,)),
            dma((TEAM,)), dma((TEAM,)),
            dma((n_s,)), dma((n_s,)),
            dma((members,)), dma((members,)),
            dma((TEAM,)), dma((TEAM,)),
        ],
        compiler_params=pltpu.CompilerParams(
            collective_id=0, has_side_effects=True, vmem_limit_bytes=60 * 1024 * 1024
        ),
    )(waves, vector, energies, basis, screening, coulomb, qmap)


def solution(mesh):
    return jax.shard_map(
        on_device,
        mesh=mesh,
        in_specs=(
            P(("grp", "kin"), None, None, None),
            P(("grp", "kin"), None, None),
            P(("grp", "kin"), None),
            P(),
            P(),
            P(),
            P(("grp", "kin"), None),
        ),
        out_specs=P(("grp", "kin"), None, None),
        check_vma=False,
    )
```

```python
import functools

import jax
import jax.numpy as jnp
from jax import lax
from jax.experimental import pallas as pl
from jax.experimental.pallas import tpu as pltpu
from jax.sharding import PartitionSpec as P

NV = 4
NC = 4
NT = 16
TEAM = 4
ROWS = TEAM * NT
MESH = pl.DeviceIdType.MESH
F32 = jnp.float32
BF16 = jnp.bfloat16


def iota(shape, dim):
    return lax.broadcasted_iota(jnp.int32, shape, dim)


def mm(left, right):
    return jnp.dot(left, right, preferred_element_type=F32)


def mm_nt(left, right):
    return lax.dot_general(left, right, (((1,), (1,)), ((), ())), preferred_element_type=F32)


def hi_lo(value):
    high = value.astype(BF16)
    low = (value - high.astype(F32)).astype(BF16)
    return jnp.concatenate([high, low], 0)


def one_hot(cond):
    return jnp.where(cond, 1.0, 0.0).astype(BF16)


def conj_mul(lre, lim, rre, rim):
    return lre * rre + lim * rim, lre * rim - lim * rre


def twice(rows):
    return jnp.concatenate([rows, rows], 0)


def kernel(
    groups, members, n_g,
    waves_h, vector_h, energies_h, basis_h, screening_h, coulomb_h, qmap_h, out,
    vector, energies, coulomb, qmap, basis, screening,
    stage, team, part, left, weights, weights_in, own_p, pair_p, own_d, s_own, s_in, h_send, h_recv, t_send, t_recv, d_sum, ex_sum,
    small_sem, basis_sem, screen_sem, t_ssem, t_rsem, p_ssem, p_rsem, r_ssem,
    w_ssem, w_rsem, s_ssem, s_rsem, h_ssem, h_rsem, d_ssem, d_rsem,
):
    offset = groups // 4
    half = members // 2
    teams = members // TEAM
    n_k = groups * members
    points = waves_h.shape[3]
    quarter = n_g // TEAM
    grp = lax.axis_index("grp")
    kin = lax.axis_index("kin")
    rank = lax.rem(kin, TEAM)
    sib = kin + 1 - 2 * lax.rem(kin, 2)

    def mate(s, who=kin):
        who = who + (s % 2) * (1 - 2 * lax.rem(who, 2))
        return who + (s // 2) * (2 - 4 * lax.rem(lax.div(who, 2), 2))

    def source(i):
        relayed = lax.div(i, half)
        who = kin + relayed * (sib - kin)
        return lax.rem(who + members - 2 * (i - relayed * half), members)

    up = lax.rem(grp + offset, groups)
    down = lax.rem(grp + groups - offset, groups)

    rel_s = [(dg, dt) for dg in range(groups) for dt in range(teams) if (dg, dt) != (0, 0)]

    def s_target(dg, dt):
        return (lax.rem(grp + dg, groups), lax.rem(kin + dt * TEAM, members))

    barrier = pltpu.get_barrier_semaphore()
    greet = [s_target(dg, dt) for dg, dt in rel_s] + [(grp, mate(s)) for s in range(1, TEAM)]
    for dk in range(members):
        if dk % TEAM:
            greet += [(up, lax.rem(kin + dk, members)), (down, lax.rem(kin + dk, members))]
    for target in greet:
        pl.semaphore_signal(barrier, inc=1, device_id=target, device_id_type=MESH)

    my_cols = pl.ds(pl.multiple_of(rank * quarter, 128), quarter)
    pairs = [
        (waves_h.at[0], stage.at[:, :, 0:points]), (vector_h, vector), (qmap_h, qmap),
        (energies_h, energies), (coulomb_h, coulomb),
    ]
    small = []
    for i, (src, dst) in enumerate(pairs):
        small.append(pltpu.make_async_copy(src, dst, small_sem.at[i]))
        small[-1].start()
    screen_in = pltpu.make_async_copy(screening_h, screening, screen_sem)
    screen_in.start()
    basis_in = pltpu.make_async_copy(basis_h.at[:, :, my_cols], basis, basis_sem)
    basis_in.start()

    for copy in small:
        copy.wait()
    own_vec = vector[0]
    x_pad = jnp.concatenate([own_vec, jnp.zeros((2, 128 - NT), F32)], 1)
    for comp in range(2):
        stage[comp, :, points:] = jnp.broadcast_to(x_pad[comp:comp + 1], (8, 128)).astype(BF16)
    pl.semaphore_wait(barrier, len(greet))

    def remote(src, dst, ssem, rsem, target):
        return pltpu.make_async_remote_copy(
            src_ref=src, dst_ref=dst, send_sem=ssem, recv_sem=rsem, device_id=target, device_id_type=MESH
        )

    started = []

    def go(copy):
        copy.start()
        started.append(copy)
        return copy

    team_in = [None] * TEAM
    for s in (2, 1):
        team_in[s] = go(remote(stage, team.at[s], t_ssem.at[s], t_rsem.at[s], (grp, mate(s))))
    part_in = [None] * members
    for i in range(half):
        part_in[i] = go(remote(stage, part.at[i], p_ssem.at[i], p_rsem.at[i], (up, lax.rem(kin + 2 * i, members))))

    screen_in.wait()
    base = down * members
    for b in range(members):
        weights[b:b + 1, :] = screening[pl.ds(qmap[0, base + b], 1), :]
    weight_in = [None] * TEAM
    for s in range(1, TEAM):
        cols = pl.ds(pl.multiple_of(lax.rem(mate(s), TEAM) * quarter, 128), quarter)
        weight_in[s] = go(remote(weights.at[:, cols], weights_in.at[s], w_ssem.at[s], w_rsem.at[s], (grp, mate(s))))
    weights_in[0] = weights[:, my_cols]

    side = 2 * ROWS
    col = iota((NT, side), 1)
    tr = iota((NT, side), 0)
    pick_v = one_hot((col // 4) % 4 == tr // 4)
    pick_w = one_hot(col % 4 == tr // 4)
    same_a = (iota((side, side), 0) // NT) % TEAM == (iota((side, side), 1) // NT) % TEAM
    first = iota((8, side), 1) < ROWS
    low_half = iota((8, points), 0) < 4
    row8 = iota((8, NT), 0)
    lane8 = iota((8, NT), 1)

    team_in[3] = remote(team.at[2], team.at[3], t_ssem.at[3], t_rsem.at[3], (grp, sib))

    def team_step(s, carry):
        @pl.when(s == 1)
        def _():
            team_in[2].wait_recv()
            team_in[3].start()
            team_in[1].wait_recv()

        @pl.when(s == 3)
        def _():
            team_in[3].wait_recv()

        wre = team[s, 0, :, 0:points].astype(F32)
        wim = team[s, 1, :, 0:points].astype(F32)
        cre, cim = twice(wre[NV:]), twice(wim[NV:])
        res, ims = [], []
        for h in range(4):
            lre = jnp.where(low_half, wre[2 * h:2 * h + 1], wre[2 * h + 1:2 * h + 2])
            lim = jnp.where(low_half, wim[2 * h:2 * h + 1], wim[2 * h + 1:2 * h + 2])
            left[s, h, 0] = lre
            left[s, h, 1] = lim
            if h < 2:
                pre, pim = conj_mul(lre, lim, cre, cim)
                res.append(pre)
                ims.append(pim)
        pre = jnp.concatenate(res, 0)
        pim = jnp.concatenate(ims, 0)
        re_rows = pl.ds(pl.multiple_of(s * NT, NT), NT)
        im_rows = pl.ds(pl.multiple_of(ROWS + s * NT, NT), NT)
        own_p[re_rows, 0:points] = pre.astype(BF16)
        own_p[re_rows, points:] = (-pim).astype(BF16)
        own_p[im_rows, 0:points] = pim.astype(BF16)
        own_p[im_rows, points:] = pre.astype(BF16)
        return carry

    team[0] = stage[...]
    lax.fori_loop(0, TEAM, team_step, 0)
    started.append(team_in[3])
    xs = []
    for s in range(TEAM):
        xs.append((team[s, 0, :, points:].astype(F32)[0:1, 0:NT], team[s, 1, :, points:].astype(F32)[0:1, 0:NT]))

    xr = jnp.concatenate([x[0] for x in xs], 1)
    xi = jnp.concatenate([x[1] for x in xs], 1)
    x_rows = jnp.concatenate(
        [jnp.concatenate([xr, -xi], 1), jnp.concatenate([xi, xr], 1), jnp.zeros((6, side), F32)], 0
    ).astype(BF16)

    basis_in.wait()
    dens = mm(own_p[...], basis[...].reshape(2 * points, quarter)).astype(BF16)
    own_d[...] = dens
    s_own[...] = mm(x_rows, dens)[0:2]
    s_copies = []
    for i, (dg, dt) in enumerate(rel_s):
        s_copies.append(go(remote(s_own, s_in.at[i], s_ssem.at[i], s_rsem.at[i], s_target(dg, dt))))

    a_re, a_im = [], []
    for s in range(TEAM):
        for c in range(0, NC, 2):
            hit = lane8 % 4 == c + row8 // 4
            a_re.append(jnp.where(hit, xs[s][0], 0.0))
            a_im.append(jnp.where(hit, xs[s][1], 0.0))
    spread = mm(jnp.concatenate(a_re + a_im, 0).astype(BF16), pick_v)
    a_re, a_im = spread[0:ROWS], spread[ROWS:]
    first_all = iota((ROWS, side), 1) < ROWS
    u1 = jnp.where(first_all, a_re, a_im)
    u2 = jnp.where(first_all, -a_im, a_re)

    for s in range(1, TEAM):
        weight_in[s].wait_recv()

    d_sum[...] = jnp.zeros((side, side), F32)

    def relay(i):
        return remote(part.at[i], part.at[half + i], r_ssem.at[i], p_rsem.at[half + i], (grp, sib))

    def h_copy(i):
        return remote(h_send.at[i], h_recv.at[i], h_ssem.at[i], h_rsem.at[i], (down, source(i)))

    def partner_step(i, carry):
        remote(stage, part.at[i], p_ssem.at[0], p_rsem.at[i], (up, kin)).wait_recv()

        @pl.when(i < half)
        def _():
            relay(i).start()

        @pl.when(i == members - 1)
        def _():
            total = s_own[...]
            for j, copy in enumerate(s_copies):
                copy.wait_recv()
                total = total + s_in[j]
            pot = coulomb[my_cols].reshape(1, quarter) * total
            ex = mm_nt(jnp.concatenate([hi_lo(pot), jnp.zeros((4, quarter), BF16)], 0), own_d[...])
            ex = ex[0:2] + ex[2:4]
            ex_sum[...] = jnp.concatenate(
                [ex[0:1, 0:ROWS] + ex[1:2, ROWS:], ex[1:2, 0:ROWS] - ex[0:1, ROWS:]], 0)

        wre = part[i, 0, :, 0:points].astype(F32)
        wim = part[i, 1, :, 0:points].astype(F32)
        right = [(twice(wre[NV:]), twice(wim[NV:])), (twice(wre[0:NV]), twice(wim[0:NV]))]

        def product_step(s, carry):
            for kind in range(2):
                res, ims = [], []
                for h in range(2):
                    t = h + 2 - 2 * kind
                    pre, pim = conj_mul(left[s, t, 0], left[s, t, 1], *right[kind])
                    res.append(pre)
                    ims.append(pim)
                pre = jnp.concatenate(res, 0)
                pim = jnp.concatenate(ims, 0)
                re_rows = pl.ds(pl.multiple_of(kind * side + s * NT, NT), NT)
                im_rows = pl.ds(pl.multiple_of(kind * side + ROWS + s * NT, NT), NT)
                pair_p[re_rows, 0:points] = pre.astype(BF16)
                pair_p[re_rows, points:] = (-pim).astype(BF16)
                pair_p[im_rows, 0:points] = pim.astype(BF16)
                pair_p[im_rows, points:] = pre.astype(BF16)
            return carry

        lax.fori_loop(0, TEAM, product_step, 0)

        dens = mm(pair_p[...], basis[...].reshape(2 * points, quarter)).astype(BF16)
        b = source(i)
        weight = jnp.concatenate(
            [jnp.broadcast_to(weights_in[s, pl.ds(b, 1), :], (NT, quarter)) for s in range(TEAM)] * 2, 0)
        cond = (dens[0:side].astype(F32) * weight).astype(BF16)
        kern = jnp.where(same_a, mm_nt(cond, dens[side:]), 0.0)
        k_re, k_im = kern[0:ROWS], kern[ROWS:]

        h_re = k_re * u1 + k_im * u2
        h_im = k_im * u1 - k_re * u2

        def fold(value):
            total = value[0:8]
            for r in range(8, ROWS, 8):
                total = total + value[r:r + 8]
            return total

        h_sums = mm_nt(hi_lo(jnp.concatenate([fold(h_re), fold(h_im)], 0)), pick_w)
        h_sums = h_sums[0:16] + h_sums[16:32]
        hit = row8 % 4 == lane8 % 4
        h_send[i] = jnp.concatenate(
            [jnp.sum(jnp.where(hit, h_sums[0:8], 0.0), 0, keepdims=True),
             jnp.sum(jnp.where(hit, h_sums[8:16], 0.0), 0, keepdims=True)], 0)
        h_copy(i).start()

        xbr = part[i, 0, :, points:].astype(F32)[:, 0:NT]
        xbi = part[i, 1, :, points:].astype(F32)[:, 0:NT]
        xx = mm(jnp.concatenate([jnp.where(hit, xbr, 0.0), jnp.where(hit, xbi, 0.0)], 0).astype(BF16), pick_w)
        w1 = jnp.where(first, xx[0:8], -xx[8:16])
        w2 = jnp.where(first, xx[8:16], xx[0:8])
        w1 = jnp.concatenate([w1] * (ROWS // 8), 0)
        w2 = jnp.concatenate([w2] * (ROWS // 8), 0)
        d_sum[0:ROWS] += k_re * w1 + k_im * w2
        d_sum[ROWS:] += k_re * w2 - k_im * w1
        return carry

    lax.fori_loop(0, members, partner_step, 0)
    exchange = ex_sum[...]
    h_copies = [h_copy(i) for i in range(members)]
    started += [relay(i) for i in range(half)] + h_copies

    scale = 1.0 / n_k
    d_sums = mm_nt(hi_lo(d_sum[...]), pick_v)
    d_sums = d_sums[0:side] + d_sums[side:]
    d_sums = jnp.where((iota((side, NT), 0) // 4) % 4 == iota((side, NT), 1) % 4, d_sums, 0.0)
    mine = None
    d_copies = []
    for s in (3, 2, 1, 0):
        direct = jnp.concatenate(
            [jnp.sum(d_sums[r:r + NT], 0, keepdims=True) for r in (s * NT, ROWS + s * NT)], 0)
        both = (2.0 * scale) * exchange[:, s * NT:(s + 1) * NT] - scale * direct
        if s == 0:
            mine = both
        else:
            t_send[s] = both
            d_copies.append(go(remote(t_send.at[s], t_recv.at[s], d_ssem.at[s], d_rsem.at[s], (grp, mate(s)))))

    result = energies[...] * own_vec + mine
    for copy in h_copies:
        copy.wait_recv()
    back = h_recv[0]
    for i in range(1, members):
        back = back + h_recv[i]
    for copy in d_copies:
        copy.wait_recv()
    for s in range(1, TEAM):
        result = result + t_recv[s]
    out[0] = result - scale * back

    for copy in started:
        copy.wait_send()


def on_device(waves, vector, energies, basis, screening, coulomb, qmap):
    groups = lax.axis_size("grp")
    members = lax.axis_size("kin")
    half = members // 2
    n_s = groups * (members // TEAM) - 1
    points = waves.shape[3]
    n_g = basis.shape[2]
    quarter = n_g // TEAM
    any_space = pl.BlockSpec(memory_space=pl.ANY)
    dma = pltpu.SemaphoreType.DMA
    vmem = pltpu.VMEM
    stage = (2, 8, points + 128)
    return pl.pallas_call(
        functools.partial(kernel, groups, members, n_g),
        out_shape=jax.ShapeDtypeStruct(vector.shape, F32),
        in_specs=[any_space] * 7,
        out_specs=pl.BlockSpec(memory_space=vmem),
        scratch_shapes=[
            vmem(vector.shape, F32),
            vmem(energies.shape, F32),
            vmem(coulomb.shape, F32),
            pltpu.SMEM(qmap.shape, jnp.int32),
            vmem((2, points, quarter), BF16),
            vmem(screening.shape, F32),
            vmem(stage, BF16),
            vmem((TEAM,) + stage, BF16),
            vmem((members,) + stage, BF16),
            vmem((TEAM, 4, 2, 8, points), F32),
            vmem((members, n_g), F32),
            vmem((TEAM, members, quarter), F32),
            vmem((2 * ROWS, 2 * points), BF16),
            vmem((4 * ROWS, 2 * points), BF16),
            vmem((2 * ROWS, quarter), BF16),
            vmem((2, quarter), F32),
            vmem((n_s, 2, quarter), F32),
            vmem((members, 2, NT), F32),
            vmem((members, 2, NT), F32),
            vmem((TEAM, 2, NT), F32),
            vmem((TEAM, 2, NT), F32),
            vmem((2 * ROWS, 2 * ROWS), F32),
            vmem((2, ROWS), F32),
            dma((5,)), dma, dma,
            dma((TEAM,)), dma((TEAM,)),
            dma((half,)), dma((members,)), dma((half,)),
            dma((TEAM,)), dma((TEAM,)),
            dma((n_s,)), dma((n_s,)),
            dma((members,)), dma((members,)),
            dma((TEAM,)), dma((TEAM,)),
        ],
        compiler_params=pltpu.CompilerParams(
            collective_id=0, has_side_effects=True, vmem_limit_bytes=60 * 1024 * 1024
        ),
    )(waves, vector, energies, basis, screening, coulomb, qmap)


def solution(mesh):
    return jax.shard_map(
        on_device,
        mesh=mesh,
        in_specs=(
            P(("grp", "kin"), None, None, None),
            P(("grp", "kin"), None, None),
            P(("grp", "kin"), None),
            P(),
            P(),
            P(),
            P(("grp", "kin"), None),
        ),
        out_specs=P(("grp", "kin"), None, None),
        check_vma=False,
    )
```

```python
import functools

import jax
import jax.numpy as jnp
from jax import lax
from jax.experimental import pallas as pl
from jax.experimental.pallas import tpu as pltpu
from jax.sharding import PartitionSpec as P

NV = 4
NC = 4
NT = 16
TEAM = 2
ROWS = 2 * TEAM * NT
CHUNK = 256
MESH = pl.DeviceIdType.MESH
F32 = jnp.float32
BF16 = jnp.bfloat16


def iota(shape, dim):
    return lax.broadcasted_iota(jnp.int32, shape, dim)


def mm(left, right):
    return jnp.dot(left, right, preferred_element_type=F32)


def mm_nt(left, right):
    return lax.dot_general(left, right, (((1,), (1,)), ((), ())), preferred_element_type=F32)


def hi_lo(value):
    high = value.astype(BF16)
    low = (value - high.astype(F32)).astype(BF16)
    return jnp.concatenate([high, low], 0)


def one_hot(cond):
    return jnp.where(cond, 1.0, 0.0).astype(BF16)


def conj_mul(lre, lim, rre, rim):
    return lre * rre + lim * rim, lre * rim - lim * rre


def twice(rows):
    return jnp.concatenate([rows, rows], 0)


def kernel(
    groups, members, n_g,
    waves_h, vector_h, energies_h, basis_h, screening_h, coulomb_h, qmap_h, out,
    energies, coulomb, qmap, basis, screening, team, team_vec, part, part_vec,
    left, weights, weights_in, own_p, pair_p, own_d, s_own, s_in, s_pair, s_all, h_send, h_recv, t_send, t_recv,
    small_sem, basis_sem, screen_sem, t_ssem, t_rsem, tv_ssem, tv_rsem, p_ssem, p_rsem, pv_ssem, pv_rsem, r_ssem,
    w_ssem, w_rsem, s_ssem, s_rsem, g_ssem, g_rsem, h_ssem, h_rsem, d_ssem, d_rsem,
):
    offset = groups // 4
    half = members // 2
    teams = members // TEAM
    n_k = groups * members
    points = waves_h.shape[3]
    share = n_g // TEAM
    n_chunk = share // CHUNK
    grp = lax.axis_index("grp")
    kin = lax.axis_index("kin")
    rank = lax.rem(kin, TEAM)
    sib = kin + 1 - 2 * rank
    up = lax.rem(grp + offset, groups)
    down = lax.rem(grp + groups - offset, groups)

    def source(i):
        if i < half:
            return lax.rem(kin + members - 2 * i, members)
        return lax.rem(sib + members - 2 * (i - half), members)

    def group_at(dg):
        return (lax.rem(grp + dg, groups), kin)

    def kin_at(g, dk):
        return (g, lax.rem(kin + dk, members))

    greet = [kin_at(g, dk) for g in (up, down) for dk in range(1, members)]
    greet += [group_at(dg) for dg in range(1, groups)] + [kin_at(grp, dk) for dk in range(1, members)]
    barrier = pltpu.get_barrier_semaphore()
    for target in greet:
        pl.semaphore_signal(barrier, inc=1, device_id=target, device_id_type=MESH)

    my_cols = pl.ds(pl.multiple_of(rank * share, 128), share)
    pairs = [
        (waves_h, team.at[pl.ds(0, 1)]), (vector_h, team_vec.at[pl.ds(0, 1)]), (qmap_h, qmap),
        (energies_h, energies), (coulomb_h, coulomb),
    ]
    small = []
    for i, (src, dst) in enumerate(pairs):
        small.append(pltpu.make_async_copy(src, dst, small_sem.at[i]))
        small[-1].start()
    basis_in = []
    for n in range(n_chunk):
        src = pl.ds(pl.multiple_of(rank * share + n * CHUNK, 128), CHUNK)
        basis_in.append(pltpu.make_async_copy(
            basis_h.at[:, :, src], basis.at[:, :, pl.ds(n * CHUNK, CHUNK)], basis_sem.at[n]))
        basis_in[-1].start()
        if n == 0:
            screen_in = pltpu.make_async_copy(screening_h, screening, screen_sem)
            screen_in.start()
    pl.semaphore_wait(barrier, len(greet))

    started = []

    def send(src, dst, ssem, rsem, target):
        copy = pltpu.make_async_remote_copy(
            src_ref=src, dst_ref=dst, send_sem=ssem, recv_sem=rsem, device_id=target, device_id_type=MESH
        )
        copy.start()
        started.append(copy)
        return copy

    one = pl.ds(1, 1)
    part_in = [None] * members
    for i in range(half):
        part_in[i] = send(waves_h, part.at[pl.ds(i, 1)], p_ssem.at[i], p_rsem.at[i], kin_at(up, 2 * i))
    team_in = send(waves_h, team.at[one], t_ssem, t_rsem, (grp, sib))
    team_vec_in = send(vector_h, team_vec.at[one], tv_ssem, tv_rsem, (grp, sib))
    vec_in = []
    for i in range(members):
        if i < half:
            target = kin_at(up, 2 * i)
        else:
            target = (up, lax.rem(sib + 2 * (i - half), members))
        vec_in.append(send(vector_h, part_vec.at[pl.ds(i, 1)], pv_ssem.at[i], pv_rsem.at[i], target))

    for copy in small:
        copy.wait()
    low_half = iota((8, points), 0) < 4
    re_rows, im_rows = slice(0, ROWS), slice(ROWS, 2 * ROWS)

    def team_part(s):
        wre = team[s, 0].astype(F32)
        wim = team[s, 1].astype(F32)
        cre, cim = twice(wre[NV:]), twice(wim[NV:])
        res, ims = [], []
        for h in range(4):
            lre = jnp.where(low_half, wre[2 * h:2 * h + 1], wre[2 * h + 1:2 * h + 2])
            lim = jnp.where(low_half, wim[2 * h:2 * h + 1], wim[2 * h + 1:2 * h + 2])
            left[s, h, 0] = lre
            left[s, h, 1] = lim
            if h < 2:
                pre, pim = conj_mul(lre, lim, cre, cim)
                res.append(pre)
                ims.append(pim)
        pre = jnp.concatenate(res, 0)
        pim = jnp.concatenate(ims, 0)
        r0 = s * NT
        r1 = TEAM * NT + s * NT
        own_p[r0:r0 + NT, 0:points] = pre.astype(BF16)
        own_p[r0:r0 + NT, points:] = (-pim).astype(BF16)
        own_p[r1:r1 + NT, 0:points] = pim.astype(BF16)
        own_p[r1:r1 + NT, points:] = pre.astype(BF16)

    team_part(0)

    side = 2 * ROWS
    col = iota((NT, side), 1)
    tr = iota((NT, side), 0)
    pick_v = one_hot((col // 4) % 4 == tr // 4)
    pick_w = one_hot(col % 4 == tr // 4)
    same = (iota((side, side), 0) // NT) % 4 == (iota((side, side), 1) // NT) % 4
    first = iota((8, side), 1) < ROWS
    row8 = iota((8, NT), 0)
    lane8 = iota((8, NT), 1)
    hit_d = row8 % 4 == lane8 % 4

    screen_in.wait()
    base = down * members
    for b in range(members):
        weights[b:b + 1, :] = screening[pl.ds(qmap[0, base + b], 1), :]
    sib_cols = pl.ds(pl.multiple_of((1 - rank) * share, 128), share)
    weight_in = send(weights.at[:, sib_cols], weights_in.at[1], w_ssem, w_rsem, (grp, sib))
    weights_in[0] = weights[:, my_cols]

    team_in.wait_recv()
    team_vec_in.wait_recv()
    team_part(1)
    xs = []
    for s in range(TEAM):
        x = team_vec[s].astype(BF16).astype(F32)
        xs.append((x[0:1], x[1:2]))
    xr = jnp.concatenate([x[0] for x in xs], 1)
    xi = jnp.concatenate([x[1] for x in xs], 1)
    x_rows = jnp.concatenate(
        [jnp.concatenate([xr, -xi], 1), jnp.concatenate([xi, xr], 1), jnp.zeros((6, 2 * TEAM * NT), F32)], 0
    ).astype(BF16)

    def basis_cols(n):
        return basis[:, :, n * CHUNK:(n + 1) * CHUNK].reshape(2 * points, CHUNK)

    for n in range(n_chunk):
        basis_in[n].wait()
        cols = slice(n * CHUNK, (n + 1) * CHUNK)
        dens = mm(own_p[...], basis_cols(n)).astype(BF16)
        own_d[:, cols] = dens
        s_own[:, cols] = mm(x_rows, dens)[0:2]
    s_copies = []
    for i in range(teams - 1):
        s_copies.append(send(s_own, s_in.at[i], s_ssem.at[i], s_rsem.at[i], kin_at(grp, TEAM * (i + 1))))

    a_re, a_im = [], []
    for s in range(TEAM):
        for c in range(0, NC, 2):
            hit = lane8 % 4 == c + row8 // 4
            a_re.append(jnp.where(hit, xs[s][0], 0.0))
            a_im.append(jnp.where(hit, xs[s][1], 0.0))
    spread = mm(jnp.concatenate(a_re + a_im, 0).astype(BF16), pick_v)
    first_32 = iota((TEAM * NT, side), 1) < ROWS
    a_re, a_im = spread[0:TEAM * NT], spread[TEAM * NT:]
    u1 = twice(jnp.where(first_32, a_re, a_im))
    u2 = twice(jnp.where(first_32, -a_im, a_re))

    def products(i, batch, j):
        wre = part[i, 0].astype(F32)
        wim = part[i, 1].astype(F32)
        for kind in range(2):
            bands = slice(NV, NV + NC) if kind == 0 else slice(0, NV)
            rre, rim = twice(wre[bands]), twice(wim[bands])
            for s in range(TEAM):
                res, ims = [], []
                for h in range(2):
                    t = h + 2 - 2 * kind
                    pre, pim = conj_mul(left[s, t, 0], left[s, t, 1], rre, rim)
                    res.append(pre)
                    ims.append(pim)
                pre = jnp.concatenate(res, 0)
                pim = jnp.concatenate(ims, 0)
                r0 = kind * side + j * TEAM * NT + s * NT
                r1 = r0 + ROWS
                pair_p[batch, r0:r0 + NT, 0:points] = pre.astype(BF16)
                pair_p[batch, r0:r0 + NT, points:] = (-pim).astype(BF16)
                pair_p[batch, r1:r1 + NT, 0:points] = pim.astype(BF16)
                pair_p[batch, r1:r1 + NT, points:] = pre.astype(BF16)

    def kernel_of(batch):
        total = None
        for n in range(n_chunk):
            cols = slice(n * CHUNK, (n + 1) * CHUNK)
            dens = mm(pair_p[batch % 2], basis_cols(n)).astype(BF16)
            rows = []
            for j in range(2):
                b = source(2 * batch + j)
                rows += [jnp.broadcast_to(weights_in[s, pl.ds(b, 1), cols], (NT, CHUNK)) for s in range(TEAM)]
            weight = jnp.concatenate(rows * 2, 0)
            cond = (dens[0:side].astype(F32) * weight).astype(BF16)
            term = mm_nt(cond, dens[side:])
            total = term if total is None else total + term
        return jnp.where(same, total, 0.0)

    kerns = []
    for batch in range(members // 2):
        for i in (2 * batch, 2 * batch + 1):
            if i >= half:
                k = pl.ds(i, 1)
                part_in[i] = pltpu.make_async_remote_copy(
                    src_ref=part.at[k], dst_ref=part.at[k], send_sem=r_ssem.at[i - half], recv_sem=p_rsem.at[i],
                    device_id=(grp, sib), device_id_type=MESH)
            part_in[i].wait_recv()
            if i < half:
                send(part.at[i], part.at[half + i], r_ssem.at[i], p_rsem.at[half + i], (grp, sib))
        if batch == 0:
            weight_in.wait_recv()
        for j in range(2):
            products(2 * batch + j, batch % 2, j)
        kerns.append(kernel_of(batch))
        if batch == 0:
            total = s_own[...]
            for i, copy in enumerate(s_copies):
                copy.wait_recv()
                total = total + s_in[i]
            s_pair[...] = total
            g_copies = []
            for i in range(groups - 1):
                g_copies.append(send(s_pair, s_all.at[i], g_ssem.at[i], g_rsem.at[i], group_at(i + 1)))

    h_rows = []
    for kern in kerns:
        k_re, k_im = kern[re_rows], kern[im_rows]
        for value in (k_re * u1 + k_im * u2, k_im * u1 - k_re * u2):
            for j in range(2):
                r0 = j * TEAM * NT
                h_rows.append(value[r0:r0 + 8] + value[r0 + 8:r0 + 16] + value[r0 + 16:r0 + 24] + value[r0 + 24:r0 + 32])
    n_h = 8 * len(h_rows)
    h_sums = mm_nt(hi_lo(jnp.concatenate(h_rows, 0)), pick_w)
    h_sums = h_sums[0:n_h] + h_sums[n_h:]

    def h_row(batch, comp, j):
        r0 = 8 * (4 * batch + 2 * comp + j)
        return jnp.sum(jnp.where(hit_d, h_sums[r0:r0 + 8], 0.0), 0, keepdims=True)

    h_copies = []
    for i in range(members):
        h_send[i] = jnp.concatenate([h_row(i // 2, 0, i % 2), h_row(i // 2, 1, i % 2)], 0)
    for i in range(members):
        h_copies.append(send(h_send.at[i], h_recv.at[i], h_ssem.at[i], h_rsem.at[i], (down, source(i))))

    for copy in vec_in:
        copy.wait_recv()
    d_re = jnp.zeros((ROWS, side), F32)
    d_im = jnp.zeros((ROWS, side), F32)
    for batch, kern in enumerate(kerns):
        k_re, k_im = kern[re_rows], kern[im_rows]
        x_parts = []
        for j in range(2):
            xb = part_vec[2 * batch + j].astype(BF16).astype(F32)
            x_parts += [jnp.where(hit_d, xb[0:1], 0.0), jnp.where(hit_d, xb[1:2], 0.0)]
        xx = mm(jnp.concatenate(x_parts, 0).astype(BF16), pick_w)
        w1, w2 = [], []
        for j in range(2):
            x_re, x_im = xx[16 * j:16 * j + 8], xx[16 * j + 8:16 * j + 16]
            w1 += [jnp.where(first, x_re, -x_im)] * (2 * TEAM)
            w2 += [jnp.where(first, x_im, x_re)] * (2 * TEAM)
        w1 = jnp.concatenate(w1, 0)
        w2 = jnp.concatenate(w2, 0)
        d_re = d_re + (k_re * w1 + k_im * w2)
        d_im = d_im + (k_re * w2 - k_im * w1)
    n_d = TEAM * NT
    d_rows = jnp.concatenate([d_re[0:n_d] + d_re[n_d:], d_im[0:n_d] + d_im[n_d:]], 0)
    d_sums = mm_nt(hi_lo(d_rows), pick_v)
    d_sums = d_sums[0:2 * n_d] + d_sums[2 * n_d:]
    d_sums = jnp.where((iota((2 * n_d, NT), 0) // 4) % 4 == iota((2 * n_d, NT), 1) % 4, d_sums, 0.0)

    total = s_pair[...]
    for i, copy in enumerate(g_copies):
        copy.wait_recv()
        total = total + s_all[i]
    pot = coulomb[my_cols].reshape(1, share) * total
    ex = mm_nt(jnp.concatenate([hi_lo(pot), jnp.zeros((4, share), BF16)], 0), own_d[...])
    ex = ex[0:2] + ex[2:4]
    exchange = jnp.concatenate([ex[0:1, 0:n_d] + ex[1:2, n_d:], ex[1:2, 0:n_d] - ex[0:1, n_d:]], 0)

    scale = 1.0 / n_k
    sums = []
    for s in range(TEAM):
        direct = jnp.concatenate(
            [jnp.sum(d_sums[r:r + NT], 0, keepdims=True) for r in (s * NT, n_d + s * NT)], 0)
        sums.append((2.0 * scale) * exchange[:, s * NT:(s + 1) * NT] - scale * direct)
    t_send[...] = sums[1]
    d_copy = send(t_send, t_recv, d_ssem, d_rsem, (grp, sib))
    result = energies[...] * team_vec[0] + sums[0]
    for copy in h_copies:
        copy.wait_recv()
    back = h_recv[0]
    for i in range(1, members):
        back = back + h_recv[i]
    d_copy.wait_recv()
    out[0] = result + t_recv[...] - scale * back

    for copy in started:
        copy.wait_send()


def on_device(waves, vector, energies, basis, screening, coulomb, qmap):
    groups = lax.axis_size("grp")
    members = lax.axis_size("kin")
    half = members // 2
    points = waves.shape[3]
    n_g = basis.shape[2]
    share = n_g // TEAM
    n_s = max(members // TEAM - 1, 1)
    any_space = pl.BlockSpec(memory_space=pl.ANY)
    dma = pltpu.SemaphoreType.DMA
    vmem = pltpu.VMEM
    n_own = 2 * TEAM * NT
    return pl.pallas_call(
        functools.partial(kernel, groups, members, n_g),
        out_shape=jax.ShapeDtypeStruct(vector.shape, F32),
        in_specs=[any_space] * 7,
        out_specs=pl.BlockSpec(memory_space=vmem),
        scratch_shapes=[
            vmem(energies.shape, F32),
            vmem(coulomb.shape, F32),
            pltpu.SMEM(qmap.shape, jnp.int32),
            vmem((2, points, share), BF16),
            vmem(screening.shape, F32),
            vmem((TEAM,) + waves.shape[1:], BF16),
            vmem((TEAM, 2, NT), F32),
            vmem((members,) + waves.shape[1:], BF16),
            vmem((members, 2, NT), F32),
            vmem((TEAM, 4, 2, 8, points), F32),
            vmem((members, n_g), F32),
            vmem((TEAM, members, share), F32),
            vmem((n_own, 2 * points), BF16),
            vmem((2, 4 * ROWS, 2 * points), BF16),
            vmem((n_own, share), BF16),
            vmem((2, share), F32),
            vmem((n_s, 2, share), F32),
            vmem((2, share), F32),
            vmem((groups - 1, 2, share), F32),
            vmem((members, 2, NT), F32),
            vmem((members, 2, NT), F32),
            vmem((2, NT), F32),
            vmem((2, NT), F32),
            dma((5,)), dma((share // CHUNK,)), dma,
            dma, dma, dma, dma,
            dma((half,)), dma((members,)),
            dma((members,)), dma((members,)),
            dma((half,)),
            dma, dma,
            dma((n_s,)), dma((n_s,)),
            dma((groups - 1,)), dma((groups - 1,)),
            dma((members,)), dma((members,)),
            dma, dma,
        ],
        compiler_params=pltpu.CompilerParams(
            collective_id=0, has_side_effects=True, vmem_limit_bytes=60 * 1024 * 1024
        ),
    )(waves, vector, energies, basis, screening, coulomb, qmap)


def solution(mesh):
    return jax.shard_map(
        on_device,
        mesh=mesh,
        in_specs=(
            P(("grp", "kin"), None, None, None),
            P(("grp", "kin"), None, None),
            P(("grp", "kin"), None),
            P(),
            P(),
            P(),
            P(("grp", "kin"), None),
        ),
        out_specs=P(("grp", "kin"), None, None),
        check_vma=False,
    )
```

```python
import functools

import jax
import jax.numpy as jnp
from jax import lax
from jax.experimental import pallas as pl
from jax.experimental.pallas import tpu as pltpu
from jax.sharding import PartitionSpec as P

NV = 4
NC = 4
NT = 16
TEAM = 2
ROWS = 2 * TEAM * NT
CHUNK = 256
MESH = pl.DeviceIdType.MESH
F32 = jnp.float32
BF16 = jnp.bfloat16


def iota(shape, dim):
    return lax.broadcasted_iota(jnp.int32, shape, dim)


def mm(left, right):
    return jnp.dot(left, right, preferred_element_type=F32)


def mm_nt(left, right):
    return lax.dot_general(left, right, (((1,), (1,)), ((), ())), preferred_element_type=F32)


def hi_lo(value):
    high = value.astype(BF16)
    low = (value - high.astype(F32)).astype(BF16)
    return jnp.concatenate([high, low], 0)


def one_hot(cond):
    return jnp.where(cond, 1.0, 0.0).astype(BF16)


def conj_mul(lre, lim, rre, rim):
    return lre * rre + lim * rim, lre * rim - lim * rre


def twice(rows):
    return jnp.concatenate([rows, rows], 0)


def kernel(
    groups, members, n_g,
    waves_h, vector_h, energies_h, basis_h, screening_h, coulomb_h, qmap_h, out,
    energies, coulomb, qmap, basis, screening, team, team_vec, part, part_vec,
    left, weights, weights_in, own_p, pair_a, pair_b, own_d, s_own, s_in, s_pair, s_all, h_send, h_recv, t_send, t_recv,
    small_sem, basis_sem, screen_sem, t_ssem, t_rsem, tv_ssem, tv_rsem, p_ssem, p_rsem, pv_ssem, pv_rsem,
    w_ssem, w_rsem, s_ssem, s_rsem, g_ssem, g_rsem, h_ssem, h_rsem, d_ssem, d_rsem,
):
    offset = groups // 4
    half = members // 2
    teams = members // TEAM
    n_k = groups * members
    points = waves_h.shape[3]
    share = n_g // TEAM
    n_chunk = share // CHUNK
    grp = lax.axis_index("grp")
    kin = lax.axis_index("kin")
    rank = lax.rem(kin, TEAM)
    sib = kin + 1 - 2 * rank
    up = lax.rem(grp + offset, groups)
    down = lax.rem(grp + groups - offset, groups)

    def source(i):
        if i < half:
            return lax.rem(kin + members - 2 * i, members)
        return lax.rem(sib + members - 2 * (i - half), members)

    def group_at(dg):
        return (lax.rem(grp + dg, groups), kin)

    def kin_at(g, dk):
        return (g, lax.rem(kin + dk, members))

    greet = [kin_at(g, dk) for g in (up, down) for dk in range(1, members)]
    greet += [group_at(dg) for dg in range(1, groups)] + [kin_at(grp, dk) for dk in range(1, members)]
    barrier = pltpu.get_barrier_semaphore()
    for target in greet:
        pl.semaphore_signal(barrier, inc=1, device_id=target, device_id_type=MESH)

    my_cols = pl.ds(pl.multiple_of(rank * share, 128), share)
    pairs = [
        (waves_h, team.at[pl.ds(0, 1)]), (vector_h, team_vec.at[pl.ds(0, 1)]), (qmap_h, qmap),
        (energies_h, energies), (coulomb_h, coulomb),
    ]
    small = []
    for i, (src, dst) in enumerate(pairs):
        small.append(pltpu.make_async_copy(src, dst, small_sem.at[i]))
        small[-1].start()
    basis_in = []
    for n in range(n_chunk):
        src = pl.ds(pl.multiple_of(rank * share + n * CHUNK, 128), CHUNK)
        basis_in.append(pltpu.make_async_copy(
            basis_h.at[:, :, src], basis.at[:, :, pl.ds(n * CHUNK, CHUNK)], basis_sem.at[n]))
        basis_in[-1].start()
        if n == 0:
            screen_in = pltpu.make_async_copy(screening_h, screening, screen_sem)
            screen_in.start()
    pl.semaphore_wait(barrier, len(greet))

    started = []

    def send(src, dst, ssem, rsem, target):
        copy = pltpu.make_async_remote_copy(
            src_ref=src, dst_ref=dst, send_sem=ssem, recv_sem=rsem, device_id=target, device_id_type=MESH
        )
        copy.start()
        started.append(copy)
        return copy

    one = pl.ds(1, 1)
    targets = [kin_at(up, 2 * i) for i in range(half)]
    targets += [(up, lax.rem(sib + 2 * i, members)) for i in range(half)]
    part_in = []
    team_in = send(waves_h, team.at[one], t_ssem, t_rsem, (grp, sib))
    team_vec_in = send(vector_h, team_vec.at[one], tv_ssem, tv_rsem, (grp, sib))
    for i, target in enumerate(targets):
        part_in.append(send(waves_h, part.at[pl.ds(i, 1)], p_ssem.at[i], p_rsem.at[i], target))
    vec_in = []
    for i, target in enumerate(targets):
        vec_in.append(send(vector_h, part_vec.at[pl.ds(i, 1)], pv_ssem.at[i], pv_rsem.at[i], target))

    for copy in small:
        copy.wait()
    low_half = iota((8, points), 0) < 4
    re_rows, im_rows = slice(0, ROWS), slice(ROWS, 2 * ROWS)

    def team_part(s):
        wre = team[s, 0].astype(F32)
        wim = team[s, 1].astype(F32)
        cre, cim = twice(wre[NV:]), twice(wim[NV:])
        res, ims = [], []
        for h in range(4):
            lre = jnp.where(low_half, wre[2 * h:2 * h + 1], wre[2 * h + 1:2 * h + 2])
            lim = jnp.where(low_half, wim[2 * h:2 * h + 1], wim[2 * h + 1:2 * h + 2])
            left[s, h, 0] = lre
            left[s, h, 1] = lim
            if h < 2:
                pre, pim = conj_mul(lre, lim, cre, cim)
                res.append(pre)
                ims.append(pim)
        pre = jnp.concatenate(res, 0)
        pim = jnp.concatenate(ims, 0)
        r0 = s * NT
        r1 = TEAM * NT + s * NT
        own_p[r0:r0 + NT, 0:points] = pre.astype(BF16)
        own_p[r0:r0 + NT, points:] = (-pim).astype(BF16)
        own_p[r1:r1 + NT, 0:points] = pim.astype(BF16)
        own_p[r1:r1 + NT, points:] = pre.astype(BF16)

    team_part(0)

    side = 2 * ROWS
    col = iota((NT, side), 1)
    tr = iota((NT, side), 0)
    pick_v = one_hot((col // 4) % 4 == tr // 4)
    pick_w = one_hot(col % 4 == tr // 4)
    same = (iota((side, side), 0) // NT) % 4 == (iota((side, side), 1) // NT) % 4
    first = iota((8, side), 1) < ROWS
    row8 = iota((8, NT), 0)
    lane8 = iota((8, NT), 1)
    hit_d = row8 % 4 == lane8 % 4

    screen_in.wait()
    base = down * members
    for b in range(members):
        weights[b:b + 1, :] = screening[pl.ds(qmap[0, base + b], 1), :]
    sib_cols = pl.ds(pl.multiple_of((1 - rank) * share, 128), share)
    weight_in = send(weights.at[:, sib_cols], weights_in.at[1], w_ssem, w_rsem, (grp, sib))
    weights_in[0] = weights[:, my_cols]

    team_in.wait_recv()
    team_vec_in.wait_recv()
    team_part(1)
    xs = []
    for s in range(TEAM):
        x = team_vec[s].astype(BF16).astype(F32)
        xs.append((x[0:1], x[1:2]))
    xr = jnp.concatenate([x[0] for x in xs], 1)
    xi = jnp.concatenate([x[1] for x in xs], 1)
    x_rows = jnp.concatenate(
        [jnp.concatenate([xr, -xi], 1), jnp.concatenate([xi, xr], 1), jnp.zeros((6, 2 * TEAM * NT), F32)], 0
    ).astype(BF16)

    def basis_cols(n):
        return basis[:, :, n * CHUNK:(n + 1) * CHUNK].reshape(2 * points, CHUNK)

    for n in range(n_chunk):
        basis_in[n].wait()
        cols = slice(n * CHUNK, (n + 1) * CHUNK)
        dens = mm(own_p[...], basis_cols(n)).astype(BF16)
        own_d[:, cols] = dens
        s_own[:, cols] = mm(x_rows, dens)[0:2]
    s_copies = []
    for i in range(teams - 1):
        s_copies.append(send(s_own, s_in.at[i], s_ssem.at[i], s_rsem.at[i], kin_at(grp, TEAM * (i + 1))))

    a_re, a_im = [], []
    for s in range(TEAM):
        for c in range(0, NC, 2):
            hit = lane8 % 4 == c + row8 // 4
            a_re.append(jnp.where(hit, xs[s][0], 0.0))
            a_im.append(jnp.where(hit, xs[s][1], 0.0))
    spread = mm(jnp.concatenate(a_re + a_im, 0).astype(BF16), pick_v)
    first_32 = iota((TEAM * NT, side), 1) < ROWS
    a_re, a_im = spread[0:TEAM * NT], spread[TEAM * NT:]
    u1 = twice(jnp.where(first_32, a_re, a_im))
    u2 = twice(jnp.where(first_32, -a_im, a_re))

    def products(i, pair_p, j):
        wre = part[i, 0].astype(F32)
        wim = part[i, 1].astype(F32)
        for kind in range(2):
            bands = slice(NV, NV + NC) if kind == 0 else slice(0, NV)
            rre, rim = twice(wre[bands]), twice(wim[bands])
            for s in range(TEAM):
                res, ims = [], []
                for h in range(2):
                    t = h + 2 - 2 * kind
                    pre, pim = conj_mul(left[s, t, 0], left[s, t, 1], rre, rim)
                    res.append(pre)
                    ims.append(pim)
                pre = jnp.concatenate(res, 0)
                pim = jnp.concatenate(ims, 0)
                r0 = kind * side + j * TEAM * NT + s * NT
                r1 = r0 + ROWS
                pair_p[r0:r0 + NT, 0:points] = pre.astype(BF16)
                pair_p[r0:r0 + NT, points:] = (-pim).astype(BF16)
                pair_p[r1:r1 + NT, 0:points] = pim.astype(BF16)
                pair_p[r1:r1 + NT, points:] = pre.astype(BF16)

    def kernel_of(batch, pair_p):
        total = None
        for n in range(n_chunk):
            cols = slice(n * CHUNK, (n + 1) * CHUNK)
            dens = mm(pair_p[...], basis_cols(n)).astype(BF16)
            rows = []
            for j in range(2):
                b = source(2 * batch + j)
                rows += [jnp.broadcast_to(weights_in[s, pl.ds(b, 1), cols], (NT, CHUNK)) for s in range(TEAM)]
            weight = jnp.concatenate(rows * 2, 0)
            cond = (dens[0:side].astype(F32) * weight).astype(BF16)
            term = mm_nt(cond, dens[side:])
            total = term if total is None else total + term
        return jnp.where(same, total, 0.0)

    weight_in.wait_recv()
    for copy in part_in + vec_in:
        copy.wait_recv()
    pairs_of = (pair_a, pair_b)

    def both_products(batch):
        for j in range(2):
            products(2 * batch + j, pairs_of[batch % 2], j)

    both_products(0)
    total = s_own[...]
    for i, copy in enumerate(s_copies):
        copy.wait_recv()
        total = total + s_in[i]
    s_pair[...] = total
    g_copies = []
    for i in range(groups - 1):
        g_copies.append(send(s_pair, s_all.at[i], g_ssem.at[i], g_rsem.at[i], group_at(i + 1)))

    kerns = []
    for batch in range(half):
        if batch + 1 < half:
            both_products(batch + 1)
        kerns.append(kernel_of(batch, pairs_of[batch % 2]))

    h_rows = []
    for kern in kerns:
        k_re, k_im = kern[re_rows], kern[im_rows]
        for value in (k_re * u1 + k_im * u2, k_im * u1 - k_re * u2):
            for j in range(2):
                r0 = j * TEAM * NT
                h_rows.append(value[r0:r0 + 8] + value[r0 + 8:r0 + 16] + value[r0 + 16:r0 + 24] + value[r0 + 24:r0 + 32])
    n_h = 8 * len(h_rows)
    h_sums = mm_nt(hi_lo(jnp.concatenate(h_rows, 0)), pick_w)
    h_sums = h_sums[0:n_h] + h_sums[n_h:]

    def h_row(batch, comp, j):
        r0 = 8 * (4 * batch + 2 * comp + j)
        return jnp.sum(jnp.where(hit_d, h_sums[r0:r0 + 8], 0.0), 0, keepdims=True)

    h_copies = []
    for i in range(members):
        h_send[i] = jnp.concatenate([h_row(i // 2, 0, i % 2), h_row(i // 2, 1, i % 2)], 0)
    d_re = jnp.zeros((ROWS, side), F32)
    d_im = jnp.zeros((ROWS, side), F32)
    for batch, kern in enumerate(kerns):
        k_re, k_im = kern[re_rows], kern[im_rows]
        x_parts = []
        for j in range(2):
            xb = part_vec[2 * batch + j].astype(BF16).astype(F32)
            x_parts += [jnp.where(hit_d, xb[0:1], 0.0), jnp.where(hit_d, xb[1:2], 0.0)]
        xx = mm(jnp.concatenate(x_parts, 0).astype(BF16), pick_w)
        w1, w2 = [], []
        for j in range(2):
            x_re, x_im = xx[16 * j:16 * j + 8], xx[16 * j + 8:16 * j + 16]
            w1 += [jnp.where(first, x_re, -x_im)] * (2 * TEAM)
            w2 += [jnp.where(first, x_im, x_re)] * (2 * TEAM)
        w1 = jnp.concatenate(w1, 0)
        w2 = jnp.concatenate(w2, 0)
        d_re = d_re + (k_re * w1 + k_im * w2)
        d_im = d_im + (k_re * w2 - k_im * w1)
    n_d = TEAM * NT
    d_rows = jnp.concatenate([d_re[0:n_d] + d_re[n_d:], d_im[0:n_d] + d_im[n_d:]], 0)
    d_sums = mm_nt(hi_lo(d_rows), pick_v)
    d_sums = d_sums[0:2 * n_d] + d_sums[2 * n_d:]
    d_sums = jnp.where((iota((2 * n_d, NT), 0) // 4) % 4 == iota((2 * n_d, NT), 1) % 4, d_sums, 0.0)

    for i in range(members):
        h_copies.append(send(h_send.at[i], h_recv.at[i], h_ssem.at[i], h_rsem.at[i], (down, source(i))))

    total = s_pair[...]
    for i, copy in enumerate(g_copies):
        copy.wait_recv()
        total = total + s_all[i]
    pot = coulomb[my_cols].reshape(1, share) * total
    ex = mm_nt(jnp.concatenate([hi_lo(pot), jnp.zeros((4, share), BF16)], 0), own_d[...])
    ex = ex[0:2] + ex[2:4]
    exchange = jnp.concatenate([ex[0:1, 0:n_d] + ex[1:2, n_d:], ex[1:2, 0:n_d] - ex[0:1, n_d:]], 0)

    scale = 1.0 / n_k
    sums = []
    for s in range(TEAM):
        direct = jnp.concatenate(
            [jnp.sum(d_sums[r:r + NT], 0, keepdims=True) for r in (s * NT, n_d + s * NT)], 0)
        sums.append((2.0 * scale) * exchange[:, s * NT:(s + 1) * NT] - scale * direct)
    t_send[...] = sums[1]
    d_copy = send(t_send, t_recv, d_ssem, d_rsem, (grp, sib))
    result = energies[...] * team_vec[0] + sums[0]
    for copy in started:
        copy.wait_send()
    for copy in h_copies:
        copy.wait_recv()
    back = h_recv[0]
    for i in range(1, members):
        back = back + h_recv[i]
    d_copy.wait_recv()
    out[0] = result + t_recv[...] - scale * back


def on_device(waves, vector, energies, basis, screening, coulomb, qmap):
    groups = lax.axis_size("grp")
    members = lax.axis_size("kin")
    half = members // 2
    points = waves.shape[3]
    n_g = basis.shape[2]
    share = n_g // TEAM
    n_s = max(members // TEAM - 1, 1)
    any_space = pl.BlockSpec(memory_space=pl.ANY)
    dma = pltpu.SemaphoreType.DMA
    vmem = pltpu.VMEM
    n_own = 2 * TEAM * NT
    return pl.pallas_call(
        functools.partial(kernel, groups, members, n_g),
        out_shape=jax.ShapeDtypeStruct(vector.shape, F32),
        in_specs=[any_space] * 7,
        out_specs=pl.BlockSpec(memory_space=vmem),
        scratch_shapes=[
            vmem(energies.shape, F32),
            vmem(coulomb.shape, F32),
            pltpu.SMEM(qmap.shape, jnp.int32),
            vmem((2, points, share), BF16),
            vmem(screening.shape, F32),
            vmem((TEAM,) + waves.shape[1:], BF16),
            vmem((TEAM, 2, NT), F32),
            vmem((members,) + waves.shape[1:], BF16),
            vmem((members, 2, NT), F32),
            vmem((TEAM, 4, 2, 8, points), F32),
            vmem((members, n_g), F32),
            vmem((TEAM, members, share), F32),
            vmem((n_own, 2 * points), BF16),
            vmem((4 * ROWS, 2 * points), BF16),
            vmem((4 * ROWS, 2 * points), BF16),
            vmem((n_own, share), BF16),
            vmem((2, share), F32),
            vmem((n_s, 2, share), F32),
            vmem((2, share), F32),
            vmem((groups - 1, 2, share), F32),
            vmem((members, 2, NT), F32),
            vmem((members, 2, NT), F32),
            vmem((2, NT), F32),
            vmem((2, NT), F32),
            dma((5,)), dma((share // CHUNK,)), dma,
            dma, dma, dma, dma,
            dma((members,)), dma((members,)),
            dma((members,)), dma((members,)),
            dma, dma,
            dma((n_s,)), dma((n_s,)),
            dma((groups - 1,)), dma((groups - 1,)),
            dma((members,)), dma((members,)),
            dma, dma,
        ],
        compiler_params=pltpu.CompilerParams(
            collective_id=0, has_side_effects=True, vmem_limit_bytes=60 * 1024 * 1024
        ),
    )(waves, vector, energies, basis, screening, coulomb, qmap)


def solution(mesh):
    return jax.shard_map(
        on_device,
        mesh=mesh,
        in_specs=(
            P(("grp", "kin"), None, None, None),
            P(("grp", "kin"), None, None),
            P(("grp", "kin"), None),
            P(),
            P(),
            P(),
            P(("grp", "kin"), None),
        ),
        out_specs=P(("grp", "kin"), None, None),
        check_vma=False,
    )
```

```python
import functools

import jax
import jax.numpy as jnp
from jax import lax
from jax.experimental import pallas as pl
from jax.experimental.pallas import tpu as pltpu
from jax.sharding import PartitionSpec as P

NV = 4
NC = 4
NT = 16
TEAM = 2
ROWS = 2 * TEAM * NT
CHUNK = 256
MESH = pl.DeviceIdType.MESH
F32 = jnp.float32
BF16 = jnp.bfloat16


def iota(shape, dim):
    return lax.broadcasted_iota(jnp.int32, shape, dim)


def mm(left, right):
    return jnp.dot(left, right, preferred_element_type=F32)


def mm_nt(left, right):
    return lax.dot_general(left, right, (((1,), (1,)), ((), ())), preferred_element_type=F32)


def hi_lo(value):
    high = value.astype(BF16)
    low = (value - high.astype(F32)).astype(BF16)
    return jnp.concatenate([high, low], 0)


def one_hot(cond):
    return jnp.where(cond, 1.0, 0.0).astype(BF16)


def conj_mul(lre, lim, rre, rim):
    return lre * rre + lim * rim, lre * rim - lim * rre


def twice(rows):
    return jnp.concatenate([rows, rows], 0)


def kernel(
    groups, members, n_g,
    waves_h, vector_h, energies_h, basis_h, screening_h, coulomb_h, qmap_h, out,
    energies, coulomb, qmap, basis, screening, team, team_vec, part, part_vec,
    left, weights, weights_in, own_p, pair_a, pair_b, own_d, s_own, s_in, s_plane, s_all, h_send, h_recv, t_send, t_recv,
    small_sem, basis_sem, screen_sem, t_ssem, t_rsem, tv_ssem, tv_rsem, p_ssem, p_rsem, pv_ssem, pv_rsem,
    w_ssem, w_rsem, s_ssem, s_rsem, g_ssem, g_rsem, h_ssem, h_rsem, d_ssem, d_rsem,
):
    offset = groups // 4
    half = members // 2
    teams = members // TEAM
    n_k = groups * members
    points = waves_h.shape[3]
    share = n_g // TEAM
    n_chunk = share // CHUNK
    grp = lax.axis_index("grp")
    kin = lax.axis_index("kin")
    rank = lax.rem(kin, TEAM)
    sib = kin + 1 - 2 * rank
    up = lax.rem(grp + offset, groups)
    down = lax.rem(grp + groups - offset, groups)

    def source(i):
        if i < half:
            return lax.rem(kin + members - 2 * i, members)
        return lax.rem(sib + members - 2 * (i - half), members)

    def group_at(dg):
        return (lax.rem(grp + dg, groups), kin)

    def spot_at(ds, dk):
        level = lax.div(grp, offset)
        return kin_at(level * offset + lax.rem(grp - level * offset + ds, offset), dk)

    def kin_at(g, dk):
        return (g, lax.rem(kin + dk, members))

    plane = [(ds, dt) for ds in range(offset) for dt in range(teams) if (ds, dt) != (0, 0)]
    plane_at = [spot_at(ds, TEAM * dt) for ds, dt in plane]
    greet = [kin_at(g, dk) for g in (up, down) for dk in range(members)] + [group_at(2 * offset), (grp, sib)] + plane_at
    barrier = pltpu.get_barrier_semaphore()
    for target in greet:
        pl.semaphore_signal(barrier, inc=1, device_id=target, device_id_type=MESH)

    my_cols = pl.ds(pl.multiple_of(rank * share, 128), share)
    pairs = [
        (waves_h, team.at[pl.ds(0, 1)]), (vector_h, team_vec.at[pl.ds(0, 1)]), (qmap_h, qmap),
        (energies_h, energies), (coulomb_h, coulomb),
    ]
    small = []
    for i, (src, dst) in enumerate(pairs):
        small.append(pltpu.make_async_copy(src, dst, small_sem.at[i]))
        small[-1].start()
    basis_in = []
    for n in range(n_chunk):
        src = pl.ds(pl.multiple_of(rank * share + n * CHUNK, 128), CHUNK)
        basis_in.append(pltpu.make_async_copy(
            basis_h.at[:, :, src], basis.at[:, :, pl.ds(n * CHUNK, CHUNK)], basis_sem.at[n]))
        basis_in[-1].start()
        if n == 0:
            screen_in = pltpu.make_async_copy(screening_h, screening, screen_sem)
            screen_in.start()
    pl.semaphore_wait(barrier, len(greet))

    started = []

    def send(src, dst, ssem, rsem, target):
        copy = pltpu.make_async_remote_copy(
            src_ref=src, dst_ref=dst, send_sem=ssem, recv_sem=rsem, device_id=target, device_id_type=MESH
        )
        copy.start()
        started.append(copy)
        return copy

    one = pl.ds(1, 1)
    targets = [kin_at(up, 2 * i) for i in range(half)]
    targets += [(up, lax.rem(sib + 2 * i, members)) for i in range(half)]
    part_in = [send(waves_h, part.at[pl.ds(0, 1)], p_ssem.at[0], p_rsem.at[0], kin_at(up, 0))]
    team_in = send(waves_h, team.at[one], t_ssem, t_rsem, (grp, sib))
    team_vec_in = send(vector_h, team_vec.at[one], tv_ssem, tv_rsem, (grp, sib))
    vec_in = []
    for i, target in enumerate(targets):
        vec_in.append(send(vector_h, part_vec.at[pl.ds(i, 1)], pv_ssem.at[i], pv_rsem.at[i], target))

    for copy in small:
        copy.wait()
    low_half = iota((8, points), 0) < 4
    re_rows, im_rows = slice(0, ROWS), slice(ROWS, 2 * ROWS)

    def team_part(s):
        wre = team[s, 0].astype(F32)
        wim = team[s, 1].astype(F32)
        cre, cim = twice(wre[NV:]), twice(wim[NV:])
        res, ims = [], []
        for h in range(4):
            lre = jnp.where(low_half, wre[2 * h:2 * h + 1], wre[2 * h + 1:2 * h + 2])
            lim = jnp.where(low_half, wim[2 * h:2 * h + 1], wim[2 * h + 1:2 * h + 2])
            left[s, h, 0] = lre
            left[s, h, 1] = lim
            if h < 2:
                pre, pim = conj_mul(lre, lim, cre, cim)
                res.append(pre)
                ims.append(pim)
        pre = jnp.concatenate(res, 0)
        pim = jnp.concatenate(ims, 0)
        r0 = s * NT
        r1 = TEAM * NT + s * NT
        own_p[r0:r0 + NT, 0:points] = pre.astype(BF16)
        own_p[r0:r0 + NT, points:] = (-pim).astype(BF16)
        own_p[r1:r1 + NT, 0:points] = pim.astype(BF16)
        own_p[r1:r1 + NT, points:] = pre.astype(BF16)

    team_part(0)

    side = 2 * ROWS
    col = iota((NT, side), 1)
    tr = iota((NT, side), 0)
    pick_v = one_hot((col // 4) % 4 == tr // 4)
    pick_w = one_hot(col % 4 == tr // 4)
    same = (iota((side, side), 0) // NT) % 4 == (iota((side, side), 1) // NT) % 4
    first = iota((8, side), 1) < ROWS
    row8 = iota((8, NT), 0)
    lane8 = iota((8, NT), 1)
    hit_d = row8 % 4 == lane8 % 4

    screen_in.wait()
    base = down * members
    for b in range(members):
        weights[b:b + 1, :] = screening[pl.ds(qmap[0, base + b], 1), :]
    sib_cols = pl.ds(pl.multiple_of((1 - rank) * share, 128), share)
    weight_in = send(weights.at[:, sib_cols], weights_in.at[1], w_ssem, w_rsem, (grp, sib))
    weights_in[0] = weights[:, my_cols]

    team_in.wait_recv()
    team_vec_in.wait_recv()
    team_part(1)

    part_in[0].wait_recv()
    sib_in = [send(part.at[0], part.at[half], p_ssem.at[half], p_rsem.at[half], (grp, sib))]
    for i in range(1, half):
        part_in.append(send(part.at[0], part.at[i], p_ssem.at[i], p_rsem.at[i], kin_at(grp, 2 * i)))

    def pass_on():
        for i in range(1, half):
            part_in[i].wait_recv()
            sib_in.append(send(part.at[i], part.at[half + i], p_ssem.at[half + i], p_rsem.at[half + i], (grp, sib)))

    xs = []
    for s in range(TEAM):
        x = team_vec[s].astype(BF16).astype(F32)
        xs.append((x[0:1], x[1:2]))
    xr = jnp.concatenate([x[0] for x in xs], 1)
    xi = jnp.concatenate([x[1] for x in xs], 1)
    x_rows = jnp.concatenate(
        [jnp.concatenate([xr, -xi], 1), jnp.concatenate([xi, xr], 1), jnp.zeros((6, 2 * TEAM * NT), F32)], 0
    ).astype(BF16)

    def basis_cols(n):
        return basis[:, :, n * CHUNK:(n + 1) * CHUNK].reshape(2 * points, CHUNK)

    for n in range(n_chunk):
        if n == n_chunk - 1:
            pass_on()
        basis_in[n].wait()
        cols = slice(n * CHUNK, (n + 1) * CHUNK)
        dens = mm(own_p[...], basis_cols(n)).astype(BF16)
        own_d[:, cols] = dens
        s_own[:, cols] = mm(x_rows, dens)[0:2]
    s_copies = []
    for i, target in enumerate(plane_at):
        s_copies.append(send(s_own, s_in.at[i], s_ssem.at[i], s_rsem.at[i], target))

    a_re, a_im = [], []
    for s in range(TEAM):
        for c in range(0, NC, 2):
            hit = lane8 % 4 == c + row8 // 4
            a_re.append(jnp.where(hit, xs[s][0], 0.0))
            a_im.append(jnp.where(hit, xs[s][1], 0.0))
    spread = mm(jnp.concatenate(a_re + a_im, 0).astype(BF16), pick_v)
    first_32 = iota((TEAM * NT, side), 1) < ROWS
    a_re, a_im = spread[0:TEAM * NT], spread[TEAM * NT:]
    u1 = twice(jnp.where(first_32, a_re, a_im))
    u2 = twice(jnp.where(first_32, -a_im, a_re))

    def products(i, pair_p, j):
        wre = part[i, 0].astype(F32)
        wim = part[i, 1].astype(F32)
        for kind in range(2):
            bands = slice(NV, NV + NC) if kind == 0 else slice(0, NV)
            rre, rim = twice(wre[bands]), twice(wim[bands])
            for s in range(TEAM):
                res, ims = [], []
                for h in range(2):
                    t = h + 2 - 2 * kind
                    pre, pim = conj_mul(left[s, t, 0], left[s, t, 1], rre, rim)
                    res.append(pre)
                    ims.append(pim)
                pre = jnp.concatenate(res, 0)
                pim = jnp.concatenate(ims, 0)
                r0 = kind * side + j * TEAM * NT + s * NT
                r1 = r0 + ROWS
                pair_p[r0:r0 + NT, 0:points] = pre.astype(BF16)
                pair_p[r0:r0 + NT, points:] = (-pim).astype(BF16)
                pair_p[r1:r1 + NT, 0:points] = pim.astype(BF16)
                pair_p[r1:r1 + NT, points:] = pre.astype(BF16)

    def kernel_of(batch, pair_p):
        total = None
        for n in range(n_chunk):
            cols = slice(n * CHUNK, (n + 1) * CHUNK)
            dens = mm(pair_p[...], basis_cols(n)).astype(BF16)
            rows = []
            for j in range(2):
                b = source(j * half + batch)
                rows += [jnp.broadcast_to(weights_in[s, pl.ds(b, 1), cols], (NT, CHUNK)) for s in range(TEAM)]
            weight = jnp.concatenate(rows * 2, 0)
            cond = (dens[0:side].astype(F32) * weight).astype(BF16)
            term = mm_nt(cond, dens[side:])
            total = term if total is None else total + term
        return jnp.where(same, total, 0.0)

    weight_in.wait_recv()
    sib_in[0].wait_recv()
    pairs_of = (pair_a, pair_b)

    def both_products(batch):
        for j in range(2):
            products(j * half + batch, pairs_of[batch % 2], j)

    both_products(0)
    total = s_own[...]
    for i, copy in enumerate(s_copies):
        copy.wait_recv()
        total = total + s_in[i]
    s_plane[...] = total
    g_copies = []
    for i in range(3):
        g_copies.append(send(s_plane, s_all.at[i], g_ssem.at[i], g_rsem.at[i], group_at(offset * (i + 1))))

    kerns = []
    for batch in range(half):
        kerns.append(kernel_of(batch, pairs_of[batch % 2]))
        if batch + 1 < half:
            sib_in[batch + 1].wait_recv()
            both_products(batch + 1)
    for copy in vec_in:
        copy.wait_recv()

    h_rows = []
    for kern in kerns:
        k_re, k_im = kern[re_rows], kern[im_rows]
        for value in (k_re * u1 + k_im * u2, k_im * u1 - k_re * u2):
            for j in range(2):
                r0 = j * TEAM * NT
                h_rows.append(value[r0:r0 + 8] + value[r0 + 8:r0 + 16] + value[r0 + 16:r0 + 24] + value[r0 + 24:r0 + 32])
    n_h = 8 * len(h_rows)
    h_sums = mm_nt(hi_lo(jnp.concatenate(h_rows, 0)), pick_w)
    h_sums = h_sums[0:n_h] + h_sums[n_h:]

    def h_row(batch, comp, j):
        r0 = 8 * (4 * batch + 2 * comp + j)
        return jnp.sum(jnp.where(hit_d, h_sums[r0:r0 + 8], 0.0), 0, keepdims=True)

    h_copies = []
    for i in range(members):
        h_send[i] = jnp.concatenate([h_row(i % half, 0, i // half), h_row(i % half, 1, i // half)], 0)
    d_re = jnp.zeros((ROWS, side), F32)
    d_im = jnp.zeros((ROWS, side), F32)
    for batch, kern in enumerate(kerns):
        k_re, k_im = kern[re_rows], kern[im_rows]
        x_parts = []
        for j in range(2):
            xb = part_vec[j * half + batch].astype(BF16).astype(F32)
            x_parts += [jnp.where(hit_d, xb[0:1], 0.0), jnp.where(hit_d, xb[1:2], 0.0)]
        xx = mm(jnp.concatenate(x_parts, 0).astype(BF16), pick_w)
        w1, w2 = [], []
        for j in range(2):
            x_re, x_im = xx[16 * j:16 * j + 8], xx[16 * j + 8:16 * j + 16]
            w1 += [jnp.where(first, x_re, -x_im)] * (2 * TEAM)
            w2 += [jnp.where(first, x_im, x_re)] * (2 * TEAM)
        w1 = jnp.concatenate(w1, 0)
        w2 = jnp.concatenate(w2, 0)
        d_re = d_re + (k_re * w1 + k_im * w2)
        d_im = d_im + (k_re * w2 - k_im * w1)
    n_d = TEAM * NT
    d_rows = jnp.concatenate([d_re[0:n_d] + d_re[n_d:], d_im[0:n_d] + d_im[n_d:]], 0)
    d_sums = mm_nt(hi_lo(d_rows), pick_v)
    d_sums = d_sums[0:2 * n_d] + d_sums[2 * n_d:]
    d_sums = jnp.where((iota((2 * n_d, NT), 0) // 4) % 4 == iota((2 * n_d, NT), 1) % 4, d_sums, 0.0)

    for i in range(members):
        h_copies.append(send(h_send.at[i], h_recv.at[i], h_ssem.at[i], h_rsem.at[i], (down, source(i))))

    total = s_plane[...]
    for i, copy in enumerate(g_copies):
        copy.wait_recv()
        total = total + s_all[i]
    pot = coulomb[my_cols].reshape(1, share) * total
    ex = mm_nt(jnp.concatenate([hi_lo(pot), jnp.zeros((4, share), BF16)], 0), own_d[...])
    ex = ex[0:2] + ex[2:4]
    exchange = jnp.concatenate([ex[0:1, 0:n_d] + ex[1:2, n_d:], ex[1:2, 0:n_d] - ex[0:1, n_d:]], 0)

    scale = 1.0 / n_k
    sums = []
    for s in range(TEAM):
        direct = jnp.concatenate(
            [jnp.sum(d_sums[r:r + NT], 0, keepdims=True) for r in (s * NT, n_d + s * NT)], 0)
        sums.append((2.0 * scale) * exchange[:, s * NT:(s + 1) * NT] - scale * direct)
    t_send[...] = sums[1]
    d_copy = send(t_send, t_recv, d_ssem, d_rsem, (grp, sib))
    result = energies[...] * team_vec[0] + sums[0]
    for copy in started:
        copy.wait_send()
    for copy in h_copies:
        copy.wait_recv()
    back = h_recv[0]
    for i in range(1, members):
        back = back + h_recv[i]
    d_copy.wait_recv()
    out[0] = result + t_recv[...] - scale * back


def on_device(waves, vector, energies, basis, screening, coulomb, qmap):
    groups = lax.axis_size("grp")
    members = lax.axis_size("kin")
    half = members // 2
    points = waves.shape[3]
    n_g = basis.shape[2]
    share = n_g // TEAM
    n_s = groups // 4 * (members // TEAM) - 1
    any_space = pl.BlockSpec(memory_space=pl.ANY)
    dma = pltpu.SemaphoreType.DMA
    vmem = pltpu.VMEM
    n_own = 2 * TEAM * NT
    return pl.pallas_call(
        functools.partial(kernel, groups, members, n_g),
        out_shape=jax.ShapeDtypeStruct(vector.shape, F32),
        in_specs=[any_space] * 7,
        out_specs=pl.BlockSpec(memory_space=vmem),
        scratch_shapes=[
            vmem(energies.shape, F32),
            vmem(coulomb.shape, F32),
            pltpu.SMEM(qmap.shape, jnp.int32),
            vmem((2, points, share), BF16),
            vmem(screening.shape, F32),
            vmem((TEAM,) + waves.shape[1:], BF16),
            vmem((TEAM, 2, NT), F32),
            vmem((members,) + waves.shape[1:], BF16),
            vmem((members, 2, NT), F32),
            vmem((TEAM, 4, 2, 8, points), F32),
            vmem((members, n_g), F32),
            vmem((TEAM, members, share), F32),
            vmem((n_own, 2 * points), BF16),
            vmem((4 * ROWS, 2 * points), BF16),
            vmem((4 * ROWS, 2 * points), BF16),
            vmem((n_own, share), BF16),
            vmem((2, share), F32),
            vmem((n_s, 2, share), F32),
            vmem((2, share), F32),
            vmem((3, 2, share), F32),
            vmem((members, 2, NT), F32),
            vmem((members, 2, NT), F32),
            vmem((2, NT), F32),
            vmem((2, NT), F32),
            dma((5,)), dma((share // CHUNK,)), dma,
            dma, dma, dma, dma,
            dma((members,)), dma((members,)),
            dma((members,)), dma((members,)),
            dma, dma,
            dma((n_s,)), dma((n_s,)),
            dma((3,)), dma((3,)),
            dma((members,)), dma((members,)),
            dma, dma,
        ],
        compiler_params=pltpu.CompilerParams(
            collective_id=0, has_side_effects=True, vmem_limit_bytes=60 * 1024 * 1024
        ),
    )(waves, vector, energies, basis, screening, coulomb, qmap)


def solution(mesh):
    return jax.shard_map(
        on_device,
        mesh=mesh,
        in_specs=(
            P(("grp", "kin"), None, None, None),
            P(("grp", "kin"), None, None),
            P(("grp", "kin"), None),
            P(),
            P(),
            P(),
            P(("grp", "kin"), None),
        ),
        out_specs=P(("grp", "kin"), None, None),
        check_vma=False,
    )
```

```python
import functools

import jax
import jax.numpy as jnp
from jax import lax
from jax.experimental import pallas as pl
from jax.experimental.pallas import tpu as pltpu
from jax.sharding import PartitionSpec as P

NV = 4
NC = 4
NT = 16
TEAM = 2
ROWS = 2 * TEAM * NT
CHUNK = 256
MESH = pl.DeviceIdType.MESH
F32 = jnp.float32
BF16 = jnp.bfloat16


def iota(shape, dim):
    return lax.broadcasted_iota(jnp.int32, shape, dim)


def mm(left, right):
    return jnp.dot(left, right, preferred_element_type=F32)


def mm_nt(left, right):
    return lax.dot_general(left, right, (((1,), (1,)), ((), ())), preferred_element_type=F32)


def hi_lo(value):
    high = value.astype(BF16)
    low = (value - high.astype(F32)).astype(BF16)
    return jnp.concatenate([high, low], 0)


def one_hot(cond):
    return jnp.where(cond, 1.0, 0.0).astype(BF16)


def conj_mul(lre, lim, rre, rim):
    return lre * rre + lim * rim, lre * rim - lim * rre


def twice(rows):
    return jnp.concatenate([rows, rows], 0)


def kernel(
    groups, members, n_g,
    waves_h, vector_h, energies_h, basis_h, screening_h, coulomb_h, qmap_h, out,
    energies, coulomb, qmap, basis, basis_o, screening, team, team_vec, part, part_vec,
    left, weights, weights_in, own_p, pair_a, pair_b, own_d, s_own, s_in, s_plane, s_all, h_send, h_recv, t_send, t_recv,
    small_sem, basis_sem, screen_sem, t_ssem, t_rsem, tv_ssem, tv_rsem, p_ssem, p_rsem, pv_ssem, pv_rsem,
    w_ssem, w_rsem, s_ssem, s_rsem, g_ssem, g_rsem, h_ssem, h_rsem, d_ssem, d_rsem,
):
    offset = groups // 4
    half = members // 2
    teams = members // TEAM
    n_k = groups * members
    points = waves_h.shape[3]
    share = n_g // TEAM
    n_chunk = share // CHUNK
    grp = lax.axis_index("grp")
    kin = lax.axis_index("kin")
    rank = lax.rem(kin, TEAM)
    sib = kin + 1 - 2 * rank
    up = lax.rem(grp + offset, groups)
    down = lax.rem(grp + groups - offset, groups)

    def source(i):
        if i < half:
            return lax.rem(kin + members - 2 * i, members)
        return lax.rem(sib + members - 2 * (i - half), members)

    def group_at(dg):
        return (lax.rem(grp + dg, groups), kin)

    def spot_at(ds, dk):
        level = lax.div(grp, offset)
        return kin_at(level * offset + lax.rem(grp - level * offset + ds, offset), dk)

    def kin_at(g, dk):
        return (g, lax.rem(kin + dk, members))

    plane = [(ds, dk) for ds in range(offset) for dk in range(members) if (ds, dk) != (0, 0)]
    plane_at = [spot_at(ds, dk) for ds, dk in plane]
    greet = [kin_at(g, dk) for g in (up, down) for dk in range(members)] + [group_at(2 * offset)] + plane_at
    barrier = pltpu.get_barrier_semaphore()
    for target in greet:
        pl.semaphore_signal(barrier, inc=1, device_id=target, device_id_type=MESH)

    my_cols = pl.ds(pl.multiple_of(rank * share, 128), share)
    pairs = [
        (waves_h, team.at[pl.ds(0, 1)]), (vector_h, team_vec.at[pl.ds(0, 1)]), (qmap_h, qmap),
        (energies_h, energies), (coulomb_h, coulomb),
    ]
    small = []
    for i, (src, dst) in enumerate(pairs):
        small.append(pltpu.make_async_copy(src, dst, small_sem.at[i]))
        small[-1].start()
    basis_in = []
    starts = [pl.multiple_of(r * share + n * CHUNK, 128) for r in (rank, 1 - rank) for n in range(n_chunk)]
    for n, start in enumerate(starts):
        dst = (basis if n < n_chunk else basis_o).at[:, :, pl.ds(n % n_chunk * CHUNK, CHUNK)]
        basis_in.append(pltpu.make_async_copy(basis_h.at[:, :, pl.ds(start, CHUNK)], dst, basis_sem.at[n]))
        basis_in[-1].start()
        if n == 0:
            screen_in = pltpu.make_async_copy(screening_h, screening, screen_sem)
            screen_in.start()
    pl.semaphore_wait(barrier, len(greet))

    started = []

    def send(src, dst, ssem, rsem, target):
        copy = pltpu.make_async_remote_copy(
            src_ref=src, dst_ref=dst, send_sem=ssem, recv_sem=rsem, device_id=target, device_id_type=MESH
        )
        copy.start()
        started.append(copy)
        return copy

    one = pl.ds(1, 1)
    targets = [kin_at(up, 2 * i) for i in range(half)]
    targets += [(up, lax.rem(sib + 2 * i, members)) for i in range(half)]
    team_in = send(waves_h, team.at[one], t_ssem, t_rsem, (grp, sib))
    team_vec_in = send(vector_h, team_vec.at[one], tv_ssem, tv_rsem, (grp, sib))
    part_in = []
    for i, target in enumerate(targets):
        part_in.append(send(waves_h, part.at[pl.ds(i, 1)], p_ssem.at[i], p_rsem.at[i], target))
    vec_in = []
    for i, target in enumerate(targets):
        vec_in.append(send(vector_h, part_vec.at[pl.ds(i, 1)], pv_ssem.at[i], pv_rsem.at[i], target))

    for copy in small:
        copy.wait()
    low_half = iota((8, points), 0) < 4
    re_rows, im_rows = slice(0, ROWS), slice(ROWS, 2 * ROWS)

    def team_part(s):
        wre = team[s, 0].astype(F32)
        wim = team[s, 1].astype(F32)
        cre, cim = twice(wre[NV:]), twice(wim[NV:])
        res, ims = [], []
        for h in range(4):
            lre = jnp.where(low_half, wre[2 * h:2 * h + 1], wre[2 * h + 1:2 * h + 2])
            lim = jnp.where(low_half, wim[2 * h:2 * h + 1], wim[2 * h + 1:2 * h + 2])
            left[s, h, 0] = lre
            left[s, h, 1] = lim
            if s == 0 and h < 2:
                pre, pim = conj_mul(lre, lim, cre, cim)
                res.append(pre)
                ims.append(pim)
        if s == 0:
            pre = jnp.concatenate(res, 0)
            pim = jnp.concatenate(ims, 0)
            own_p[0:NT, 0:points] = pre.astype(BF16)
            own_p[0:NT, points:] = (-pim).astype(BF16)
            own_p[NT:2 * NT, 0:points] = pim.astype(BF16)
            own_p[NT:2 * NT, points:] = pre.astype(BF16)

    team_part(0)

    side = 2 * ROWS
    col = iota((NT, side), 1)
    tr = iota((NT, side), 0)
    pick_v = one_hot((col // 4) % 4 == tr // 4)
    pick_w = one_hot(col % 4 == tr // 4)
    same = (iota((side, side), 0) // NT) % 4 == (iota((side, side), 1) // NT) % 4
    first = iota((8, side), 1) < ROWS
    row8 = iota((8, NT), 0)
    lane8 = iota((8, NT), 1)
    hit_d = row8 % 4 == lane8 % 4

    screen_in.wait()
    base = down * members
    for b in range(members):
        weights[b:b + 1, :] = screening[pl.ds(qmap[0, base + b], 1), :]
    sib_cols = pl.ds(pl.multiple_of((1 - rank) * share, 128), share)
    weight_in = send(weights.at[:, sib_cols], weights_in.at[1], w_ssem, w_rsem, (grp, sib))
    weights_in[0] = weights[:, my_cols]

    def vector_of(ref):
        x = ref.astype(BF16).astype(F32)
        return x[0:1], x[1:2]

    xr, xi = vector_of(team_vec[0])
    x_rows = jnp.concatenate(
        [jnp.concatenate([xr, -xi], 1), jnp.concatenate([xi, xr], 1), jnp.zeros((6, 2 * NT), F32)], 0
    ).astype(BF16)

    def basis_cols(n, ref):
        return ref[:, :, n * CHUNK:(n + 1) * CHUNK].reshape(2 * points, CHUNK)

    for n, start in enumerate(starts):
        basis_in[n].wait()
        dens = mm(own_p[...], basis_cols(n % n_chunk, basis if n < n_chunk else basis_o)).astype(BF16)
        own_d[:, pl.ds(start, CHUNK)] = dens
        s_own[:, pl.ds(start, CHUNK)] = mm(x_rows, dens)[0:2]
    s_copies = []
    for i, target in enumerate(plane_at):
        s_copies.append(send(s_own, s_in.at[i], s_ssem.at[i], s_rsem.at[i], target))

    team_in.wait_recv()
    team_vec_in.wait_recv()
    team_part(1)
    xs = [(xr, xi), vector_of(team_vec[1])]

    a_re, a_im = [], []
    for s in range(TEAM):
        for c in range(0, NC, 2):
            hit = lane8 % 4 == c + row8 // 4
            a_re.append(jnp.where(hit, xs[s][0], 0.0))
            a_im.append(jnp.where(hit, xs[s][1], 0.0))
    spread = mm(jnp.concatenate(a_re + a_im, 0).astype(BF16), pick_v)
    first_32 = iota((TEAM * NT, side), 1) < ROWS
    a_re, a_im = spread[0:TEAM * NT], spread[TEAM * NT:]
    u1 = twice(jnp.where(first_32, a_re, a_im))
    u2 = twice(jnp.where(first_32, -a_im, a_re))

    def products(i, pair_p, j):
        wre = part[i, 0].astype(F32)
        wim = part[i, 1].astype(F32)
        for kind in range(2):
            bands = slice(NV, NV + NC) if kind == 0 else slice(0, NV)
            rre, rim = twice(wre[bands]), twice(wim[bands])
            for s in range(TEAM):
                res, ims = [], []
                for h in range(2):
                    t = h + 2 - 2 * kind
                    pre, pim = conj_mul(left[s, t, 0], left[s, t, 1], rre, rim)
                    res.append(pre)
                    ims.append(pim)
                pre = jnp.concatenate(res, 0)
                pim = jnp.concatenate(ims, 0)
                r0 = kind * side + j * TEAM * NT + s * NT
                r1 = r0 + ROWS
                pair_p[r0:r0 + NT, 0:points] = pre.astype(BF16)
                pair_p[r0:r0 + NT, points:] = (-pim).astype(BF16)
                pair_p[r1:r1 + NT, 0:points] = pim.astype(BF16)
                pair_p[r1:r1 + NT, points:] = pre.astype(BF16)

    def kernel_of(batch, pair_p):
        total = None
        for n in range(n_chunk):
            cols = slice(n * CHUNK, (n + 1) * CHUNK)
            dens = mm(pair_p[...], basis_cols(n, basis)).astype(BF16)
            rows = []
            for j in range(2):
                b = source(2 * batch + j)
                rows += [jnp.broadcast_to(weights_in[s, pl.ds(b, 1), cols], (NT, CHUNK)) for s in range(TEAM)]
            weight = jnp.concatenate(rows * 2, 0)
            cond = (dens[0:side].astype(F32) * weight).astype(BF16)
            term = mm_nt(cond, dens[side:])
            total = term if total is None else total + term
        return jnp.where(same, total, 0.0)

    weight_in.wait_recv()
    pairs_of = (pair_a, pair_b)

    def both_products(batch):
        for j in range(2):
            part_in[2 * batch + j].wait_recv()
        for j in range(2):
            products(2 * batch + j, pairs_of[batch % 2], j)

    both_products(0)
    kerns = [kernel_of(0, pairs_of[0])]
    total = s_own[...]
    for i, copy in enumerate(s_copies):
        copy.wait_recv()
        total = total + s_in[i]
    s_plane[...] = total
    g_copies = []
    for i in range(3):
        g_copies.append(send(s_plane, s_all.at[i], g_ssem.at[i], g_rsem.at[i], group_at(offset * (i + 1))))
    for batch in range(1, half):
        both_products(batch)
        kerns.append(kernel_of(batch, pairs_of[batch % 2]))
    for copy in vec_in:
        copy.wait_recv()

    h_rows = []
    for kern in kerns:
        k_re, k_im = kern[re_rows], kern[im_rows]
        for value in (k_re * u1 + k_im * u2, k_im * u1 - k_re * u2):
            for j in range(2):
                r0 = j * TEAM * NT
                h_rows.append(value[r0:r0 + 8] + value[r0 + 8:r0 + 16] + value[r0 + 16:r0 + 24] + value[r0 + 24:r0 + 32])
    n_h = 8 * len(h_rows)
    h_sums = mm_nt(hi_lo(jnp.concatenate(h_rows, 0)), pick_w)
    h_sums = h_sums[0:n_h] + h_sums[n_h:]

    def h_row(batch, comp, j):
        r0 = 8 * (4 * batch + 2 * comp + j)
        return jnp.sum(jnp.where(hit_d, h_sums[r0:r0 + 8], 0.0), 0, keepdims=True)

    h_copies = []
    for i in range(members):
        h_send[i] = jnp.concatenate([h_row(i // 2, 0, i % 2), h_row(i // 2, 1, i % 2)], 0)
    d_re = jnp.zeros((ROWS, side), F32)
    d_im = jnp.zeros((ROWS, side), F32)
    for batch, kern in enumerate(kerns):
        k_re, k_im = kern[re_rows], kern[im_rows]
        x_parts = []
        for j in range(2):
            xb = part_vec[2 * batch + j].astype(BF16).astype(F32)
            x_parts += [jnp.where(hit_d, xb[0:1], 0.0), jnp.where(hit_d, xb[1:2], 0.0)]
        xx = mm(jnp.concatenate(x_parts, 0).astype(BF16), pick_w)
        w1, w2 = [], []
        for j in range(2):
            x_re, x_im = xx[16 * j:16 * j + 8], xx[16 * j + 8:16 * j + 16]
            w1 += [jnp.where(first, x_re, -x_im)] * (2 * TEAM)
            w2 += [jnp.where(first, x_im, x_re)] * (2 * TEAM)
        w1 = jnp.concatenate(w1, 0)
        w2 = jnp.concatenate(w2, 0)
        d_re = d_re + (k_re * w1 + k_im * w2)
        d_im = d_im + (k_re * w2 - k_im * w1)
    n_d = TEAM * NT
    d_rows = jnp.concatenate([d_re[0:n_d] + d_re[n_d:], d_im[0:n_d] + d_im[n_d:]], 0)
    d_sums = mm_nt(hi_lo(d_rows), pick_v)
    d_sums = d_sums[0:2 * n_d] + d_sums[2 * n_d:]
    d_sums = jnp.where((iota((2 * n_d, NT), 0) // 4) % 4 == iota((2 * n_d, NT), 1) % 4, d_sums, 0.0)

    for i in range(members):
        h_copies.append(send(h_send.at[i], h_recv.at[i], h_ssem.at[i], h_rsem.at[i], (down, source(i))))

    scale = 1.0 / n_k
    sums = []
    for s in range(TEAM):
        sums.append(jnp.concatenate(
            [jnp.sum(d_sums[r:r + NT], 0, keepdims=True) for r in (s * NT, n_d + s * NT)], 0))
    t_send[...] = sums[1]
    d_copy = send(t_send, t_recv, d_ssem, d_rsem, (grp, sib))

    total = s_plane[...]
    for i, copy in enumerate(g_copies):
        copy.wait_recv()
        total = total + s_all[i]
    pot = coulomb[...].reshape(1, n_g) * total
    ex = mm_nt(jnp.concatenate([hi_lo(pot), jnp.zeros((4, n_g), BF16)], 0), own_d[...])
    ex = ex[0:2] + ex[2:4]
    exchange = jnp.concatenate([ex[0:1, 0:NT] + ex[1:2, NT:], ex[1:2, 0:NT] - ex[0:1, NT:]], 0)
    result = energies[...] * team_vec[0] + (2.0 * scale) * exchange
    for copy in started:
        copy.wait_send()
    for copy in h_copies:
        copy.wait_recv()
    back = sums[0] + h_recv[0]
    for i in range(1, members):
        back = back + h_recv[i]
    d_copy.wait_recv()
    out[0] = result - scale * (back + t_recv[...])


def on_device(waves, vector, energies, basis, screening, coulomb, qmap):
    groups = lax.axis_size("grp")
    members = lax.axis_size("kin")
    half = members // 2
    points = waves.shape[3]
    n_g = basis.shape[2]
    share = n_g // TEAM
    n_s = groups // 4 * members - 1
    any_space = pl.BlockSpec(memory_space=pl.ANY)
    dma = pltpu.SemaphoreType.DMA
    vmem = pltpu.VMEM
    n_own = 2 * NT
    return pl.pallas_call(
        functools.partial(kernel, groups, members, n_g),
        out_shape=jax.ShapeDtypeStruct(vector.shape, F32),
        in_specs=[any_space] * 7,
        out_specs=pl.BlockSpec(memory_space=vmem),
        scratch_shapes=[
            vmem(energies.shape, F32),
            vmem(coulomb.shape, F32),
            pltpu.SMEM(qmap.shape, jnp.int32),
            vmem((2, points, share), BF16),
            vmem((2, points, share), BF16),
            vmem(screening.shape, F32),
            vmem((TEAM,) + waves.shape[1:], BF16),
            vmem((TEAM, 2, NT), F32),
            vmem((members,) + waves.shape[1:], BF16),
            vmem((members, 2, NT), F32),
            vmem((TEAM, 4, 2, 8, points), F32),
            vmem((members, n_g), F32),
            vmem((TEAM, members, share), F32),
            vmem((n_own, 2 * points), BF16),
            vmem((4 * ROWS, 2 * points), BF16),
            vmem((4 * ROWS, 2 * points), BF16),
            vmem((n_own, n_g), BF16),
            vmem((2, n_g), F32),
            vmem((n_s, 2, n_g), F32),
            vmem((2, n_g), F32),
            vmem((3, 2, n_g), F32),
            vmem((members, 2, NT), F32),
            vmem((members, 2, NT), F32),
            vmem((2, NT), F32),
            vmem((2, NT), F32),
            dma((5,)), dma((n_g // CHUNK,)), dma,
            dma, dma, dma, dma,
            dma((members,)), dma((members,)),
            dma((members,)), dma((members,)),
            dma, dma,
            dma((n_s,)), dma((n_s,)),
            dma((3,)), dma((3,)),
            dma((members,)), dma((members,)),
            dma, dma,
        ],
        compiler_params=pltpu.CompilerParams(
            collective_id=0, has_side_effects=True, vmem_limit_bytes=60 * 1024 * 1024
        ),
    )(waves, vector, energies, basis, screening, coulomb, qmap)


def solution(mesh):
    return jax.shard_map(
        on_device,
        mesh=mesh,
        in_specs=(
            P(("grp", "kin"), None, None, None),
            P(("grp", "kin"), None, None),
            P(("grp", "kin"), None),
            P(),
            P(),
            P(),
            P(("grp", "kin"), None),
        ),
        out_specs=P(("grp", "kin"), None, None),
        check_vma=False,
    )
```

```python
import functools

import jax
import jax.numpy as jnp
from jax import lax
from jax.experimental import pallas as pl
from jax.experimental.pallas import tpu as pltpu
from jax.sharding import PartitionSpec as P

NV = 4
NC = 4
NT = 16
TEAM = 2
ROWS = 2 * TEAM * NT
CHUNK = 256
MESH = pl.DeviceIdType.MESH
F32 = jnp.float32
BF16 = jnp.bfloat16


def iota(shape, dim):
    return lax.broadcasted_iota(jnp.int32, shape, dim)


def mm(left, right):
    return jnp.dot(left, right, preferred_element_type=F32)


def mm_nt(left, right):
    return lax.dot_general(left, right, (((1,), (1,)), ((), ())), preferred_element_type=F32)


def hi_lo(value):
    high = value.astype(BF16)
    low = (value - high.astype(F32)).astype(BF16)
    return jnp.concatenate([high, low], 0)


def one_hot(cond):
    return jnp.where(cond, 1.0, 0.0).astype(BF16)


def conj_mul(lre, lim, rre, rim):
    return lre * rre + lim * rim, lre * rim - lim * rre


def twice(rows):
    return jnp.concatenate([rows, rows], 0)


def kernel(
    groups, members, n_g,
    waves_h, vector_h, energies_h, basis_h, screening_h, coulomb_h, qmap_h, out,
    energies, coulomb, qmap, basis, screening, team, team_vec, part, part_vec,
    left, weights, weights_in, own_p, pair_p, own_d, s_own, s_in, s_plane, s_all, h_send, h_recv, t_send, t_recv,
    small_sem, basis_sem, screen_sem, t_ssem, t_rsem, tv_ssem, tv_rsem, p_ssem, p_rsem, pv_ssem, pv_rsem, r_ssem,
    w_ssem, w_rsem, s_ssem, s_rsem, g_ssem, g_rsem, h_ssem, h_rsem, d_ssem, d_rsem,
):
    offset = groups // 4
    half = members // 2
    teams = members // TEAM
    n_k = groups * members
    points = waves_h.shape[3]
    share = n_g // TEAM
    n_chunk = share // CHUNK
    grp = lax.axis_index("grp")
    kin = lax.axis_index("kin")
    rank = lax.rem(kin, TEAM)
    sib = kin + 1 - 2 * rank
    up = lax.rem(grp + offset, groups)
    down = lax.rem(grp + groups - offset, groups)

    def source(i):
        if i < half:
            return lax.rem(kin + members - 2 * i, members)
        return lax.rem(sib + members - 2 * (i - half), members)

    def group_at(dg):
        return (lax.rem(grp + dg, groups), kin)

    def spot_at(ds, dk):
        level = lax.div(grp, offset)
        return kin_at(level * offset + lax.rem(grp - level * offset + ds, offset), dk)

    def kin_at(g, dk):
        return (g, lax.rem(kin + dk, members))

    plane = [(ds, dt) for ds in range(offset) for dt in range(teams) if (ds, dt) != (0, 0)]
    plane_at = [spot_at(ds, TEAM * dt) for ds, dt in plane]
    greet = [kin_at(g, dk) for g in (up, down) for dk in range(members)] + [group_at(2 * offset), (grp, sib)] + plane_at
    barrier = pltpu.get_barrier_semaphore()
    for target in greet:
        pl.semaphore_signal(barrier, inc=1, device_id=target, device_id_type=MESH)

    my_cols = pl.ds(pl.multiple_of(rank * share, 128), share)
    pairs = [
        (waves_h, team.at[pl.ds(0, 1)]), (vector_h, team_vec.at[pl.ds(0, 1)]), (qmap_h, qmap),
        (energies_h, energies), (coulomb_h, coulomb),
    ]
    small = []
    for i, (src, dst) in enumerate(pairs):
        small.append(pltpu.make_async_copy(src, dst, small_sem.at[i]))
        small[-1].start()
    basis_in = []
    for n in range(n_chunk):
        src = pl.ds(pl.multiple_of(rank * share + n * CHUNK, 128), CHUNK)
        basis_in.append(pltpu.make_async_copy(
            basis_h.at[:, :, src], basis.at[:, :, pl.ds(n * CHUNK, CHUNK)], basis_sem.at[n]))
        basis_in[-1].start()
        if n == 0:
            screen_in = pltpu.make_async_copy(screening_h, screening, screen_sem)
            screen_in.start()
    pl.semaphore_wait(barrier, len(greet))

    started = []

    def send(src, dst, ssem, rsem, target):
        copy = pltpu.make_async_remote_copy(
            src_ref=src, dst_ref=dst, send_sem=ssem, recv_sem=rsem, device_id=target, device_id_type=MESH
        )
        copy.start()
        started.append(copy)
        return copy

    one = pl.ds(1, 1)
    part_in = [None] * members
    for i in range(half):
        part_in[i] = send(waves_h, part.at[pl.ds(i, 1)], p_ssem.at[i], p_rsem.at[i], kin_at(up, 2 * i))
    team_in = send(waves_h, team.at[one], t_ssem, t_rsem, (grp, sib))
    team_vec_in = send(vector_h, team_vec.at[one], tv_ssem, tv_rsem, (grp, sib))
    vec_in = []
    for i in range(members):
        if i < half:
            target = kin_at(up, 2 * i)
        else:
            target = (up, lax.rem(sib + 2 * (i - half), members))
        vec_in.append(send(vector_h, part_vec.at[pl.ds(i, 1)], pv_ssem.at[i], pv_rsem.at[i], target))

    for copy in small:
        copy.wait()
    low_half = iota((8, points), 0) < 4
    re_rows, im_rows = slice(0, ROWS), slice(ROWS, 2 * ROWS)

    def team_part(s):
        wre = team[s, 0].astype(F32)
        wim = team[s, 1].astype(F32)
        cre, cim = twice(wre[NV:]), twice(wim[NV:])
        res, ims = [], []
        for h in range(4):
            lre = jnp.where(low_half, wre[2 * h:2 * h + 1], wre[2 * h + 1:2 * h + 2])
            lim = jnp.where(low_half, wim[2 * h:2 * h + 1], wim[2 * h + 1:2 * h + 2])
            left[s, h, 0] = lre
            left[s, h, 1] = lim
            if h < 2:
                pre, pim = conj_mul(lre, lim, cre, cim)
                res.append(pre)
                ims.append(pim)
        pre = jnp.concatenate(res, 0)
        pim = jnp.concatenate(ims, 0)
        r0 = s * NT
        r1 = TEAM * NT + s * NT
        own_p[r0:r0 + NT, 0:points] = pre.astype(BF16)
        own_p[r0:r0 + NT, points:] = (-pim).astype(BF16)
        own_p[r1:r1 + NT, 0:points] = pim.astype(BF16)
        own_p[r1:r1 + NT, points:] = pre.astype(BF16)

    team_part(0)

    side = 2 * ROWS
    col = iota((NT, side), 1)
    tr = iota((NT, side), 0)
    pick_v = one_hot((col // 4) % 4 == tr // 4)
    pick_w = one_hot(col % 4 == tr // 4)
    same = (iota((side, side), 0) // NT) % 4 == (iota((side, side), 1) // NT) % 4
    first = iota((8, side), 1) < ROWS
    row8 = iota((8, NT), 0)
    lane8 = iota((8, NT), 1)
    hit_d = row8 % 4 == lane8 % 4

    screen_in.wait()
    base = down * members
    for b in range(members):
        weights[b:b + 1, :] = screening[pl.ds(qmap[0, base + b], 1), :]
    sib_cols = pl.ds(pl.multiple_of((1 - rank) * share, 128), share)
    weight_in = send(weights.at[:, sib_cols], weights_in.at[1], w_ssem, w_rsem, (grp, sib))
    weights_in[0] = weights[:, my_cols]

    team_in.wait_recv()
    team_vec_in.wait_recv()
    team_part(1)
    xs = []
    for s in range(TEAM):
        x = team_vec[s].astype(BF16).astype(F32)
        xs.append((x[0:1], x[1:2]))
    xr = jnp.concatenate([x[0] for x in xs], 1)
    xi = jnp.concatenate([x[1] for x in xs], 1)
    x_rows = jnp.concatenate(
        [jnp.concatenate([xr, -xi], 1), jnp.concatenate([xi, xr], 1), jnp.zeros((6, 2 * TEAM * NT), F32)], 0
    ).astype(BF16)

    def basis_cols(n):
        return basis[:, :, n * CHUNK:(n + 1) * CHUNK].reshape(2 * points, CHUNK)

    for n in range(n_chunk):
        basis_in[n].wait()
        cols = slice(n * CHUNK, (n + 1) * CHUNK)
        dens = mm(own_p[...], basis_cols(n)).astype(BF16)
        own_d[:, cols] = dens
        s_own[:, cols] = mm(x_rows, dens)[0:2]
    s_copies = []
    for i, target in enumerate(plane_at):
        s_copies.append(send(s_own, s_in.at[i], s_ssem.at[i], s_rsem.at[i], target))

    a_re, a_im = [], []
    for s in range(TEAM):
        for c in range(0, NC, 2):
            hit = lane8 % 4 == c + row8 // 4
            a_re.append(jnp.where(hit, xs[s][0], 0.0))
            a_im.append(jnp.where(hit, xs[s][1], 0.0))
    spread = mm(jnp.concatenate(a_re + a_im, 0).astype(BF16), pick_v)
    first_32 = iota((TEAM * NT, side), 1) < ROWS
    a_re, a_im = spread[0:TEAM * NT], spread[TEAM * NT:]
    u1 = twice(jnp.where(first_32, a_re, a_im))
    u2 = twice(jnp.where(first_32, -a_im, a_re))

    def products(i, batch, j):
        wre = part[i, 0].astype(F32)
        wim = part[i, 1].astype(F32)
        for kind in range(2):
            bands = slice(NV, NV + NC) if kind == 0 else slice(0, NV)
            rre, rim = twice(wre[bands]), twice(wim[bands])
            for s in range(TEAM):
                res, ims = [], []
                for h in range(2):
                    t = h + 2 - 2 * kind
                    pre, pim = conj_mul(left[s, t, 0], left[s, t, 1], rre, rim)
                    res.append(pre)
                    ims.append(pim)
                pre = jnp.concatenate(res, 0)
                pim = jnp.concatenate(ims, 0)
                r0 = kind * side + j * TEAM * NT + s * NT
                r1 = r0 + ROWS
                pair_p[batch, r0:r0 + NT, 0:points] = pre.astype(BF16)
                pair_p[batch, r0:r0 + NT, points:] = (-pim).astype(BF16)
                pair_p[batch, r1:r1 + NT, 0:points] = pim.astype(BF16)
                pair_p[batch, r1:r1 + NT, points:] = pre.astype(BF16)

    def kernel_of(batch):
        total = None
        for n in range(n_chunk):
            cols = slice(n * CHUNK, (n + 1) * CHUNK)
            dens = mm(pair_p[batch % 2], basis_cols(n)).astype(BF16)
            rows = []
            for j in range(2):
                b = source(2 * batch + j)
                rows += [jnp.broadcast_to(weights_in[s, pl.ds(b, 1), cols], (NT, CHUNK)) for s in range(TEAM)]
            weight = jnp.concatenate(rows * 2, 0)
            cond = (dens[0:side].astype(F32) * weight).astype(BF16)
            term = mm_nt(cond, dens[side:])
            total = term if total is None else total + term
        return jnp.where(same, total, 0.0)

    kerns = []
    for batch in range(members // 2):
        for i in (2 * batch, 2 * batch + 1):
            if i >= half:
                k = pl.ds(i, 1)
                part_in[i] = pltpu.make_async_remote_copy(
                    src_ref=part.at[k], dst_ref=part.at[k], send_sem=r_ssem.at[i - half], recv_sem=p_rsem.at[i],
                    device_id=(grp, sib), device_id_type=MESH)
            part_in[i].wait_recv()
            if i < half:
                send(part.at[i], part.at[half + i], r_ssem.at[i], p_rsem.at[half + i], (grp, sib))
        vec_in[2 * batch].wait_recv()
        vec_in[2 * batch + 1].wait_recv()
        if batch == 0:
            weight_in.wait_recv()
        for j in range(2):
            products(2 * batch + j, batch % 2, j)
        kerns.append(kernel_of(batch))
        if batch == 0:
            total = s_own[...]
            for i, copy in enumerate(s_copies):
                copy.wait_recv()
                total = total + s_in[i]
            s_plane[...] = total
            g_copies = []
            for i in range(3):
                g_copies.append(send(s_plane, s_all.at[i], g_ssem.at[i], g_rsem.at[i], group_at(offset * (i + 1))))

    h_rows = []
    for kern in kerns:
        k_re, k_im = kern[re_rows], kern[im_rows]
        for value in (k_re * u1 + k_im * u2, k_im * u1 - k_re * u2):
            for j in range(2):
                r0 = j * TEAM * NT
                h_rows.append(value[r0:r0 + 8] + value[r0 + 8:r0 + 16] + value[r0 + 16:r0 + 24] + value[r0 + 24:r0 + 32])
    n_h = 8 * len(h_rows)
    h_sums = mm_nt(hi_lo(jnp.concatenate(h_rows, 0)), pick_w)
    h_sums = h_sums[0:n_h] + h_sums[n_h:]

    def h_row(batch, comp, j):
        r0 = 8 * (4 * batch + 2 * comp + j)
        return jnp.sum(jnp.where(hit_d, h_sums[r0:r0 + 8], 0.0), 0, keepdims=True)

    h_copies = []
    for i in range(members):
        h_send[i] = jnp.concatenate([h_row(i // 2, 0, i % 2), h_row(i // 2, 1, i % 2)], 0)

    d_re = jnp.zeros((ROWS, side), F32)
    d_im = jnp.zeros((ROWS, side), F32)
    for batch, kern in enumerate(kerns):
        k_re, k_im = kern[re_rows], kern[im_rows]
        x_parts = []
        for j in range(2):
            xb = part_vec[2 * batch + j].astype(BF16).astype(F32)
            x_parts += [jnp.where(hit_d, xb[0:1], 0.0), jnp.where(hit_d, xb[1:2], 0.0)]
        xx = mm(jnp.concatenate(x_parts, 0).astype(BF16), pick_w)
        w1, w2 = [], []
        for j in range(2):
            x_re, x_im = xx[16 * j:16 * j + 8], xx[16 * j + 8:16 * j + 16]
            w1 += [jnp.where(first, x_re, -x_im)] * (2 * TEAM)
            w2 += [jnp.where(first, x_im, x_re)] * (2 * TEAM)
        w1 = jnp.concatenate(w1, 0)
        w2 = jnp.concatenate(w2, 0)
        d_re = d_re + (k_re * w1 + k_im * w2)
        d_im = d_im + (k_re * w2 - k_im * w1)
    n_d = TEAM * NT
    d_rows = jnp.concatenate([d_re[0:n_d] + d_re[n_d:], d_im[0:n_d] + d_im[n_d:]], 0)
    d_sums = mm_nt(hi_lo(d_rows), pick_v)
    d_sums = d_sums[0:2 * n_d] + d_sums[2 * n_d:]
    d_sums = jnp.where((iota((2 * n_d, NT), 0) // 4) % 4 == iota((2 * n_d, NT), 1) % 4, d_sums, 0.0)

    for i in range(members):
        h_copies.append(send(h_send.at[i], h_recv.at[i], h_ssem.at[i], h_rsem.at[i], (down, source(i))))

    total = s_plane[...]
    for i, copy in enumerate(g_copies):
        copy.wait_recv()
        total = total + s_all[i]
    pot = coulomb[my_cols].reshape(1, share) * total
    ex = mm_nt(jnp.concatenate([hi_lo(pot), jnp.zeros((4, share), BF16)], 0), own_d[...])
    ex = ex[0:2] + ex[2:4]
    exchange = jnp.concatenate([ex[0:1, 0:n_d] + ex[1:2, n_d:], ex[1:2, 0:n_d] - ex[0:1, n_d:]], 0)

    scale = 1.0 / n_k
    sums = []
    for s in range(TEAM):
        direct = jnp.concatenate(
            [jnp.sum(d_sums[r:r + NT], 0, keepdims=True) for r in (s * NT, n_d + s * NT)], 0)
        sums.append((2.0 * scale) * exchange[:, s * NT:(s + 1) * NT] - scale * direct)
    t_send[...] = sums[1]
    d_copy = send(t_send, t_recv, d_ssem, d_rsem, (grp, sib))
    result = energies[...] * team_vec[0] + sums[0]
    for copy in started:
        copy.wait_send()
    for copy in h_copies:
        copy.wait_recv()
    back = h_recv[0]
    for i in range(1, members):
        back = back + h_recv[i]
    d_copy.wait_recv()
    out[0] = result + t_recv[...] - scale * back


def on_device(waves, vector, energies, basis, screening, coulomb, qmap):
    groups = lax.axis_size("grp")
    members = lax.axis_size("kin")
    half = members // 2
    points = waves.shape[3]
    n_g = basis.shape[2]
    share = n_g // TEAM
    n_s = groups // 4 * (members // TEAM) - 1
    any_space = pl.BlockSpec(memory_space=pl.ANY)
    dma = pltpu.SemaphoreType.DMA
    vmem = pltpu.VMEM
    n_own = 2 * TEAM * NT
    return pl.pallas_call(
        functools.partial(kernel, groups, members, n_g),
        out_shape=jax.ShapeDtypeStruct(vector.shape, F32),
        in_specs=[any_space] * 7,
        out_specs=pl.BlockSpec(memory_space=vmem),
        scratch_shapes=[
            vmem(energies.shape, F32),
            vmem(coulomb.shape, F32),
            pltpu.SMEM(qmap.shape, jnp.int32),
            vmem((2, points, share), BF16),
            vmem(screening.shape, F32),
            vmem((TEAM,) + waves.shape[1:], BF16),
            vmem((TEAM, 2, NT), F32),
            vmem((members,) + waves.shape[1:], BF16),
            vmem((members, 2, NT), F32),
            vmem((TEAM, 4, 2, 8, points), F32),
            vmem((members, n_g), F32),
            vmem((TEAM, members, share), F32),
            vmem((n_own, 2 * points), BF16),
            vmem((2, 4 * ROWS, 2 * points), BF16),
            vmem((n_own, share), BF16),
            vmem((2, share), F32),
            vmem((n_s, 2, share), F32),
            vmem((2, share), F32),
            vmem((3, 2, share), F32),
            vmem((members, 2, NT), F32),
            vmem((members, 2, NT), F32),
            vmem((2, NT), F32),
            vmem((2, NT), F32),
            dma((5,)), dma((share // CHUNK,)), dma,
            dma, dma, dma, dma,
            dma((half,)), dma((members,)),
            dma((members,)), dma((members,)),
            dma((half,)),
            dma, dma,
            dma((n_s,)), dma((n_s,)),
            dma((3,)), dma((3,)),
            dma((members,)), dma((members,)),
            dma, dma,
        ],
        compiler_params=pltpu.CompilerParams(
            collective_id=0, has_side_effects=True, vmem_limit_bytes=60 * 1024 * 1024
        ),
    )(waves, vector, energies, basis, screening, coulomb, qmap)


def solution(mesh):
    return jax.shard_map(
        on_device,
        mesh=mesh,
        in_specs=(
            P(("grp", "kin"), None, None, None),
            P(("grp", "kin"), None, None),
            P(("grp", "kin"), None),
            P(),
            P(),
            P(),
            P(("grp", "kin"), None),
        ),
        out_specs=P(("grp", "kin"), None, None),
        check_vma=False,
    )
```

```python
import functools

import jax
import jax.numpy as jnp
from jax import lax
from jax.experimental import pallas as pl
from jax.experimental.pallas import tpu as pltpu
from jax.sharding import PartitionSpec as P

NV = 4
NC = 4
NT = 16
TEAM = 2
ROWS = 2 * TEAM * NT
CHUNK = 256
MESH = pl.DeviceIdType.MESH
F32 = jnp.float32
BF16 = jnp.bfloat16


def iota(shape, dim):
    return lax.broadcasted_iota(jnp.int32, shape, dim)


def mm(left, right):
    return jnp.dot(left, right, preferred_element_type=F32)


def mm_nt(left, right):
    return lax.dot_general(left, right, (((1,), (1,)), ((), ())), preferred_element_type=F32)


def hi_lo(value):
    high = value.astype(BF16)
    low = (value - high.astype(F32)).astype(BF16)
    return jnp.concatenate([high, low], 0)


def one_hot(cond):
    return jnp.where(cond, 1.0, 0.0).astype(BF16)


def conj_mul(lre, lim, rre, rim):
    return lre * rre + lim * rim, lre * rim - lim * rre


def twice(rows):
    return jnp.concatenate([rows, rows], 0)


def kernel(
    groups, members, n_g,
    waves_h, vector_h, energies_h, basis_h, screening_h, coulomb_h, qmap_h, out,
    energies, coulomb, qmap, basis, screening, team, team_vec, part, part_vec,
    left, weights, weights_in, own_p, pair_p, own_d, s_own, s_in, s_plane, s_all, h_send, h_recv, t_send, t_recv,
    small_sem, basis_sem, screen_sem, t_ssem, t_rsem, tv_ssem, tv_rsem, p_ssem, p_rsem, pv_ssem, pv_rsem, r_ssem,
    w_ssem, w_rsem, s_ssem, s_rsem, g_ssem, g_rsem, h_ssem, h_rsem, d_ssem, d_rsem,
):
    offset = groups // 4
    half = members // 2
    teams = members // TEAM
    n_k = groups * members
    points = waves_h.shape[3]
    share = n_g // TEAM
    n_chunk = share // CHUNK
    grp = lax.axis_index("grp")
    kin = lax.axis_index("kin")
    rank = lax.rem(kin, TEAM)
    sib = kin + 1 - 2 * rank
    up = lax.rem(grp + offset, groups)
    down = lax.rem(grp + groups - offset, groups)

    def source(i):
        if i < half:
            return lax.rem(kin + members - 2 * i, members)
        return lax.rem(sib + members - 2 * (i - half), members)

    def group_at(dg):
        return (lax.rem(grp + dg, groups), kin)

    def spot_at(ds, dk):
        level = lax.div(grp, offset)
        return kin_at(level * offset + lax.rem(grp - level * offset + ds, offset), dk)

    def kin_at(g, dk):
        return (g, lax.rem(kin + dk, members))

    plane = [(ds, dt) for ds in range(offset) for dt in range(teams) if (ds, dt) != (0, 0)]
    plane_at = [spot_at(ds, TEAM * dt) for ds, dt in plane]
    greet = [kin_at(g, dk) for g in (up, down) for dk in range(members)] + [group_at(2 * offset), (grp, sib)] + plane_at
    barrier = pltpu.get_barrier_semaphore()
    for target in greet:
        pl.semaphore_signal(barrier, inc=1, device_id=target, device_id_type=MESH)

    my_cols = pl.ds(pl.multiple_of(rank * share, 128), share)
    pairs = [
        (waves_h, team.at[pl.ds(0, 1)]), (vector_h, team_vec.at[pl.ds(0, 1)]), (qmap_h, qmap),
        (energies_h, energies), (coulomb_h, coulomb),
    ]
    small = []
    for i, (src, dst) in enumerate(pairs):
        small.append(pltpu.make_async_copy(src, dst, small_sem.at[i]))
        small[-1].start()
    basis_in = []
    for n in range(n_chunk):
        src = pl.ds(pl.multiple_of(rank * share + n * CHUNK, 128), CHUNK)
        basis_in.append(pltpu.make_async_copy(
            basis_h.at[:, :, src], basis.at[:, :, pl.ds(n * CHUNK, CHUNK)], basis_sem.at[n]))
        basis_in[-1].start()
        if n == 0:
            screen_in = pltpu.make_async_copy(screening_h, screening, screen_sem)
            screen_in.start()
    pl.semaphore_wait(barrier, len(greet))

    started = []

    def send(src, dst, ssem, rsem, target):
        copy = pltpu.make_async_remote_copy(
            src_ref=src, dst_ref=dst, send_sem=ssem, recv_sem=rsem, device_id=target, device_id_type=MESH
        )
        copy.start()
        started.append(copy)
        return copy

    one = pl.ds(1, 1)
    part_in = [None] * members
    for i in range(half):
        part_in[i] = send(waves_h, part.at[pl.ds(i, 1)], p_ssem.at[i], p_rsem.at[i], kin_at(up, 2 * i))
    team_in = send(waves_h, team.at[one], t_ssem, t_rsem, (grp, sib))
    team_vec_in = send(vector_h, team_vec.at[one], tv_ssem, tv_rsem, (grp, sib))
    vec_in = []
    for i in range(members):
        if i < half:
            target = kin_at(up, 2 * i)
        else:
            target = (up, lax.rem(sib + 2 * (i - half), members))
        vec_in.append(send(vector_h, part_vec.at[pl.ds(i, 1)], pv_ssem.at[i], pv_rsem.at[i], target))

    for copy in small:
        copy.wait()
    low_half = iota((8, points), 0) < 4
    re_rows, im_rows = slice(0, ROWS), slice(ROWS, 2 * ROWS)

    def team_part(s):
        wre = team[s, 0].astype(F32)
        wim = team[s, 1].astype(F32)
        cre, cim = twice(wre[NV:]), twice(wim[NV:])
        res, ims = [], []
        for h in range(4):
            lre = jnp.where(low_half, wre[2 * h:2 * h + 1], wre[2 * h + 1:2 * h + 2])
            lim = jnp.where(low_half, wim[2 * h:2 * h + 1], wim[2 * h + 1:2 * h + 2])
            left[s, h, 0] = lre
            left[s, h, 1] = lim
            if h < 2:
                pre, pim = conj_mul(lre, lim, cre, cim)
                res.append(pre)
                ims.append(pim)
        pre = jnp.concatenate(res, 0)
        pim = jnp.concatenate(ims, 0)
        r0 = s * NT
        r1 = TEAM * NT + s * NT
        own_p[r0:r0 + NT, 0:points] = pre.astype(BF16)
        own_p[r0:r0 + NT, points:] = (-pim).astype(BF16)
        own_p[r1:r1 + NT, 0:points] = pim.astype(BF16)
        own_p[r1:r1 + NT, points:] = pre.astype(BF16)

    team_part(0)

    side = 2 * ROWS
    col = iota((NT, side), 1)
    tr = iota((NT, side), 0)
    pick_v = one_hot((col // 4) % 4 == tr // 4)
    pick_w = one_hot(col % 4 == tr // 4)
    same = (iota((side, side), 0) // NT) % 4 == (iota((side, side), 1) // NT) % 4
    first = iota((8, side), 1) < ROWS
    row8 = iota((8, NT), 0)
    lane8 = iota((8, NT), 1)
    hit_d = row8 % 4 == lane8 % 4

    screen_in.wait()
    base = down * members
    for b in range(members):
        weights[b:b + 1, :] = screening[pl.ds(qmap[0, base + b], 1), :]
    sib_cols = pl.ds(pl.multiple_of((1 - rank) * share, 128), share)
    weight_in = send(weights.at[:, sib_cols], weights_in.at[1], w_ssem, w_rsem, (grp, sib))
    weights_in[0] = weights[:, my_cols]

    team_in.wait_recv()
    team_vec_in.wait_recv()
    team_part(1)
    xs = []
    for s in range(TEAM):
        x = team_vec[s].astype(BF16).astype(F32)
        xs.append((x[0:1], x[1:2]))
    xr = jnp.concatenate([x[0] for x in xs], 1)
    xi = jnp.concatenate([x[1] for x in xs], 1)
    x_rows = jnp.concatenate(
        [jnp.concatenate([xr, -xi], 1), jnp.concatenate([xi, xr], 1), jnp.zeros((6, 2 * TEAM * NT), F32)], 0
    ).astype(BF16)

    def basis_cols(n):
        return basis[:, :, n * CHUNK:(n + 1) * CHUNK].reshape(2 * points, CHUNK)

    for n in range(n_chunk):
        if n == n_chunk - 1:
            for i in range(half):
                part_in[i].wait_recv()
                send(part.at[i], part.at[half + i], r_ssem.at[i], p_rsem.at[half + i], (grp, sib))
        basis_in[n].wait()
        cols = slice(n * CHUNK, (n + 1) * CHUNK)
        dens = mm(own_p[...], basis_cols(n)).astype(BF16)
        own_d[:, cols] = dens
        s_own[:, cols] = mm(x_rows, dens)[0:2]
    s_copies = []
    for i, target in enumerate(plane_at):
        s_copies.append(send(s_own, s_in.at[i], s_ssem.at[i], s_rsem.at[i], target))

    a_re, a_im = [], []
    for s in range(TEAM):
        for c in range(0, NC, 2):
            hit = lane8 % 4 == c + row8 // 4
            a_re.append(jnp.where(hit, xs[s][0], 0.0))
            a_im.append(jnp.where(hit, xs[s][1], 0.0))
    spread = mm(jnp.concatenate(a_re + a_im, 0).astype(BF16), pick_v)
    first_32 = iota((TEAM * NT, side), 1) < ROWS
    a_re, a_im = spread[0:TEAM * NT], spread[TEAM * NT:]
    u1 = twice(jnp.where(first_32, a_re, a_im))
    u2 = twice(jnp.where(first_32, -a_im, a_re))

    def products(i, batch, j):
        wre = part[i, 0].astype(F32)
        wim = part[i, 1].astype(F32)
        for kind in range(2):
            bands = slice(NV, NV + NC) if kind == 0 else slice(0, NV)
            rre, rim = twice(wre[bands]), twice(wim[bands])
            for s in range(TEAM):
                res, ims = [], []
                for h in range(2):
                    t = h + 2 - 2 * kind
                    pre, pim = conj_mul(left[s, t, 0], left[s, t, 1], rre, rim)
                    res.append(pre)
                    ims.append(pim)
                pre = jnp.concatenate(res, 0)
                pim = jnp.concatenate(ims, 0)
                r0 = kind * side + j * TEAM * NT + s * NT
                r1 = r0 + ROWS
                pair_p[batch, r0:r0 + NT, 0:points] = pre.astype(BF16)
                pair_p[batch, r0:r0 + NT, points:] = (-pim).astype(BF16)
                pair_p[batch, r1:r1 + NT, 0:points] = pim.astype(BF16)
                pair_p[batch, r1:r1 + NT, points:] = pre.astype(BF16)

    def kernel_of(batch):
        total = None
        for n in range(n_chunk):
            cols = slice(n * CHUNK, (n + 1) * CHUNK)
            dens = mm(pair_p[batch % 2], basis_cols(n)).astype(BF16)
            rows = []
            for j in range(2):
                b = source(2 * batch + j)
                rows += [jnp.broadcast_to(weights_in[s, pl.ds(b, 1), cols], (NT, CHUNK)) for s in range(TEAM)]
            weight = jnp.concatenate(rows * 2, 0)
            cond = (dens[0:side].astype(F32) * weight).astype(BF16)
            term = mm_nt(cond, dens[side:])
            total = term if total is None else total + term
        return jnp.where(same, total, 0.0)

    kerns = []
    for batch in range(members // 2):
        for i in (2 * batch, 2 * batch + 1):
            if i >= half:
                k = pl.ds(i, 1)
                part_in[i] = pltpu.make_async_remote_copy(
                    src_ref=part.at[k], dst_ref=part.at[k], send_sem=r_ssem.at[i - half], recv_sem=p_rsem.at[i],
                    device_id=(grp, sib), device_id_type=MESH)
                part_in[i].wait_recv()
        vec_in[2 * batch].wait_recv()
        vec_in[2 * batch + 1].wait_recv()
        if batch == 0:
            weight_in.wait_recv()
        for j in range(2):
            products(2 * batch + j, batch % 2, j)
        kerns.append(kernel_of(batch))
        if batch == 0:
            total = s_own[...]
            for i, copy in enumerate(s_copies):
                copy.wait_recv()
                total = total + s_in[i]
            s_plane[...] = total
            g_copies = []
            for i in range(3):
                g_copies.append(send(s_plane, s_all.at[i], g_ssem.at[i], g_rsem.at[i], group_at(offset * (i + 1))))

    h_rows = []
    for kern in kerns:
        k_re, k_im = kern[re_rows], kern[im_rows]
        for value in (k_re * u1 + k_im * u2, k_im * u1 - k_re * u2):
            for j in range(2):
                r0 = j * TEAM * NT
                h_rows.append(value[r0:r0 + 8] + value[r0 + 8:r0 + 16] + value[r0 + 16:r0 + 24] + value[r0 + 24:r0 + 32])
    n_h = 8 * len(h_rows)
    h_sums = mm_nt(hi_lo(jnp.concatenate(h_rows, 0)), pick_w)
    h_sums = h_sums[0:n_h] + h_sums[n_h:]

    def h_row(batch, comp, j):
        r0 = 8 * (4 * batch + 2 * comp + j)
        return jnp.sum(jnp.where(hit_d, h_sums[r0:r0 + 8], 0.0), 0, keepdims=True)

    h_copies = []
    for i in range(members):
        h_send[i] = jnp.concatenate([h_row(i // 2, 0, i % 2), h_row(i // 2, 1, i % 2)], 0)

    d_re = jnp.zeros((ROWS, side), F32)
    d_im = jnp.zeros((ROWS, side), F32)
    for batch, kern in enumerate(kerns):
        k_re, k_im = kern[re_rows], kern[im_rows]
        x_parts = []
        for j in range(2):
            xb = part_vec[2 * batch + j].astype(BF16).astype(F32)
            x_parts += [jnp.where(hit_d, xb[0:1], 0.0), jnp.where(hit_d, xb[1:2], 0.0)]
        xx = mm(jnp.concatenate(x_parts, 0).astype(BF16), pick_w)
        w1, w2 = [], []
        for j in range(2):
            x_re, x_im = xx[16 * j:16 * j + 8], xx[16 * j + 8:16 * j + 16]
            w1 += [jnp.where(first, x_re, -x_im)] * (2 * TEAM)
            w2 += [jnp.where(first, x_im, x_re)] * (2 * TEAM)
        w1 = jnp.concatenate(w1, 0)
        w2 = jnp.concatenate(w2, 0)
        d_re = d_re + (k_re * w1 + k_im * w2)
        d_im = d_im + (k_re * w2 - k_im * w1)
    n_d = TEAM * NT
    d_rows = jnp.concatenate([d_re[0:n_d] + d_re[n_d:], d_im[0:n_d] + d_im[n_d:]], 0)
    d_sums = mm_nt(hi_lo(d_rows), pick_v)
    d_sums = d_sums[0:2 * n_d] + d_sums[2 * n_d:]
    d_sums = jnp.where((iota((2 * n_d, NT), 0) // 4) % 4 == iota((2 * n_d, NT), 1) % 4, d_sums, 0.0)

    for i in range(members):
        h_copies.append(send(h_send.at[i], h_recv.at[i], h_ssem.at[i], h_rsem.at[i], (down, source(i))))

    total = s_plane[...]
    for i, copy in enumerate(g_copies):
        copy.wait_recv()
        total = total + s_all[i]
    pot = coulomb[my_cols].reshape(1, share) * total
    ex = mm_nt(jnp.concatenate([hi_lo(pot), jnp.zeros((4, share), BF16)], 0), own_d[...])
    ex = ex[0:2] + ex[2:4]
    exchange = jnp.concatenate([ex[0:1, 0:n_d] + ex[1:2, n_d:], ex[1:2, 0:n_d] - ex[0:1, n_d:]], 0)

    scale = 1.0 / n_k
    sums = []
    for s in range(TEAM):
        direct = jnp.concatenate(
            [jnp.sum(d_sums[r:r + NT], 0, keepdims=True) for r in (s * NT, n_d + s * NT)], 0)
        sums.append((2.0 * scale) * exchange[:, s * NT:(s + 1) * NT] - scale * direct)
    t_send[...] = sums[1]
    d_copy = send(t_send, t_recv, d_ssem, d_rsem, (grp, sib))
    result = energies[...] * team_vec[0] + sums[0]
    for copy in started:
        copy.wait_send()
    for copy in h_copies:
        copy.wait_recv()
    back = h_recv[0]
    for i in range(1, members):
        back = back + h_recv[i]
    d_copy.wait_recv()
    out[0] = result + t_recv[...] - scale * back


def on_device(waves, vector, energies, basis, screening, coulomb, qmap):
    groups = lax.axis_size("grp")
    members = lax.axis_size("kin")
    half = members // 2
    points = waves.shape[3]
    n_g = basis.shape[2]
    share = n_g // TEAM
    n_s = groups // 4 * (members // TEAM) - 1
    any_space = pl.BlockSpec(memory_space=pl.ANY)
    dma = pltpu.SemaphoreType.DMA
    vmem = pltpu.VMEM
    n_own = 2 * TEAM * NT
    return pl.pallas_call(
        functools.partial(kernel, groups, members, n_g),
        out_shape=jax.ShapeDtypeStruct(vector.shape, F32),
        in_specs=[any_space] * 7,
        out_specs=pl.BlockSpec(memory_space=vmem),
        scratch_shapes=[
            vmem(energies.shape, F32),
            vmem(coulomb.shape, F32),
            pltpu.SMEM(qmap.shape, jnp.int32),
            vmem((2, points, share), BF16),
            vmem(screening.shape, F32),
            vmem((TEAM,) + waves.shape[1:], BF16),
            vmem((TEAM, 2, NT), F32),
            vmem((members,) + waves.shape[1:], BF16),
            vmem((members, 2, NT), F32),
            vmem((TEAM, 4, 2, 8, points), F32),
            vmem((members, n_g), F32),
            vmem((TEAM, members, share), F32),
            vmem((n_own, 2 * points), BF16),
            vmem((2, 4 * ROWS, 2 * points), BF16),
            vmem((n_own, share), BF16),
            vmem((2, share), F32),
            vmem((n_s, 2, share), F32),
            vmem((2, share), F32),
            vmem((3, 2, share), F32),
            vmem((members, 2, NT), F32),
            vmem((members, 2, NT), F32),
            vmem((2, NT), F32),
            vmem((2, NT), F32),
            dma((5,)), dma((share // CHUNK,)), dma,
            dma, dma, dma, dma,
            dma((half,)), dma((members,)),
            dma((members,)), dma((members,)),
            dma((half,)),
            dma, dma,
            dma((n_s,)), dma((n_s,)),
            dma((3,)), dma((3,)),
            dma((members,)), dma((members,)),
            dma, dma,
        ],
        compiler_params=pltpu.CompilerParams(
            collective_id=0, has_side_effects=True, vmem_limit_bytes=60 * 1024 * 1024
        ),
    )(waves, vector, energies, basis, screening, coulomb, qmap)


def solution(mesh):
    return jax.shard_map(
        on_device,
        mesh=mesh,
        in_specs=(
            P(("grp", "kin"), None, None, None),
            P(("grp", "kin"), None, None),
            P(("grp", "kin"), None),
            P(),
            P(),
            P(),
            P(("grp", "kin"), None),
        ),
        out_specs=P(("grp", "kin"), None, None),
        check_vma=False,
    )
```

```python
import functools

import jax
import jax.numpy as jnp
from jax import lax
from jax.experimental import pallas as pl
from jax.experimental.pallas import tpu as pltpu
from jax.sharding import PartitionSpec as P

NV = 4
NC = 4
NT = 16
TEAM = 2
ROWS = 2 * TEAM * NT
CHUNK = 256
MESH = pl.DeviceIdType.MESH
F32 = jnp.float32
BF16 = jnp.bfloat16


def iota(shape, dim):
    return lax.broadcasted_iota(jnp.int32, shape, dim)


def mm(left, right):
    return jnp.dot(left, right, preferred_element_type=F32)


def mm_nt(left, right):
    return lax.dot_general(left, right, (((1,), (1,)), ((), ())), preferred_element_type=F32)


def hi_lo(value):
    high = value.astype(BF16)
    low = (value - high.astype(F32)).astype(BF16)
    return jnp.concatenate([high, low], 0)


def one_hot(cond):
    return jnp.where(cond, 1.0, 0.0).astype(BF16)


def conj_mul(lre, lim, rre, rim):
    return lre * rre + lim * rim, lre * rim - lim * rre


def twice(rows):
    return jnp.concatenate([rows, rows], 0)


def kernel(
    groups, members, n_g,
    waves_h, vector_h, energies_h, basis_h, screening_h, coulomb_h, qmap_h, out,
    energies, coulomb, qmap, basis, screening, team, team_vec, part, part_vec,
    left, weights, weights_in, own_p, pair_p, own_d, s_own, s_in, s_pair, s_all, h_send, h_recv, t_send, t_recv,
    small_sem, basis_sem, screen_sem, t_ssem, t_rsem, tv_ssem, tv_rsem, p_ssem, p_rsem, pv_ssem, pv_rsem, r_ssem,
    w_ssem, w_rsem, s_ssem, s_rsem, g_ssem, g_rsem, h_ssem, h_rsem, d_ssem, d_rsem,
):
    offset = groups // 4
    half = members // 2
    teams = members // TEAM
    n_k = groups * members
    points = waves_h.shape[3]
    share = n_g // TEAM
    n_chunk = share // CHUNK
    grp = lax.axis_index("grp")
    kin = lax.axis_index("kin")
    rank = lax.rem(kin, TEAM)
    sib = kin + 1 - 2 * rank
    up = lax.rem(grp + offset, groups)
    down = lax.rem(grp + groups - offset, groups)

    def source(i):
        if i < half:
            return lax.rem(kin + members - 2 * i, members)
        return lax.rem(sib + members - 2 * (i - half), members)

    def group_at(dg):
        return (lax.rem(grp + dg, groups), kin)

    def kin_at(g, dk):
        return (g, lax.rem(kin + dk, members))

    greet = [kin_at(g, dk) for g in (up, down) for dk in range(1, members)]
    greet += [group_at(dg) for dg in range(1, groups)] + [kin_at(grp, dk) for dk in range(1, members)]
    barrier = pltpu.get_barrier_semaphore()
    for target in greet:
        pl.semaphore_signal(barrier, inc=1, device_id=target, device_id_type=MESH)

    my_cols = pl.ds(pl.multiple_of(rank * share, 128), share)
    pairs = [
        (waves_h, team.at[pl.ds(0, 1)]), (vector_h, team_vec.at[pl.ds(0, 1)]), (qmap_h, qmap),
        (energies_h, energies), (coulomb_h, coulomb),
    ]
    small = []
    for i, (src, dst) in enumerate(pairs):
        small.append(pltpu.make_async_copy(src, dst, small_sem.at[i]))
        small[-1].start()
    basis_in = []
    for n in range(n_chunk):
        src = pl.ds(pl.multiple_of(rank * share + n * CHUNK, 128), CHUNK)
        basis_in.append(pltpu.make_async_copy(
            basis_h.at[:, :, src], basis.at[:, :, pl.ds(n * CHUNK, CHUNK)], basis_sem.at[n]))
        basis_in[-1].start()
        if n == 0:
            screen_in = pltpu.make_async_copy(screening_h, screening, screen_sem)
            screen_in.start()
    pl.semaphore_wait(barrier, len(greet))

    started = []

    def send(src, dst, ssem, rsem, target):
        copy = pltpu.make_async_remote_copy(
            src_ref=src, dst_ref=dst, send_sem=ssem, recv_sem=rsem, device_id=target, device_id_type=MESH
        )
        copy.start()
        started.append(copy)
        return copy

    one = pl.ds(1, 1)
    part_in = [None] * members
    for i in range(half):
        part_in[i] = send(waves_h, part.at[pl.ds(i, 1)], p_ssem.at[i], p_rsem.at[i], kin_at(up, 2 * i))
    team_in = send(waves_h, team.at[one], t_ssem, t_rsem, (grp, sib))
    team_vec_in = send(vector_h, team_vec.at[one], tv_ssem, tv_rsem, (grp, sib))
    vec_in = []
    for i in range(members):
        if i < half:
            target = kin_at(up, 2 * i)
        else:
            target = (up, lax.rem(sib + 2 * (i - half), members))
        vec_in.append(send(vector_h, part_vec.at[pl.ds(i, 1)], pv_ssem.at[i], pv_rsem.at[i], target))

    for copy in small:
        copy.wait()
    low_half = iota((8, points), 0) < 4
    re_rows, im_rows = slice(0, ROWS), slice(ROWS, 2 * ROWS)

    def team_part(s):
        wre = team[s, 0].astype(F32)
        wim = team[s, 1].astype(F32)
        cre, cim = twice(wre[NV:]), twice(wim[NV:])
        res, ims = [], []
        for h in range(4):
            lre = jnp.where(low_half, wre[2 * h:2 * h + 1], wre[2 * h + 1:2 * h + 2])
            lim = jnp.where(low_half, wim[2 * h:2 * h + 1], wim[2 * h + 1:2 * h + 2])
            left[s, h, 0] = lre
            left[s, h, 1] = lim
            if h < 2:
                pre, pim = conj_mul(lre, lim, cre, cim)
                res.append(pre)
                ims.append(pim)
        pre = jnp.concatenate(res, 0)
        pim = jnp.concatenate(ims, 0)
        r0 = s * NT
        r1 = TEAM * NT + s * NT
        own_p[r0:r0 + NT, 0:points] = pre.astype(BF16)
        own_p[r0:r0 + NT, points:] = (-pim).astype(BF16)
        own_p[r1:r1 + NT, 0:points] = pim.astype(BF16)
        own_p[r1:r1 + NT, points:] = pre.astype(BF16)

    team_part(0)

    side = 2 * ROWS
    col = iota((NT, side), 1)
    tr = iota((NT, side), 0)
    pick_v = one_hot((col // 4) % 4 == tr // 4)
    pick_w = one_hot(col % 4 == tr // 4)
    same = (iota((side, side), 0) // NT) % 4 == (iota((side, side), 1) // NT) % 4
    first = iota((8, side), 1) < ROWS
    row8 = iota((8, NT), 0)
    lane8 = iota((8, NT), 1)
    hit_d = row8 % 4 == lane8 % 4

    screen_in.wait()
    base = down * members
    for b in range(members):
        weights[b:b + 1, :] = screening[pl.ds(qmap[0, base + b], 1), :]
    sib_cols = pl.ds(pl.multiple_of((1 - rank) * share, 128), share)
    weight_in = send(weights.at[:, sib_cols], weights_in.at[1], w_ssem, w_rsem, (grp, sib))
    weights_in[0] = weights[:, my_cols]

    team_in.wait_recv()
    team_vec_in.wait_recv()
    team_part(1)
    xs = []
    for s in range(TEAM):
        x = team_vec[s].astype(BF16).astype(F32)
        xs.append((x[0:1], x[1:2]))
    xr = jnp.concatenate([x[0] for x in xs], 1)
    xi = jnp.concatenate([x[1] for x in xs], 1)
    x_rows = jnp.concatenate(
        [jnp.concatenate([xr, -xi], 1), jnp.concatenate([xi, xr], 1), jnp.zeros((6, 2 * TEAM * NT), F32)], 0
    ).astype(BF16)

    def basis_cols(n):
        return basis[:, :, n * CHUNK:(n + 1) * CHUNK].reshape(2 * points, CHUNK)

    for n in range(n_chunk):
        basis_in[n].wait()
        cols = slice(n * CHUNK, (n + 1) * CHUNK)
        dens = mm(own_p[...], basis_cols(n)).astype(BF16)
        own_d[:, cols] = dens
        s_own[:, cols] = mm(x_rows, dens)[0:2]
    s_copies = []
    for i in range(teams - 1):
        s_copies.append(send(s_own, s_in.at[i], s_ssem.at[i], s_rsem.at[i], kin_at(grp, TEAM * (i + 1))))

    a_re, a_im = [], []
    for s in range(TEAM):
        for c in range(0, NC, 2):
            hit = lane8 % 4 == c + row8 // 4
            a_re.append(jnp.where(hit, xs[s][0], 0.0))
            a_im.append(jnp.where(hit, xs[s][1], 0.0))
    spread = mm(jnp.concatenate(a_re + a_im, 0).astype(BF16), pick_v)
    first_32 = iota((TEAM * NT, side), 1) < ROWS
    a_re, a_im = spread[0:TEAM * NT], spread[TEAM * NT:]
    u1 = twice(jnp.where(first_32, a_re, a_im))
    u2 = twice(jnp.where(first_32, -a_im, a_re))

    def products(i, batch, j):
        wre = part[i, 0].astype(F32)
        wim = part[i, 1].astype(F32)
        for kind in range(2):
            bands = slice(NV, NV + NC) if kind == 0 else slice(0, NV)
            rre, rim = twice(wre[bands]), twice(wim[bands])
            for s in range(TEAM):
                res, ims = [], []
                for h in range(2):
                    t = h + 2 - 2 * kind
                    pre, pim = conj_mul(left[s, t, 0], left[s, t, 1], rre, rim)
                    res.append(pre)
                    ims.append(pim)
                pre = jnp.concatenate(res, 0)
                pim = jnp.concatenate(ims, 0)
                r0 = kind * side + j * TEAM * NT + s * NT
                r1 = r0 + ROWS
                pair_p[batch, r0:r0 + NT, 0:points] = pre.astype(BF16)
                pair_p[batch, r0:r0 + NT, points:] = (-pim).astype(BF16)
                pair_p[batch, r1:r1 + NT, 0:points] = pim.astype(BF16)
                pair_p[batch, r1:r1 + NT, points:] = pre.astype(BF16)

    def kernel_of(batch):
        total = None
        for n in range(n_chunk):
            cols = slice(n * CHUNK, (n + 1) * CHUNK)
            dens = mm(pair_p[batch % 2], basis_cols(n)).astype(BF16)
            rows = []
            for j in range(2):
                b = source(2 * batch + j)
                rows += [jnp.broadcast_to(weights_in[s, pl.ds(b, 1), cols], (NT, CHUNK)) for s in range(TEAM)]
            weight = jnp.concatenate(rows * 2, 0)
            cond = (dens[0:side].astype(F32) * weight).astype(BF16)
            term = mm_nt(cond, dens[side:])
            total = term if total is None else total + term
        return jnp.where(same, total, 0.0)

    kerns = []
    for batch in range(members // 2):
        for i in (2 * batch, 2 * batch + 1):
            if i >= half:
                k = pl.ds(i, 1)
                part_in[i] = pltpu.make_async_remote_copy(
                    src_ref=part.at[k], dst_ref=part.at[k], send_sem=r_ssem.at[i - half], recv_sem=p_rsem.at[i],
                    device_id=(grp, sib), device_id_type=MESH)
            part_in[i].wait_recv()
            if i < half:
                send(part.at[i], part.at[half + i], r_ssem.at[i], p_rsem.at[half + i], (grp, sib))
        if batch == 0:
            weight_in.wait_recv()
        for j in range(2):
            products(2 * batch + j, batch % 2, j)
        if batch == 1:
            total = s_own[...]
            for i, copy in enumerate(s_copies):
                copy.wait_recv()
                total = total + s_in[i]
            s_pair[...] = total
            g_copies = []
            for i in range(groups - 1):
                g_copies.append(send(s_pair, s_all.at[i], g_ssem.at[i], g_rsem.at[i], group_at(i + 1)))
        kerns.append(kernel_of(batch))

    h_rows = []
    for kern in kerns:
        k_re, k_im = kern[re_rows], kern[im_rows]
        for value in (k_re * u1 + k_im * u2, k_im * u1 - k_re * u2):
            for j in range(2):
                r0 = j * TEAM * NT
                h_rows.append(value[r0:r0 + 8] + value[r0 + 8:r0 + 16] + value[r0 + 16:r0 + 24] + value[r0 + 24:r0 + 32])
    n_h = 8 * len(h_rows)
    h_sums = mm_nt(hi_lo(jnp.concatenate(h_rows, 0)), pick_w)
    h_sums = h_sums[0:n_h] + h_sums[n_h:]

    def h_row(batch, comp, j):
        r0 = 8 * (4 * batch + 2 * comp + j)
        return jnp.sum(jnp.where(hit_d, h_sums[r0:r0 + 8], 0.0), 0, keepdims=True)

    h_copies = []
    for i in range(members):
        h_send[i] = jnp.concatenate([h_row(i // 2, 0, i % 2), h_row(i // 2, 1, i % 2)], 0)
    for i in range(members):
        h_copies.append(send(h_send.at[i], h_recv.at[i], h_ssem.at[i], h_rsem.at[i], (down, source(i))))

    for copy in vec_in:
        copy.wait_recv()
    d_re = jnp.zeros((ROWS, side), F32)
    d_im = jnp.zeros((ROWS, side), F32)
    for batch, kern in enumerate(kerns):
        k_re, k_im = kern[re_rows], kern[im_rows]
        x_parts = []
        for j in range(2):
            xb = part_vec[2 * batch + j].astype(BF16).astype(F32)
            x_parts += [jnp.where(hit_d, xb[0:1], 0.0), jnp.where(hit_d, xb[1:2], 0.0)]
        xx = mm(jnp.concatenate(x_parts, 0).astype(BF16), pick_w)
        w1, w2 = [], []
        for j in range(2):
            x_re, x_im = xx[16 * j:16 * j + 8], xx[16 * j + 8:16 * j + 16]
            w1 += [jnp.where(first, x_re, -x_im)] * (2 * TEAM)
            w2 += [jnp.where(first, x_im, x_re)] * (2 * TEAM)
        w1 = jnp.concatenate(w1, 0)
        w2 = jnp.concatenate(w2, 0)
        d_re = d_re + (k_re * w1 + k_im * w2)
        d_im = d_im + (k_re * w2 - k_im * w1)
    n_d = TEAM * NT
    d_rows = jnp.concatenate([d_re[0:n_d] + d_re[n_d:], d_im[0:n_d] + d_im[n_d:]], 0)
    d_sums = mm_nt(hi_lo(d_rows), pick_v)
    d_sums = d_sums[0:2 * n_d] + d_sums[2 * n_d:]
    d_sums = jnp.where((iota((2 * n_d, NT), 0) // 4) % 4 == iota((2 * n_d, NT), 1) % 4, d_sums, 0.0)

    total = s_pair[...]
    for i, copy in enumerate(g_copies):
        copy.wait_recv()
        total = total + s_all[i]
    pot = coulomb[my_cols].reshape(1, share) * total
    ex = mm_nt(jnp.concatenate([hi_lo(pot), jnp.zeros((4, share), BF16)], 0), own_d[...])
    ex = ex[0:2] + ex[2:4]
    exchange = jnp.concatenate([ex[0:1, 0:n_d] + ex[1:2, n_d:], ex[1:2, 0:n_d] - ex[0:1, n_d:]], 0)

    scale = 1.0 / n_k
    sums = []
    for s in range(TEAM):
        direct = jnp.concatenate(
            [jnp.sum(d_sums[r:r + NT], 0, keepdims=True) for r in (s * NT, n_d + s * NT)], 0)
        sums.append((2.0 * scale) * exchange[:, s * NT:(s + 1) * NT] - scale * direct)
    t_send[...] = sums[1]
    d_copy = send(t_send, t_recv, d_ssem, d_rsem, (grp, sib))
    result = energies[...] * team_vec[0] + sums[0]
    for copy in h_copies:
        copy.wait_recv()
    back = h_recv[0]
    for i in range(1, members):
        back = back + h_recv[i]
    d_copy.wait_recv()
    out[0] = result + t_recv[...] - scale * back

    for copy in started:
        copy.wait_send()


def on_device(waves, vector, energies, basis, screening, coulomb, qmap):
    groups = lax.axis_size("grp")
    members = lax.axis_size("kin")
    half = members // 2
    points = waves.shape[3]
    n_g = basis.shape[2]
    share = n_g // TEAM
    n_s = max(members // TEAM - 1, 1)
    any_space = pl.BlockSpec(memory_space=pl.ANY)
    dma = pltpu.SemaphoreType.DMA
    vmem = pltpu.VMEM
    n_own = 2 * TEAM * NT
    return pl.pallas_call(
        functools.partial(kernel, groups, members, n_g),
        out_shape=jax.ShapeDtypeStruct(vector.shape, F32),
        in_specs=[any_space] * 7,
        out_specs=pl.BlockSpec(memory_space=vmem),
        scratch_shapes=[
            vmem(energies.shape, F32),
            vmem(coulomb.shape, F32),
            pltpu.SMEM(qmap.shape, jnp.int32),
            vmem((2, points, share), BF16),
            vmem(screening.shape, F32),
            vmem((TEAM,) + waves.shape[1:], BF16),
            vmem((TEAM, 2, NT), F32),
            vmem((members,) + waves.shape[1:], BF16),
            vmem((members, 2, NT), F32),
            vmem((TEAM, 4, 2, 8, points), F32),
            vmem((members, n_g), F32),
            vmem((TEAM, members, share), F32),
            vmem((n_own, 2 * points), BF16),
            vmem((2, 4 * ROWS, 2 * points), BF16),
            vmem((n_own, share), BF16),
            vmem((2, share), F32),
            vmem((n_s, 2, share), F32),
            vmem((2, share), F32),
            vmem((groups - 1, 2, share), F32),
            vmem((members, 2, NT), F32),
            vmem((members, 2, NT), F32),
            vmem((2, NT), F32),
            vmem((2, NT), F32),
            dma((5,)), dma((share // CHUNK,)), dma,
            dma, dma, dma, dma,
            dma((half,)), dma((members,)),
            dma((members,)), dma((members,)),
            dma((half,)),
            dma, dma,
            dma((n_s,)), dma((n_s,)),
            dma((groups - 1,)), dma((groups - 1,)),
            dma((members,)), dma((members,)),
            dma, dma,
        ],
        compiler_params=pltpu.CompilerParams(
            collective_id=0, has_side_effects=True, vmem_limit_bytes=60 * 1024 * 1024
        ),
    )(waves, vector, energies, basis, screening, coulomb, qmap)


def solution(mesh):
    return jax.shard_map(
        on_device,
        mesh=mesh,
        in_specs=(
            P(("grp", "kin"), None, None, None),
            P(("grp", "kin"), None, None),
            P(("grp", "kin"), None),
            P(),
            P(),
            P(),
            P(("grp", "kin"), None),
        ),
        out_specs=P(("grp", "kin"), None, None),
        check_vma=False,
    )
```
